256 devices in a mesh: dp: 32 (over z, y), tensor: 8 (over x, core).
Axes of the slice: x: 4, y: 4, z: 8, core: 2. Of those that a mesh axis runs over, the one named last changes fastest.
Arguments:
- query_moment: float32 [8192, 8192], P('dp', 'tensor'), may hold values from -63 to 63
- query_gradient: bfloat16 [8192, 8192], P('dp', 'tensor'), may hold values from -6 to 6
- query_factor: float32 [8192, 256], P('tensor'), may hold values from -6 to 6
- key_moment: float32 [8192, 1024], P('dp', 'tensor'), may hold values from -63 to 63
- key_gradient: bfloat16 [8192, 1024], P('dp', 'tensor'), may hold values from -6 to 6
- key_factor: float32 [1024, 256], P('tensor'), may hold values from -6 to 6
- value_moment: float32 [8192, 1024], P('dp', 'tensor'), may hold values from -63 to 63
- value_gradient: bfloat16 [8192, 1024], P('dp', 'tensor'), may hold values from -6 to 6
- value_factor: float32 [1024, 256], P('tensor'), may hold values from -6 to 6
- output_moment: float32 [8192, 8192], P('dp', 'tensor'), may hold values from -63 to 63
- output_gradient: bfloat16 [8192, 8192], P('dp', 'tensor'), may hold values from -6 to 6
- output_factor: float32 [8192, 256], P('tensor'), may hold values from -6 to 6
Outputs:
- query_update: float32 [8192, 8192], P('dp', 'tensor')
- query_momentum: float32 [8192, 8192], P('dp', 'tensor')
- query_basis: float32 [8192, 256], P('tensor')
- key_update: float32 [8192, 1024], P('dp', 'tensor')
- key_momentum: float32 [8192, 1024], P('dp', 'tensor')
- key_basis: float32 [1024, 256], P('tensor')
- value_update: float32 [8192, 1024], P('dp', 'tensor')
- value_momentum: float32 [8192, 1024], P('dp', 'tensor')
- value_basis: float32 [1024, 256], P('tensor')
- output_update: float32 [8192, 8192], P('dp', 'tensor')
- output_momentum: float32 [8192, 8192], P('dp', 'tensor')
- output_basis: float32 [8192, 256], P('tensor')
The draws below stay inside these ranges and needn't reach their ends.
All inputs are finite; a program needn't handle non-finite values.
Results may differ from the reference program's by a relative error of at most 0.0003.
Values sent between devices are 32-bit elements; how exact they have to be, the bound alone decides.
No kernel may reach another device: no remote copies, remote signals or barrier semaphores. Data moves between devices by JAX's collectives and lax.ppermute only.
A program may use at most 64 MiB of HBM per device.

```python
import math
import jax
import jax.numpy as jnp
from jax import lax

D = 8192
KV = 1024
RANK = 256


def scale_field(key, rows, cols):
    first_key, second_key = jax.random.split(key)
    log_low = math.log(0.3)
    log_high = math.log(3.0)
    rising = 3.0 ** (jnp.arange(rows, dtype=jnp.float32) / rows - 0.5)
    row_scale = rising * jnp.exp(jax.random.uniform(first_key, (rows,), jnp.float32, log_low, log_high))
    col_scale = jnp.exp(jax.random.uniform(second_key, (cols,), jnp.float32, log_low, log_high))
    return row_scale[:, None] * col_scale[None, :]


def draw_query_moment(key, part):
    key = jax.random.fold_in(key, 11)
    scale_key, entry_key = jax.random.split(key, 2)
    factor = scale_field(scale_key, D, D)
    values = jnp.clip(jax.random.normal(entry_key, (D, D), jnp.float32), -4.0, 4.0)
    return factor * values


def draw_key_moment(key, part):
    key = jax.random.fold_in(key, 12)
    scale_key, entry_key = jax.random.split(key, 2)
    factor = scale_field(scale_key, D, KV)
    values = jnp.clip(jax.random.normal(entry_key, (D, KV), jnp.float32), -4.0, 4.0)
    return factor * values


def draw_value_moment(key, part):
    key = jax.random.fold_in(key, 13)
    scale_key, entry_key = jax.random.split(key, 2)
    factor = scale_field(scale_key, D, KV)
    values = jnp.clip(jax.random.normal(entry_key, (D, KV), jnp.float32), -4.0, 4.0)
    return factor * values


def draw_output_moment(key, part):
    key = jax.random.fold_in(key, 14)
    scale_key, entry_key = jax.random.split(key, 2)
    factor = scale_field(scale_key, D, D)
    values = jnp.clip(jax.random.normal(entry_key, (D, D), jnp.float32), -4.0, 4.0)
    return factor * values


def block_levels(rng, shape, pieces, low, largest):
    factor_of = 1.0
    for dim, shards_of in pieces:
        heights = jax.random.uniform(jax.random.fold_in(jax.random.fold_in(rng, 6), dim), (shards_of,), jnp.float32, low / len(pieces), largest / len(pieces))
        factor_of = factor_of * jnp.repeat(jnp.exp(heights), shape[dim] // shards_of).reshape((-1,) + (1,) * (len(shape) - 1 - dim))
    return factor_of


def noise(stream_key, extent, scale, limit, cuts=(), kind=jnp.bfloat16):
    result = jax.random.normal(stream_key, extent, jnp.float32) * scale
    if len(cuts) > 0:
        result = block_levels(stream_key, extent, cuts, -0.22, 0.18) * result
    return jnp.clip(result, min=-limit, max=limit).astype(kind)


def setup_inputs(seed: int = 0) -> dict:
    keys = jax.random.split(jax.random.key(seed), 13)
    query_moment = draw_query_moment(jax.random.fold_in(keys[12], 71), 0)
    query_gradient = noise(keys[1], (D, D), 1.0, 6.0, ((0, 32), (1, 8)))
    query_factor = noise(keys[2], (D, RANK), 1.0, 6.0, ((0, 8),), jnp.float32)
    key_moment = draw_key_moment(jax.random.fold_in(keys[12], 71), 0)
    key_gradient = noise(keys[4], (D, KV), 1.0, 6.0, ((0, 32), (1, 8)))
    key_factor = noise(keys[5], (KV, RANK), 1.0, 6.0, ((0, 8),), jnp.float32)
    value_moment = draw_value_moment(jax.random.fold_in(keys[12], 71), 0)
    value_gradient = noise(keys[7], (D, KV), 1.0, 6.0, ((0, 32), (1, 8)))
    value_factor = noise(keys[8], (KV, RANK), 1.0, 6.0, ((0, 8),), jnp.float32)
    output_moment = draw_output_moment(jax.random.fold_in(keys[12], 71), 0)
    output_gradient = noise(keys[10], (D, D), 1.0, 6.0, ((0, 32), (1, 8)))
    output_factor = noise(keys[11], (D, RANK), 1.0, 6.0, ((0, 8),), jnp.float32)
    return {"query_moment": query_moment, "query_gradient": query_gradient, "query_factor": query_factor, "key_moment": key_moment, "key_gradient": key_gradient, "key_factor": key_factor, "value_moment": value_moment, "value_gradient": value_gradient, "value_factor": value_factor, "output_moment": output_moment, "output_gradient": output_gradient, "output_factor": output_factor}


PRECISE = lax.Precision.HIGHEST
MOMENTUM_DECAY = 0.95
SHIFT_RATIO = 0.0001
EPSILON = 1e-06

def dion_single(moment, gradient, factor):
    buffer = moment + gradient.astype(jnp.float32)
    product = jnp.dot(buffer.astype(jnp.float32), factor.astype(jnp.float32), precision=PRECISE, preferred_element_type=jnp.float32)
    gram_matrix = jnp.dot(product.T.astype(jnp.float32), product.astype(jnp.float32), precision=PRECISE, preferred_element_type=jnp.float32)
    rank_size = factor.shape[1]
    shift_value = SHIFT_RATIO * jnp.trace(gram_matrix) / rank_size
    lower_factor = jnp.linalg.cholesky(gram_matrix + shift_value * jnp.eye(rank_size, dtype=jnp.float32))
    ortho_rows = jax.scipy.linalg.solve_triangular(lower_factor, product.T, lower=True).T
    column = jnp.dot(buffer.T.astype(jnp.float32), ortho_rows.astype(jnp.float32), precision=PRECISE, preferred_element_type=jnp.float32)
    squares = lax.optimization_barrier(jnp.sum(column * column, axis=0))
    new_factor = column / jnp.sqrt(squares + EPSILON)[None, :]
    new_moment = buffer - (1.0 - MOMENTUM_DECAY) * jnp.dot(ortho_rows.astype(jnp.float32), column.T.astype(jnp.float32), precision=PRECISE, preferred_element_type=jnp.float32)
    update_scale = math.sqrt(buffer.shape[0] * buffer.shape[1] / rank_size)
    update = update_scale * jnp.dot(ortho_rows.astype(jnp.float32), new_factor.T.astype(jnp.float32), precision=PRECISE, preferred_element_type=jnp.float32)
    return (update, new_moment, new_factor)

def reference(query_moment, query_gradient, query_factor, key_moment, key_gradient, key_factor, value_moment, value_gradient, value_factor, output_moment, output_gradient, output_factor):
    query_out = dion_single(query_moment, query_gradient, query_factor)
    key_out = dion_single(key_moment, key_gradient, key_factor)
    value_out = dion_single(value_moment, value_gradient, value_factor)
    output_out = dion_single(output_moment, output_gradient, output_factor)
    return (query_out[0], query_out[1], query_out[2], key_out[0], key_out[1], key_out[2], value_out[0], value_out[1], value_out[2], output_out[0], output_out[1], output_out[2])
```

```python
import functools
import math

import jax
import jax.numpy as jnp
from jax import lax
from jax.experimental import pallas as pl
from jax.experimental.pallas import tpu as pltpu
from jax.sharding import Mesh
from jax.sharding import PartitionSpec as P

PRECISE = lax.Precision.HIGHEST
MOMENTUM_DECAY = 0.95
SHIFT_RATIO = 0.0001
EPSILON = 1e-06
RANK = 256
PANEL = 16
SIZES = {"z": 8, "y": 4, "x": 4, "core": 2}


def dot(left, right, dims):
    return lax.dot_general(
        left, right, (dims, ((), ())), precision=PRECISE, preferred_element_type=jnp.float32
    )


def split3(values):
    high = values.astype(jnp.bfloat16)
    rest = values - high.astype(jnp.float32)
    mid = rest.astype(jnp.bfloat16)
    low = (rest - mid.astype(jnp.float32)).astype(jnp.bfloat16)
    return high, mid, low


def inverse_kernel(gram_ref, out_ref, work):
    gram = gram_ref[...]
    rows = lax.broadcasted_iota(jnp.int32, (RANK, RANK), 0)
    cols = lax.broadcasted_iota(jnp.int32, (RANK, RANK), 1)
    unit = jnp.where(rows == cols, 1.0, 0.0).astype(jnp.float32)
    shift = SHIFT_RATIO * jnp.sum(gram * unit) / RANK
    work[:, :RANK] = gram + shift * unit
    work[:, RANK:] = unit
    sub = lax.broadcasted_iota(jnp.int32, (PANEL, 128), 0)
    lane = lax.broadcasted_iota(jnp.int32, (PANEL, RANK), 1)

    def step(number, carry):
        start = pl.multiple_of(number * PANEL, PANEL)
        panel = work[pl.ds(start, PANEL), :]
        block = pltpu.roll(panel[:, :RANK], RANK - start, axis=1)[:, :128]
        columns = [jnp.broadcast_to(block[:, j : j + 1], (PANEL, 128)) for j in range(PANEL)]
        parts = [panel[:, 128 * i : 128 * (i + 1)] for i in range(4)]
        scale = jnp.zeros((PANEL, 128), jnp.float32)
        for j in range(PANEL):
            pivot = columns[j][j : j + 1, :]
            scale = jnp.where(sub == j, lax.rsqrt(pivot), scale)
            if j == PANEL - 1:
                break
            mult = jnp.where(sub > j, columns[j] * (1.0 / pivot), 0.0)
            for other in range(j + 1, PANEL):
                columns[other] = columns[other] - mult * columns[other][j : j + 1, :]
            parts = [part - mult * part[j : j + 1, :] for part in parts]
        done = jnp.concatenate([part * scale for part in parts], axis=1)
        out_ref[pl.ds(start, PANEL), :] = done[:, RANK:]
        left = jnp.where(lane >= start + PANEL, done[:, :RANK], 0.0)
        left_high, left_mid, left_low = split3(left)
        high, mid, low = split3(done)
        lhs = jnp.concatenate([left_high, left_high, left_mid, left_high, left_low, left_mid], axis=0)
        rhs = jnp.concatenate([high, mid, high, low, high, mid], axis=0)
        work[...] -= lax.dot_general(
            lhs, rhs, (((0,), (0,)), ((), ())), preferred_element_type=jnp.float32
        )
        return carry

    lax.fori_loop(0, RANK // PANEL, step, 0)


def inverse_lower(gram):
    return pl.pallas_call(
        inverse_kernel,
        out_shape=jax.ShapeDtypeStruct((RANK, RANK), jnp.float32),
        scratch_shapes=[pltpu.VMEM((RANK, 2 * RANK), jnp.float32)],
        name="inverse_lower",
    )(gram)


def shift_along(values, axis, step):
    size = SIZES[axis]
    return lax.ppermute(values, axis, [((i + step) % size, i) for i in range(size)])


def part(values, place):
    return lax.dynamic_index_in_dim(values, place, 0, keepdims=False)


def scatter_sum(values, axis):
    size = SIZES[axis]
    here = lax.axis_index(axis)
    total = part(values, here)
    for step in range(1, size):
        total = total + shift_along(part(values, (here + size - step) % size), axis, step)
    return total


def gather(values, axis):
    size = SIZES[axis]
    here = lax.axis_index(axis)
    pieces = jnp.stack([values] + [shift_along(values, axis, step) for step in range(1, size)])
    doubled = jnp.concatenate([pieces, pieces], axis=0)
    return lax.dynamic_slice_in_dim(doubled, (size - here) % size, size, 0)


def gather_sum(values, axis):
    total = values
    for step in range(1, SIZES[axis]):
        total = total + shift_along(values, axis, step)
    return total


def local(*arguments):
    momenta = arguments[0::3]
    gradients = arguments[1::3]
    factors = arguments[2::3]
    height = momenta[0].shape[0]
    buffers = [m + g.astype(jnp.float32) for m, g in zip(momenta, gradients)]
    column_place = lax.axis_index("x")
    core = lax.axis_index("core")
    half = height // 2

    partial = jnp.stack([dot(b, f, ((1,), (0,))) for b, f in zip(buffers, factors)])
    partial = partial.reshape(4, 2, half, RANK)
    mine = lax.dynamic_index_in_dim(partial, core, 1, keepdims=False)
    other = lax.dynamic_index_in_dim(partial, 1 - core, 1, keepdims=False)
    halves = mine + shift_along(other, "core", 1)
    shard = scatter_sum(halves, "x")
    gathered = gather(shard, "x")
    both = gather(gathered, "core")
    products = [both[:, number].reshape(height, RANK) for number in range(4)]

    crossed = [dot(b, p, ((0,), (0,))) for b, p in zip(buffers, products)]
    query_part = crossed[0].reshape(4, 8, -1, RANK)
    narrow = jnp.concatenate([crossed[1], crossed[2]], axis=0).reshape(4, 8, -1, RANK)
    output_part = jnp.concatenate([crossed[3].reshape(4, 8, -1, RANK), narrow], axis=2)

    product = lax.dynamic_index_in_dim(both, column_place, 1, keepdims=False).reshape(height, RANK)
    left = lax.dynamic_slice_in_dim(product, core * half, half, 1)
    gram = dot(left, product, ((0,), (0,)))
    gram = scatter_sum(gram.reshape(4, half // 4, RANK), "y")
    gram = jnp.sum(gather(gram, "z"), axis=0)
    gram = gather(gram, "y").reshape(half, RANK)
    gram = gather(gram, "core").reshape(RANK, RANK)
    inverse = inverse_lower(gram)
    inverse_half = lax.dynamic_slice_in_dim(inverse, core * half, half, 0)
    inverses = gather(gather(inverse_half, "x"), "core")
    inverses = [inverses[:, number].reshape(RANK, RANK) for number in range(4)]

    query_cross, output_cross = [
        gather(gather(scatter_sum(scatter_sum(c, "y"), "z"), "z"), "y")
        for c in (query_part, output_part)
    ]
    wide = crossed[0].shape[0] // 32
    narrow = output_cross[:, :, wide:].reshape(-1, RANK)
    count = crossed[1].shape[0]
    crosses = [
        query_cross.reshape(-1, RANK),
        narrow[:count],
        narrow[count:],
        output_cross[:, :, :wide].reshape(-1, RANK),
    ]

    columns = [dot(c, i, ((1,), (1,))) for c, i in zip(crosses, inverses)]
    orthos = [dot(p, i, ((1,), (1,))) for p, i in zip(products, inverses)]
    squares = jnp.stack([jnp.sum(c * c, axis=0) for c in columns])
    squares = squares + shift_along(squares, "core", 1)
    squares = gather_sum(squares, "x")
    scales = 1.0 / jnp.sqrt(squares + EPSILON)
    results = []
    for number, buffer in enumerate(buffers):
        basis = columns[number] * scales[number][None, :]
        update_scale = math.sqrt(height * 32 * buffer.shape[1] * 8 / RANK)
        momentum = buffer - (1.0 - MOMENTUM_DECAY) * dot(
            orthos[number], columns[number], ((1,), (1,))
        )
        update = update_scale * dot(orthos[number], basis, ((1,), (1,)))
        results = results + [update, momentum, basis]
    return tuple(results)


def solution(mesh):
    devices = mesh.devices.reshape(tuple(SIZES.values()))
    finer = Mesh(devices, tuple(SIZES))
    wide = P(("z", "y"), ("x", "core"))
    tall = P(("x", "core"), None)
    return jax.shard_map(
        local,
        mesh=finer,
        in_specs=(wide, wide, tall) * 4,
        out_specs=(wide, wide, tall) * 4,
        check_vma=False,
    )
```

```python
import functools
import math

import jax
import jax.numpy as jnp
from jax import lax
from jax.experimental import pallas as pl
from jax.experimental.pallas import tpu as pltpu
from jax.sharding import Mesh
from jax.sharding import PartitionSpec as P

PRECISE = lax.Precision.HIGHEST
MOMENTUM_DECAY = 0.95
SHIFT_RATIO = 0.0001
EPSILON = 1e-06
RANK = 256
PANEL = 16
SIZES = {"z": 8, "y": 4, "x": 4, "core": 2}


def dot(left, right, dims):
    return lax.dot_general(
        left, right, (dims, ((), ())), precision=PRECISE, preferred_element_type=jnp.float32
    )


def split3(values):
    high = values.astype(jnp.bfloat16)
    rest = values - high.astype(jnp.float32)
    mid = rest.astype(jnp.bfloat16)
    low = (rest - mid.astype(jnp.float32)).astype(jnp.bfloat16)
    return high, mid, low


def inverse_kernel(place, own, next_1, next_2, next_3, packed, gram_ref, out_ref, work):
    for step, piece in enumerate((own, next_1, next_2, next_3)):
        rows = 32 * lax.rem(place[1] + step, 4)
        gram_ref[pl.ds(pl.multiple_of(rows, 32), 32), :] = piece[:32, :]
        gram_ref[pl.ds(pl.multiple_of(rows + 128, 32), 32), :] = piece[32:, :]
    gram = gram_ref[...]
    rows = lax.broadcasted_iota(jnp.int32, (RANK, RANK), 0)
    cols = lax.broadcasted_iota(jnp.int32, (RANK, RANK), 1)
    unit = jnp.where(rows == cols, 1.0, 0.0).astype(jnp.float32)
    shift = SHIFT_RATIO * jnp.sum(gram * unit) / RANK
    work[:, :RANK] = gram + shift * unit
    work[:, RANK:] = unit
    sub = lax.broadcasted_iota(jnp.int32, (PANEL, 128), 0)
    lane = lax.broadcasted_iota(jnp.int32, (PANEL, RANK), 1)

    def step(number, carry):
        start = pl.multiple_of(number * PANEL, PANEL)
        panel = work[pl.ds(start, PANEL), :]
        block = pltpu.roll(panel[:, :RANK], RANK - start, axis=1)[:, :128]
        columns = [jnp.broadcast_to(block[:, j : j + 1], (PANEL, 128)) for j in range(PANEL)]
        parts = [panel[:, 128 * i : 128 * (i + 1)] for i in range(4)]
        scale = jnp.zeros((PANEL, 128), jnp.float32)
        for j in range(PANEL):
            pivot = columns[j][j : j + 1, :]
            scale = jnp.where(sub == j, lax.rsqrt(pivot), scale)
            if j == PANEL - 1:
                break
            mult = jnp.where(sub > j, columns[j] * (1.0 / pivot), 0.0)
            for other in range(j + 1, PANEL):
                columns[other] = columns[other] - mult * columns[other][j : j + 1, :]
            parts = [part - mult * part[j : j + 1, :] for part in parts]
        done = jnp.concatenate([part * scale for part in parts], axis=1)
        out_ref[pl.ds(start, PANEL), :] = done[:, RANK:]
        left = jnp.where(lane >= start + PANEL, done[:, :RANK], 0.0)
        left_high, left_mid, left_low = split3(left)
        high, mid, low = split3(done)
        lhs = jnp.concatenate([left_high, left_high, left_mid, left_high, left_low, left_mid], axis=0)
        rhs = jnp.concatenate([high, mid, high, low, high, mid], axis=0)
        work[...] -= lax.dot_general(
            lhs, rhs, (((0,), (0,)), ((), ())), preferred_element_type=jnp.float32
        )
        return carry

    lax.fori_loop(0, RANK // PANEL, step, 0)
    packed[:64, :128] = out_ref[:64, :128]
    packed[:64, 128:] = out_ref[64:128, :128]
    packed[64:, :] = out_ref[128:, :]


def shift_along(values, axis, step):
    size = SIZES[axis]
    return lax.ppermute(values, axis, [((i + step) % size, i) for i in range(size)])


def call(body, outs, operands, name, scratch=()):
    memory = pl.BlockSpec(memory_space=pltpu.VMEM)
    return pl.pallas_call(
        body,
        out_shape=[jax.ShapeDtypeStruct(shape, jnp.float32) for shape in outs],
        in_specs=[pl.BlockSpec(memory_space=pltpu.SMEM)] + [memory] * (len(operands) - 1),
        out_specs=[memory] * len(outs),
        scratch_shapes=[pltpu.VMEM(shape, jnp.float32) for shape in scratch],
        compiler_params=pltpu.CompilerParams(vmem_limit_bytes=48 * 1024 * 1024),
        name=name,
    )(*operands)


def aligned(start, size):
    return pl.ds(pl.multiple_of(start, size), size)


def product_kernel(place, *refs):
    momenta, gradients, factors, (send, keep) = refs[:4], refs[4:8], refs[8:12], refs[12:]
    first = place[3] == 0
    for number in range(4):
        buffer = momenta[number][...] + gradients[number][...].astype(jnp.float32)
        product = dot(buffer, factors[number][...], ((1,), (0,)))
        keep[number] = jnp.where(first, product[:128], product[128:])
        send[number] = jnp.where(first, product[128:], product[:128])


def pair_kernel(place, keep, received, *outs):
    for step in range(4):
        number = lax.rem(place[2] + step, 4)
        outs[step][...] = keep[number] + received[number]


def cross_kernel(place, *refs):
    momenta, gradients, same, other = refs[:4], refs[4:8], refs[8:12], refs[12:16]
    outs, products = refs[16:20], refs[20]
    wide, narrow, gram = refs[21:]
    core = place[3]
    for step in range(4):
        number = lax.rem(place[2] + step, 4)
        products[number, aligned(128 * core, 128), :] = same[step][...]
        products[number, aligned(128 * (1 - core), 128), :] = other[step][...]
    for number in range(4):
        buffer = momenta[number][...] + gradients[number][...].astype(jnp.float32)
        crossed = dot(buffer, products[number], ((0,), (0,)))
        if number in (0, 3):
            wide[number // 3] = crossed
        else:
            narrow[number - 1] = crossed
    product = products[place[2]]
    left = products[place[2], :, aligned(128 * core, 128)]
    gram[...] = dot(left, product, ((0,), (0,)))
    for step in range(4):
        row = lax.rem(place[1] + step, 4)
        for deep in range(8):
            start = 72 * deep
            rows = aligned(256 * row + 32 * deep, 32)
            outs[step][start : start + 32, :] = wide[0, rows, :]
            outs[step][start + 32 : start + 64, :] = wide[1, rows, :]
            rows = aligned(32 * row + 8 * (deep % 4), 8)
            outs[step][start + 64 : start + 72, :] = narrow[deep // 4, rows, :]
        outs[step][576:, :] = gram[aligned(32 * row, 32), :]


def row_kernel(place, *refs):
    pieces, outs, total = refs[:4], refs[4:12], refs[12]
    total[...] = pieces[0][...] + pieces[1][...] + pieces[2][...] + pieces[3][...]
    for step in range(8):
        deep = lax.rem(place[0] + step, 8)
        outs[step][:72, :] = total[pl.ds(pl.multiple_of(72 * deep, 8), 72), :]
        outs[step][72:, :] = total[576:, :]


def deep_kernel(place, *refs):
    pieces, shard, gram, terms = refs[:8], refs[8], refs[9], refs[10]
    total = pieces[0][:72, :]
    for step in range(1, 8):
        total = total + pieces[step][:72, :]
    shard[...] = total
    for step in range(8):
        terms[lax.rem(place[0] + 8 - step, 8)] = pieces[step][72:, :]
    total = terms[0]
    for step in range(1, 8):
        total = total + terms[step]
    gram[...] = total


def join_kernel(place, *refs):
    pieces, out = refs[:8], refs[8]
    for step in range(8):
        deep = lax.rem(place[0] + step, 8)
        out[pl.ds(pl.multiple_of(72 * deep, 8), 72), :] = pieces[step][...]


def column_kernel(place, *refs):
    packed, products, pieces = refs[:4], refs[4], refs[5:9]
    columns, orthos, squares = refs[9:13], refs[13], refs[14]
    inverses, wide, narrow = refs[15:]
    zero = jnp.zeros((128, 128), jnp.float32)
    for step in range(4):
        number = lax.rem(place[2] + step, 4)
        inverses[number, :64, :128] = packed[step][:64, :128]
        inverses[number, 64:128, :128] = packed[step][:64, 128:]
        inverses[number, :128, 128:] = zero
        inverses[number, 128:, :] = packed[step][64:, :]
        row = lax.rem(place[1] + step, 4)
        for deep in range(8):
            start = 72 * deep
            rows = aligned(256 * row + 32 * deep, 32)
            wide[0, rows, :] = pieces[step][start : start + 32, :]
            wide[1, rows, :] = pieces[step][start + 32 : start + 64, :]
            rows = aligned(32 * row + 8 * (deep % 4), 8)
            narrow[deep // 4, rows, :] = pieces[step][start + 64 : start + 72, :]
    for number in range(4):
        crossed = wide[number // 3] if number in (0, 3) else narrow[number - 1]
        column = dot(crossed, inverses[number], ((1,), (1,)))
        columns[number][...] = column
        squares[number : number + 1, :] = jnp.sum(column * column, axis=0, keepdims=True)
    for number in range(4):
        orthos[number] = dot(products[number], inverses[number], ((1,), (1,)))


def local(*arguments):
    momenta = arguments[0::3]
    gradients = arguments[1::3]
    factors = arguments[2::3]
    height = momenta[0].shape[0]
    place = jnp.stack([lax.axis_index(axis) for axis in SIZES]).astype(jnp.int32)

    half = (128, RANK)
    send, keep = call(
        product_kernel,
        [(4,) + half] * 2,
        (place, *momenta, *gradients, *factors),
        "products",
    )
    received = shift_along(send, "core", 1)
    pieces = call(pair_kernel, [half] * 4, (place, keep, received), "pairs")
    shard = pieces[0]
    for step in range(1, 4):
        shard = shard + shift_along(pieces[step], "x", -step)
    same = [shard] + [shift_along(shard, "x", step) for step in range(1, 4)]
    other = [shift_along(piece, "core", 1) for piece in same]

    *pieces, products = call(
        cross_kernel,
        [(608, RANK)] * 4 + [(4, RANK, RANK)],
        (place, *momenta, *gradients, *same, *other),
        "crosses",
        [(2, 1024, RANK), (2, 128, RANK), half],
    )
    pieces = [pieces[0]] + [shift_along(pieces[step], "y", -step) for step in range(1, 4)]
    pieces = call(row_kernel, [(104, RANK)] * 8, (place, *pieces), "rows", [(608, RANK)])
    pieces = [pieces[0]] + [shift_along(pieces[step], "z", -step) for step in range(1, 8)]
    shard, gram = call(
        deep_kernel, [(72, RANK), (32, RANK)], (place, *pieces), "deeps", [(8, 32, RANK)]
    )

    beside = shift_along(gram, "core", 1)
    first = place[3] == 0
    pair = jnp.concatenate([jnp.where(first, gram, beside), jnp.where(first, beside, gram)], axis=0)
    rows = [pair] + [shift_along(pair, "y", step) for step in range(1, 4)]
    (packed,) = call(
        inverse_kernel,
        [(192, RANK)],
        (place, *rows),
        "inverse",
        [(RANK, RANK), (RANK, RANK), (RANK, 2 * RANK)],
    )
    packed = [packed] + [shift_along(packed, "x", step) for step in range(1, 4)]

    pieces = [shard] + [shift_along(shard, "z", step) for step in range(1, 8)]
    (joined,) = call(join_kernel, [(576, RANK)], (place, *pieces), "joins")
    pieces = [joined] + [shift_along(joined, "y", step) for step in range(1, 4)]

    tall = [(momentum.shape[1], RANK) for momentum in momenta]
    *columns, orthos, squares = call(
        column_kernel,
        tall + [(4, RANK, RANK), (4, RANK)],
        (place, *packed, products, *pieces),
        "columns",
        [(4, RANK, RANK), (2, 1024, RANK), (2, 128, RANK)],
    )
    squares = squares + shift_along(squares, "core", 1)
    squares = squares + sum(shift_along(squares, "x", step) for step in range(1, 4))
    scales = 1.0 / jnp.sqrt(squares + EPSILON)
    results = []
    for number, column in enumerate(columns):
        buffer = momenta[number] + gradients[number].astype(jnp.float32)
        basis = column * scales[number][None, :]
        update_scale = math.sqrt(height * 32 * buffer.shape[1] * 8 / RANK)
        momentum = buffer - (1.0 - MOMENTUM_DECAY) * dot(orthos[number], column, ((1,), (1,)))
        update = update_scale * dot(orthos[number], basis, ((1,), (1,)))
        results = results + [update, momentum, basis]
    return tuple(results)


def solution(mesh):
    devices = mesh.devices.reshape(tuple(SIZES.values()))
    finer = Mesh(devices, tuple(SIZES))
    wide = P(("z", "y"), ("x", "core"))
    tall = P(("x", "core"), None)
    return jax.shard_map(
        local,
        mesh=finer,
        in_specs=(wide, wide, tall) * 4,
        out_specs=(wide, wide, tall) * 4,
        check_vma=False,
    )
```

```python
import functools
import math

import jax
import jax.numpy as jnp
from jax import lax
from jax.experimental import pallas as pl
from jax.experimental.pallas import tpu as pltpu
from jax.sharding import Mesh
from jax.sharding import PartitionSpec as P

PRECISE = lax.Precision.HIGHEST
MOMENTUM_DECAY = 0.95
SHIFT_RATIO = 0.0001
EPSILON = 1e-06
RANK = 256
PANEL = 16
SIZES = {"z": 8, "y": 4, "x": 4, "core": 2}


def dot(left, right, dims):
    return lax.dot_general(
        left, right, (dims, ((), ())), precision=PRECISE, preferred_element_type=jnp.float32
    )


def dot_three(left, right):
    return lax.dot_general(
        left,
        right,
        (((1,), (1,)), ((), ())),
        precision=lax.Precision.HIGH,
        preferred_element_type=jnp.float32,
    )


def split3(values):
    high = values.astype(jnp.bfloat16)
    rest = values - high.astype(jnp.float32)
    mid = rest.astype(jnp.bfloat16)
    low = (rest - mid.astype(jnp.float32)).astype(jnp.bfloat16)
    return high, mid, low


def inverse_kernel(place, own, next_1, next_2, next_3, packed, gram_ref, out_ref, work):
    for step, piece in enumerate((own, next_1, next_2, next_3)):
        rows = 32 * lax.rem(place[1] + step, 4)
        gram_ref[pl.ds(pl.multiple_of(rows, 32), 32), :] = piece[:32, :]
        gram_ref[pl.ds(pl.multiple_of(rows + 128, 32), 32), :] = piece[32:, :]
    gram = gram_ref[...]
    rows = lax.broadcasted_iota(jnp.int32, (RANK, RANK), 0)
    cols = lax.broadcasted_iota(jnp.int32, (RANK, RANK), 1)
    unit = jnp.where(rows == cols, 1.0, 0.0).astype(jnp.float32)
    shift = SHIFT_RATIO * jnp.sum(gram * unit) / RANK
    work[:, :RANK] = gram + shift * unit
    work[:, RANK:] = unit
    sub = lax.broadcasted_iota(jnp.int32, (PANEL, 128), 0)
    lane = lax.broadcasted_iota(jnp.int32, (PANEL, RANK), 1)

    def step(number, carry):
        start = pl.multiple_of(number * PANEL, PANEL)
        panel = work[pl.ds(start, PANEL), :]
        block = pltpu.roll(panel[:, :RANK], RANK - start, axis=1)[:, :128]
        columns = [jnp.broadcast_to(block[:, j : j + 1], (PANEL, 128)) for j in range(PANEL)]
        parts = [panel[:, 128 * i : 128 * (i + 1)] for i in range(4)]
        scale = jnp.zeros((PANEL, 128), jnp.float32)
        for j in range(PANEL):
            pivot = columns[j][j : j + 1, :]
            scale = jnp.where(sub == j, lax.rsqrt(pivot), scale)
            if j == PANEL - 1:
                break
            mult = jnp.where(sub > j, columns[j] * (1.0 / pivot), 0.0)
            for other in range(j + 1, PANEL):
                columns[other] = columns[other] - mult * columns[other][j : j + 1, :]
            parts = [part - mult * part[j : j + 1, :] for part in parts]
        done = jnp.concatenate([part * scale for part in parts], axis=1)
        out_ref[pl.ds(start, PANEL), :] = done[:, RANK:]
        left = jnp.where(lane >= start + PANEL, done[:, :RANK], 0.0)
        left_high, left_mid, left_low = split3(left)
        high, mid, low = split3(done)
        lhs = jnp.concatenate([left_high, left_high, left_mid, left_high, left_low, left_mid], axis=0)
        rhs = jnp.concatenate([high, mid, high, low, high, mid], axis=0)
        work[...] -= lax.dot_general(
            lhs, rhs, (((0,), (0,)), ((), ())), preferred_element_type=jnp.float32
        )
        return carry

    lax.fori_loop(0, RANK // PANEL, step, 0)
    packed[:64, :128] = out_ref[:64, :128]
    packed[:64, 128:] = out_ref[64:128, :128]
    packed[64:, :] = out_ref[128:, :]


def shift_along(values, axis, step):
    size = SIZES[axis]
    return lax.ppermute(values, axis, [((i + step) % size, i) for i in range(size)])


def neighbours(near, far):
    pairs = [(i, i ^ 1) for i in range(8)]
    others = [(i, (i + 1) % 8 if i % 2 else (i + 7) % 8) for i in range(8)]
    return lax.ppermute(near, "z", pairs), lax.ppermute(far, "z", others)


def call(body, outs, operands, name, scratch=()):
    memory = pl.BlockSpec(memory_space=pltpu.VMEM)
    return pl.pallas_call(
        body,
        out_shape=[jax.ShapeDtypeStruct(shape, jnp.float32) for shape in outs],
        in_specs=[pl.BlockSpec(memory_space=pltpu.SMEM)] + [memory] * (len(operands) - 1),
        out_specs=[memory] * len(outs),
        scratch_shapes=[pltpu.VMEM(shape, jnp.float32) for shape in scratch],
        compiler_params=pltpu.CompilerParams(vmem_limit_bytes=48 * 1024 * 1024),
        name=name,
    )(*operands)


def aligned(start, size):
    return pl.ds(pl.multiple_of(start, size), size)


def product_kernel(place, *refs):
    send, keep = refs[12:14]
    held, arrived = refs[14:26], refs[26]
    copies = [
        pltpu.make_async_copy(refs[index], held[index], arrived.at[index]) for index in range(12)
    ]
    order = (1, 2, 0, 3)
    for number in order:
        for index in (8 + number, number, 4 + number):
            copies[index].start()
    first = place[3] == 0
    for number in order:
        for index in (8 + number, number, 4 + number):
            copies[index].wait()
        buffer = held[number][...] + held[4 + number][...].astype(jnp.float32)
        product = dot(buffer, held[8 + number][...], ((1,), (0,)))
        keep[number] = jnp.where(first, product[:128], product[128:])
        send[number] = jnp.where(first, product[128:], product[:128])


def product_call(place, arguments):
    memory = pl.BlockSpec(memory_space=pltpu.VMEM)
    return pl.pallas_call(
        product_kernel,
        out_shape=[jax.ShapeDtypeStruct((4, 128, RANK), jnp.float32)] * 2,
        in_specs=[pl.BlockSpec(memory_space=pltpu.SMEM)] + [pl.BlockSpec(memory_space=pl.ANY)] * 12,
        out_specs=[memory] * 2,
        scratch_shapes=[pltpu.VMEM(value.shape, value.dtype) for value in arguments]
        + [pltpu.SemaphoreType.DMA((12,))],
        compiler_params=pltpu.CompilerParams(vmem_limit_bytes=60 * 1024 * 1024),
        name="products",
    )(place, *arguments)


def pair_kernel(place, keep, received, *outs):
    for step in range(4):
        number = lax.rem(place[2] + step, 4)
        outs[step][...] = keep[number] + received[number]


def cross_kernel(place, *refs):
    momenta, gradients, same, other = refs[:4], refs[4:8], refs[8:12], refs[12:16]
    outs, products = refs[16:20], refs[20]
    wide, narrow, gram = refs[21:]
    core = place[3]
    for step in range(4):
        number = lax.rem(place[2] + step, 4)
        products[number, aligned(128 * core, 128), :] = same[step][...]
        products[number, aligned(128 * (1 - core), 128), :] = other[step][...]
    for number in range(4):
        buffer = momenta[number][...] + gradients[number][...].astype(jnp.float32)
        crossed = dot(buffer, products[number], ((0,), (0,)))
        if number in (0, 3):
            wide[number // 3] = crossed
        else:
            narrow[number - 1] = crossed
    product = products[place[2]]
    left = products[place[2], :, aligned(128 * core, 128)]
    gram[...] = dot(left, product, ((0,), (0,)))
    for step in range(4):
        row = lax.rem(place[1] + step, 4)
        for deep in range(8):
            start = 72 * deep
            rows = aligned(256 * row + 32 * deep, 32)
            outs[step][start : start + 32, :] = wide[0, rows, :]
            outs[step][start + 32 : start + 64, :] = wide[1, rows, :]
            rows = aligned(32 * row + 8 * (deep % 4), 8)
            outs[step][start + 64 : start + 72, :] = narrow[deep // 4, rows, :]
        outs[step][576:, :] = gram[aligned(32 * row, 32), :]


def row_kernel(place, *refs):
    pieces, (keep, near, far), total = refs[:4], refs[4:7], refs[7]
    total[...] = pieces[0][...] + pieces[1][...] + pieces[2][...] + pieces[3][...]
    parity = lax.rem(place[0], 2)
    for block in range(4):
        rows = slice(72 * block, 72 * block + 72)
        keep[rows, :] = total[tall_rows(2 * block + parity), :]
        out = (near, far)[block // 2]
        rows = slice(72 * (block % 2), 72 * (block % 2) + 72)
        out[rows, :] = total[tall_rows(2 * block + 1 - parity), :]
    keep[288:, :] = total[576:, :]
    near[144:, :] = total[576:592, :]
    far[144:, :] = total[592:, :]


def tall_rows(block):
    return pl.ds(pl.multiple_of(72 * block, 8), 72)


def neighbour_kernel(place, keep, near, far, *refs):
    outs, total = refs[:4], refs[4]
    total[:144, :] = keep[:144, :] + near[:144, :]
    total[144:288, :] = keep[144:288, :] + far[:144, :]
    total[288:304, :] = keep[288:304, :] + near[144:, :]
    total[304:, :] = keep[304:, :] + far[144:, :]
    for step in range(4):
        block = lax.rem(place[0] // 2 + step, 4)
        outs[step][:72, :] = total[tall_rows(block), :]
        outs[step][72:, :] = total[288:, :]


def deep_kernel(place, *refs):
    pieces, shard, gram, terms = refs[:4], refs[4], refs[5], refs[6]
    shard[...] = (
        pieces[0][:72, :] + pieces[1][:72, :] + pieces[2][:72, :] + pieces[3][:72, :]
    )
    for step in range(4):
        source = lax.rem(place[0] + 8 - 2 * step, 8)
        terms[source // 2, :16, :] = pieces[step][72:88, :]
        terms[lax.rem((source + 1) // 2, 4), 16:, :] = pieces[step][88:, :]
    gram[...] = terms[0] + terms[1] + terms[2] + terms[3]


def quad_kernel(place, *refs):
    pieces, near, far, total = refs[:4], refs[4], refs[5], refs[6]
    for step in range(4):
        total[tall_rows(lax.rem(place[0] // 2 + step, 4)), :] = pieces[step][...]
    near[...] = total[:144, :]
    far[...] = total[144:, :]


def join_kernel(place, *refs):
    same, other, out = refs[:2], refs[2:4], refs[4]
    parity = lax.rem(place[0], 2)
    for block in range(4):
        rows = slice(72 * (block % 2), 72 * (block % 2) + 72)
        out[tall_rows(2 * block + parity), :] = same[block // 2][rows, :]
        out[tall_rows(2 * block + 1 - parity), :] = other[block // 2][rows, :]


def ortho_kernel(place, *refs):
    packed, products, orthos, inverses = refs[:4], refs[4], refs[5], refs[6]
    zero = jnp.zeros((128, 128), jnp.float32)
    for step in range(4):
        number = lax.rem(place[2] + step, 4)
        inverses[number, :64, :128] = packed[step][:64, :128]
        inverses[number, 64:128, :128] = packed[step][:64, 128:]
        inverses[number, :128, 128:] = zero
        inverses[number, 128:, :] = packed[step][64:, :]
    for number in range(4):
        orthos[number] = dot(products[number], inverses[number], ((1,), (1,)))


def column_kernel(place, *refs):
    inverses, pieces = refs[0], refs[1:5]
    columns, squares, wide, narrow = refs[5:9], refs[9], refs[10], refs[11]
    for step in range(4):
        row = lax.rem(place[1] + step, 4)
        for deep in range(8):
            start = 72 * deep
            rows = aligned(256 * row + 32 * deep, 32)
            wide[0, rows, :] = pieces[step][start : start + 32, :]
            wide[1, rows, :] = pieces[step][start + 32 : start + 64, :]
            rows = aligned(32 * row + 8 * (deep % 4), 8)
            narrow[deep // 4, rows, :] = pieces[step][start + 64 : start + 72, :]
    for number in range(4):
        crossed = wide[number // 3] if number in (0, 3) else narrow[number - 1]
        column = dot(crossed, inverses[number], ((1,), (1,)))
        columns[number][...] = column
        squares[number : number + 1, :] = jnp.sum(column * column, axis=0, keepdims=True)


def local(*arguments):
    momenta = arguments[0::3]
    gradients = arguments[1::3]
    factors = arguments[2::3]
    height = momenta[0].shape[0]
    place = jnp.stack([lax.axis_index(axis) for axis in SIZES]).astype(jnp.int32)

    half = (128, RANK)
    send, keep = product_call(place, (*momenta, *gradients, *factors))
    received = shift_along(send, "core", 1)
    pieces = call(pair_kernel, [half] * 4, (place, keep, received), "pairs")
    shard = pieces[0]
    for step in range(1, 4):
        shard = shard + shift_along(pieces[step], "x", -step)
    same = [shard] + [shift_along(shard, "x", step) for step in range(1, 4)]
    other = [shift_along(piece, "core", 1) for piece in same]

    *pieces, products = call(
        cross_kernel,
        [(608, RANK)] * 4 + [(4, RANK, RANK)],
        (place, *momenta, *gradients, *same, *other),
        "crosses",
        [(2, 1024, RANK), (2, 128, RANK), half],
    )
    pieces = [pieces[0]] + [shift_along(pieces[step], "y", -step) for step in range(1, 4)]
    keep, near, far = call(
        row_kernel,
        [(320, RANK), (160, RANK), (160, RANK)],
        (place, *pieces),
        "rows",
        [(608, RANK)],
    )
    near, far = neighbours(near, far)
    pieces = call(
        neighbour_kernel, [(104, RANK)] * 4, (place, keep, near, far), "neighbours", [(320, RANK)]
    )
    pieces = [pieces[0]] + [shift_along(pieces[step], "z", -2 * step) for step in range(1, 4)]
    shard, gram = call(
        deep_kernel, [(72, RANK), (32, RANK)], (place, *pieces), "deeps", [(4, 32, RANK)]
    )

    beside = shift_along(gram, "core", 1)
    first = place[3] == 0
    pair = jnp.concatenate([jnp.where(first, gram, beside), jnp.where(first, beside, gram)], axis=0)
    rows = [pair] + [shift_along(pair, "y", step) for step in range(1, 4)]

    pieces = [shard] + [shift_along(shard, "z", 2 * step) for step in range(1, 4)]
    near, far = call(quad_kernel, [(144, RANK)] * 2, (place, *pieces), "quads", [(288, RANK)])
    (joined,) = call(
        join_kernel, [(576, RANK)], (place, near, far, *neighbours(near, far)), "joins"
    )
    joined, rows = lax.optimization_barrier((joined, rows))
    pieces = [joined] + [shift_along(joined, "y", step) for step in range(1, 4)]

    (packed,) = call(
        inverse_kernel,
        [(192, RANK)],
        (place, *rows),
        "inverse",
        [(RANK, RANK), (RANK, RANK), (RANK, 2 * RANK)],
    )
    packed = [packed] + [shift_along(packed, "x", step) for step in range(1, 4)]
    orthos, inverses = call(
        ortho_kernel, [(4, RANK, RANK)] * 2, (place, *packed, products), "orthos"
    )

    tall = [(momentum.shape[1], RANK) for momentum in momenta]
    *columns, squares = call(
        column_kernel,
        tall + [(4, RANK)],
        (place, inverses, *pieces),
        "columns",
        [(2, 1024, RANK), (2, 128, RANK)],
    )
    squares = squares + shift_along(squares, "core", 1)
    squares = squares + sum(shift_along(squares, "x", step) for step in range(1, 4))
    scales = 1.0 / jnp.sqrt(squares + EPSILON)
    results = []
    for number, column in enumerate(columns):
        buffer = momenta[number] + gradients[number].astype(jnp.float32)
        basis = column * scales[number][None, :]
        update_scale = math.sqrt(height * 32 * buffer.shape[1] * 8 / RANK)
        momentum = buffer - (1.0 - MOMENTUM_DECAY) * dot_three(orthos[number], column)
        update = update_scale * dot_three(orthos[number], basis)
        results = results + [update, momentum, basis]
    return tuple(results)


def solution(mesh):
    devices = mesh.devices.reshape(tuple(SIZES.values()))
    finer = Mesh(devices, tuple(SIZES))
    wide = P(("z", "y"), ("x", "core"))
    tall = P(("x", "core"), None)
    return jax.shard_map(
        local,
        mesh=finer,
        in_specs=(wide, wide, tall) * 4,
        out_specs=(wide, wide, tall) * 4,
        check_vma=False,
    )
```

```python
import functools
import math

import jax
import jax.numpy as jnp
from jax import lax
from jax.experimental import pallas as pl
from jax.experimental.pallas import tpu as pltpu
from jax.sharding import Mesh
from jax.sharding import PartitionSpec as P

PRECISE = lax.Precision.HIGHEST
MOMENTUM_DECAY = 0.95
SHIFT_RATIO = 0.0001
EPSILON = 1e-06
RANK = 256
PANEL = 16
SIZES = {"z": 8, "y": 4, "x": 4, "core": 2}


def dot(left, right, dims):
    return lax.dot_general(
        left, right, (dims, ((), ())), precision=PRECISE, preferred_element_type=jnp.float32
    )


def dot_three(left, right):
    dims = (((1,), (1,)), ((), ()))
    parts = []
    for values in (left, right):
        high = values.astype(jnp.bfloat16)
        parts.append((high, (values - high.astype(jnp.float32)).astype(jnp.bfloat16)))
    (left_high, left_low), (right_high, right_low) = parts
    total = lax.dot_general(left_low, right_high, dims, preferred_element_type=jnp.float32)
    total = total + lax.dot_general(left_high, right_low, dims, preferred_element_type=jnp.float32)
    return total + lax.dot_general(left_high, right_high, dims, preferred_element_type=jnp.float32)


def split3(values):
    high = values.astype(jnp.bfloat16)
    rest = values - high.astype(jnp.float32)
    mid = rest.astype(jnp.bfloat16)
    low = (rest - mid.astype(jnp.float32)).astype(jnp.bfloat16)
    return high, mid, low


def inverse_kernel(place, own, next_1, next_2, next_3, packed, mine, gram_ref, out_ref, work):
    for step, piece in enumerate((own, next_1, next_2, next_3)):
        rows = 32 * lax.rem(place[1] + step, 4)
        gram_ref[pl.ds(pl.multiple_of(rows, 32), 32), :] = piece[:32, :]
        gram_ref[pl.ds(pl.multiple_of(rows + 128, 32), 32), :] = piece[32:, :]
    gram = gram_ref[...]
    rows = lax.broadcasted_iota(jnp.int32, (RANK, RANK), 0)
    cols = lax.broadcasted_iota(jnp.int32, (RANK, RANK), 1)
    unit = jnp.where(rows == cols, 1.0, 0.0).astype(jnp.float32)
    shift = SHIFT_RATIO * jnp.sum(gram * unit) / RANK
    work[:, :RANK] = gram + shift * unit
    work[:, RANK:] = unit
    sub = lax.broadcasted_iota(jnp.int32, (PANEL, 128), 0)
    lane = lax.broadcasted_iota(jnp.int32, (PANEL, RANK), 1)

    def step(number, carry):
        start = pl.multiple_of(number * PANEL, PANEL)
        panel = work[pl.ds(start, PANEL), :]
        block = pltpu.roll(panel[:, :RANK], RANK - start, axis=1)[:, :128]
        columns = [jnp.broadcast_to(block[:, j : j + 1], (PANEL, 128)) for j in range(PANEL)]
        parts = [panel[:, 128 * i : 128 * (i + 1)] for i in range(4)]
        scale = jnp.zeros((PANEL, 128), jnp.float32)
        for j in range(PANEL):
            pivot = columns[j][j : j + 1, :]
            scale = jnp.where(sub == j, lax.rsqrt(pivot), scale)
            if j == PANEL - 1:
                break
            mult = jnp.where(sub > j, columns[j] * (1.0 / pivot), 0.0)
            for other in range(j + 1, PANEL):
                columns[other] = columns[other] - mult * columns[other][j : j + 1, :]
            parts = [part - mult * part[j : j + 1, :] for part in parts]
        done = jnp.concatenate([part * scale for part in parts], axis=1)
        out_ref[pl.ds(start, PANEL), :] = done[:, RANK:]
        left = jnp.where(lane >= start + PANEL, done[:, :RANK], 0.0)
        left_high, left_mid, left_low = split3(left)
        high, mid, low = split3(done)
        lhs = jnp.concatenate([left_high, left_high, left_mid, left_high, left_low, left_mid], axis=0)
        rhs = jnp.concatenate([high, mid, high, low, high, mid], axis=0)
        work[...] -= lax.dot_general(
            lhs, rhs, (((0,), (0,)), ((), ())), preferred_element_type=jnp.float32
        )
        return carry

    lax.fori_loop(0, RANK // PANEL, step, 0)
    packed[:64, :128] = out_ref[:64, :128]
    packed[:64, 128:] = out_ref[64:128, :128]
    packed[64:, :] = out_ref[128:, :]
    mine[...] = packed[aligned(96 * place[3], 8, 96), :]


def shift_along(values, axis, step):
    size = SIZES[axis]
    return lax.ppermute(values, axis, [((i + step) % size, i) for i in range(size)])


def neighbours(near, far):
    pairs = [(i, i ^ 1) for i in range(8)]
    others = [(i, (i + 1) % 8 if i % 2 else (i + 7) % 8) for i in range(8)]
    return lax.ppermute(near, "z", pairs), lax.ppermute(far, "z", others)


def cost(micros):
    return pl.CostEstimate(flops=int(1.1e9 * micros), bytes_accessed=0, transcendentals=0)


def call(body, outs, operands, name, scratch=(), micros=1):
    memory = pl.BlockSpec(memory_space=pltpu.VMEM)
    return pl.pallas_call(
        body,
        out_shape=[jax.ShapeDtypeStruct(shape, jnp.float32) for shape in outs],
        in_specs=[pl.BlockSpec(memory_space=pltpu.SMEM)] + [memory] * (len(operands) - 1),
        out_specs=[memory] * len(outs),
        scratch_shapes=[pltpu.VMEM(shape, jnp.float32) for shape in scratch],
        cost_estimate=cost(micros),
        compiler_params=pltpu.CompilerParams(vmem_limit_bytes=48 * 1024 * 1024),
        name=name,
    )(*operands)


def aligned(start, multiple, size=None):
    return pl.ds(pl.multiple_of(start, multiple), size or multiple)


def product_kernel(count, place, *refs):
    send, keep = refs[3 * count : 3 * count + 2]
    held, arrived = refs[3 * count + 2 : -1], refs[-1]
    copies = [
        pltpu.make_async_copy(refs[index], held[index], arrived.at[index])
        for index in range(3 * count)
    ]
    for number in range(count):
        for index in (2 * count + number, number, count + number):
            copies[index].start()
    first = place[3] == 0
    for number in range(count):
        for index in (2 * count + number, number, count + number):
            copies[index].wait()
        buffer = held[number][...] + held[count + number][...].astype(jnp.float32)
        product = dot(buffer, held[2 * count + number][...], ((1,), (0,)))
        keep[number] = jnp.where(first, product[:128], product[128:])
        send[number] = jnp.where(first, product[128:], product[:128])


def product_call(place, arguments):
    memory = pl.BlockSpec(memory_space=pltpu.VMEM)
    count = len(arguments) // 3
    return pl.pallas_call(
        functools.partial(product_kernel, count),
        out_shape=[jax.ShapeDtypeStruct((count, 128, RANK), jnp.float32)] * 2,
        in_specs=[pl.BlockSpec(memory_space=pltpu.SMEM)]
        + [pl.BlockSpec(memory_space=pl.ANY)] * (3 * count),
        out_specs=[memory] * 2,
        scratch_shapes=[pltpu.VMEM(value.shape, value.dtype) for value in arguments]
        + [pltpu.SemaphoreType.DMA((3 * count,))],
        cost_estimate=cost(7),
        compiler_params=pltpu.CompilerParams(vmem_limit_bytes=60 * 1024 * 1024),
        name="products",
    )(place, *arguments)


def pair_kernel(place, keep, received, *outs):
    for step in range(4):
        number = lax.rem(place[2] + step, 4)
        outs[step][...] = keep[number] + received[number]


def cross_kernel(query, place, *refs):
    count = 1 if query else 3
    momenta, gradients, refs = refs[:count], refs[count : 2 * count], refs[2 * count :]
    core = place[3]
    if query:
        same, other, products, refs = refs[:4], refs[4:8], refs[13], refs[8:13] + refs[14:]
        for step in range(4):
            number = lax.rem(place[2] + step, 4)
            products[number, aligned(128 * core, 128), :] = same[step][...]
            products[number, aligned(128 * (1 - core), 128), :] = other[step][...]
    else:
        products, refs = refs[0], refs[1:]
    (own, plus_first, minus_first, plus_second, minus_second, wide), refs = refs[:6], refs[6:]
    if query:
        buffer = momenta[0][...] + gradients[0][...].astype(jnp.float32)
        wide[...] = dot(buffer, products[0], ((0,), (0,)))
    else:
        narrow, gram = refs
        for number in range(3):
            buffer = momenta[number][...] + gradients[number][...].astype(jnp.float32)
            crossed = dot(buffer, products[1 + number], ((0,), (0,)))
            if number == 2:
                wide[...] = crossed
            else:
                narrow[number] = crossed
        left = products[place[2], :, aligned(128 * core, 128)]
        gram[...] = dot(left, products[place[2]], ((0,), (0,)))

    def put(out, start, step, upper):
        row = lax.rem(place[1] + step, 4)
        for deep in range(4 * upper, 4 * upper + 4):
            out[start : start + 32, :] = wide[aligned(256 * row + 32 * deep, 32), :]
            start = start + 32
            if not query:
                out[start : start + 8, :] = narrow[upper, aligned(32 * row + 8 * (deep % 4), 8), :]
                start = start + 8
        if not query:
            out[start : start + 16, :] = gram[aligned(32 * row + 16 * upper, 16), :]

    half = own.shape[0] // 2
    put(plus_first, 0, 2, 0)
    put(minus_first, 0, 2, 1)
    put(plus_first, half, 1, 1)
    put(minus_first, half, 3, 0)
    put(plus_second, 0, 1, 0)
    put(minus_second, 0, 3, 1)
    put(own, 0, 0, 0)
    put(own, half, 0, 1)


def pass_kernel(place, plus, minus, plus_in, minus_in, plus_out, minus_out):
    half = plus.shape[0]
    plus_out[...] = plus[...] + plus_in[:half, :]
    minus_out[...] = minus[...] + minus_in[:half, :]


def cross_call(query, place, operands):
    half = 128 if query else 176
    outs = [(2 * half, RANK)] * 3 + [(half, RANK)] * 2
    scratch = [(1024, RANK)]
    if query:
        outs = outs + [(4, RANK, RANK)]
    else:
        scratch = scratch + [(2, 128, RANK), (128, RANK)]
    return call(
        functools.partial(cross_kernel, query),
        outs,
        (place, *operands),
        "crosses",
        scratch,
        2 if query else 3,
    )


def pass_call(place, plus, minus, plus_in, minus_in):
    return call(
        pass_kernel, [plus.shape] * 2, (place, plus, minus, plus_in, minus_in), "passes"
    )


def row_kernel(place, *refs):
    (keep, near, far), total = refs[10:13], refs[13]
    for pieces, size, start in ((refs[:5], 32, 0), (refs[5:10], 40, 32)):
        own, plus_in, minus_in, plus, minus = pieces
        half = own.shape[0] // 2
        lower = own[:half, :] + minus_in[half:, :] + plus[...]
        upper = own[half:, :] + plus_in[half:, :] + minus[...]
        for deep in range(8):
            piece = (lower, upper)[deep // 4][size * (deep % 4) : size * (deep % 4) + size, :]
            total[72 * deep + start : 72 * deep + start + size, :] = piece
    total[576:592, :] = lower[160:, :]
    total[592:, :] = upper[160:, :]
    parity = lax.rem(place[0], 2)
    for block in range(4):
        rows = slice(72 * block, 72 * block + 72)
        keep[rows, :] = total[tall_rows(2 * block + parity), :]
        out = (near, far)[block // 2]
        rows = slice(72 * (block % 2), 72 * (block % 2) + 72)
        out[rows, :] = total[tall_rows(2 * block + 1 - parity), :]
    keep[288:, :] = total[576:, :]
    near[144:, :] = total[576:592, :]
    far[144:, :] = total[592:, :]


def tall_rows(block):
    return pl.ds(pl.multiple_of(72 * block, 8), 72)


def neighbour_kernel(place, keep, near, far, *refs):
    outs, total = refs[:4], refs[4]
    total[:144, :] = keep[:144, :] + near[:144, :]
    total[144:288, :] = keep[144:288, :] + far[:144, :]
    total[288:304, :] = keep[288:304, :] + near[144:, :]
    total[304:, :] = keep[304:, :] + far[144:, :]
    for step in range(4):
        block = lax.rem(place[0] // 2 + step, 4)
        outs[step][:72, :] = total[tall_rows(block), :]
        outs[step][72:, :] = total[288:, :]


def deep_kernel(place, *refs):
    pieces, shard, gram, terms = refs[:4], refs[4], refs[5], refs[6]
    shard[...] = (
        pieces[0][:72, :] + pieces[1][:72, :] + pieces[2][:72, :] + pieces[3][:72, :]
    )
    for step in range(4):
        source = lax.rem(place[0] + 8 - 2 * step, 8)
        terms[source // 2, :16, :] = pieces[step][72:88, :]
        terms[lax.rem((source + 1) // 2, 4), 16:, :] = pieces[step][88:, :]
    gram[...] = terms[0] + terms[1] + terms[2] + terms[3]


def quad_kernel(place, *refs):
    pieces, near, far, total = refs[:4], refs[4], refs[5], refs[6]
    for step in range(4):
        total[tall_rows(lax.rem(place[0] // 2 + step, 4)), :] = pieces[step][...]
    near[...] = total[:144, :]
    far[...] = total[144:, :]


def join_kernel(place, *refs):
    same, other, total = refs[:2], refs[2:4], refs[4]
    parity = lax.rem(place[0], 2)
    for block in range(4):
        rows = slice(72 * (block % 2), 72 * (block % 2) + 72)
        total[tall_rows(2 * block + parity), :] = same[block // 2][rows, :]
        total[tall_rows(2 * block + 1 - parity), :] = other[block // 2][rows, :]


def forward_kernel(place, before, after, lower, upper):
    lower[...] = before[:288, :]
    upper[...] = after[288:, :]


def ortho_kernel(place, *refs):
    packed, same, other = refs[0], refs[1:4], refs[4:7]
    products, orthos, inverses, joined = refs[7:]
    core = place[3]
    joined[0] = packed[...]
    for step in range(1, 4):
        joined[step, aligned(96 * core, 8, 96), :] = same[step - 1][...]
        joined[step, aligned(96 * (1 - core), 8, 96), :] = other[step - 1][...]
    zero = jnp.zeros((128, 128), jnp.float32)
    for step in range(4):
        number = lax.rem(place[2] + step, 4)
        inverses[number, :64, :128] = joined[step, :64, :128]
        inverses[number, 64:128, :128] = joined[step, :64, 128:]
        inverses[number, :128, 128:] = zero
        inverses[number, 128:, :] = joined[step, 64:, :]
    for number in range(4):
        orthos[number] = dot(products[number], inverses[number], ((1,), (1,)))


def column_kernel(place, *refs):
    inverses, pieces = refs[0], refs[1:6]
    columns, squares, wide, narrow = refs[6:10], refs[10], refs[11], refs[12]
    for step in range(4):
        row = lax.rem(place[1] + step, 4)
        for deep in range(8):
            piece = pieces[(0, 1, 2 + deep // 4, 4)[step]]
            start = 72 * (deep % 4 if step == 2 else deep)
            rows = aligned(256 * row + 32 * deep, 32)
            wide[0, rows, :] = piece[start : start + 32, :]
            wide[1, rows, :] = piece[start + 32 : start + 64, :]
            rows = aligned(32 * row + 8 * (deep % 4), 8)
            narrow[deep // 4, rows, :] = piece[start + 64 : start + 72, :]
    for number in range(4):
        crossed = wide[number // 3] if number in (0, 3) else narrow[number - 1]
        column = dot(crossed, inverses[number], ((1,), (1,)))
        columns[number][...] = column
        squares[number : number + 1, :] = jnp.sum(column * column, axis=0, keepdims=True)


def momentum_kernel(place, *refs):
    momenta, gradients, columns, orthos, outs = refs[:4], refs[4:8], refs[8:12], refs[12], refs[13:]
    for number in range(4):
        buffer = momenta[number][...] + gradients[number][...].astype(jnp.float32)
        change = dot_three(orthos[number], columns[number][...])
        outs[number][...] = buffer - (1.0 - MOMENTUM_DECAY) * change


def update_kernel(scales, place, *refs):
    squares, columns, orthos, updates, bases = refs[0], refs[1:5], refs[5], refs[6:10], refs[10:]
    inverse = 1.0 / jnp.sqrt(squares[...] + EPSILON)
    for number in range(4):
        basis = columns[number][...] * inverse[number : number + 1, :]
        bases[number][...] = basis
        updates[number][...] = scales[number] * dot_three(orthos[number], basis)


def local(*arguments):
    momenta = arguments[0::3]
    gradients = arguments[1::3]
    factors = arguments[2::3]
    height = momenta[0].shape[0]
    place = jnp.stack([lax.axis_index(axis) for axis in SIZES]).astype(jnp.int32)

    half = (128, RANK)
    send, keep = product_call(place, (*momenta, *gradients, *factors))
    received = shift_along(send, "core", 1)
    pieces = call(pair_kernel, [half] * 4, (place, keep, received), "pairs")
    shard = pieces[0]
    for step in range(1, 4):
        shard = shard + shift_along(pieces[step], "x", -step)
    same = [shard] + [shift_along(shard, "x", step) for step in range(1, 4)]
    other = [shift_along(piece, "core", 1) for piece in same]

    *query, products = cross_call(True, place, (momenta[0], gradients[0], *same, *other))
    others = cross_call(False, place, (*momenta[1:], *gradients[1:], products))
    query_in = shift_along(query[1], "y", -1), shift_along(query[2], "y", 1)
    others_in = shift_along(others[1], "y", -1), shift_along(others[2], "y", 1)
    plus, minus = pass_call(place, query[3], query[4], *query_in)
    others_in, plus, minus = lax.optimization_barrier((others_in, plus, minus))
    query_pieces = (query[0], *query_in, shift_along(plus, "y", -1), shift_along(minus, "y", 1))
    plus, minus = pass_call(place, others[3], others[4], *others_in)
    other_pieces = (others[0], *others_in, shift_along(plus, "y", -1), shift_along(minus, "y", 1))

    keep, near, far = call(
        row_kernel,
        [(320, RANK), (160, RANK), (160, RANK)],
        (place, *query_pieces, *other_pieces),
        "rows",
        [(608, RANK)],
    )
    near, far = neighbours(near, far)
    pieces = call(
        neighbour_kernel, [(104, RANK)] * 4, (place, keep, near, far), "neighbours", [(320, RANK)]
    )
    pieces = [pieces[0]] + [shift_along(pieces[step], "z", -2 * step) for step in range(1, 4)]
    shard, gram = call(
        deep_kernel, [(72, RANK), (32, RANK)], (place, *pieces), "deeps", [(4, 32, RANK)]
    )

    beside = shift_along(gram, "core", 1)
    first = place[3] == 0
    pair = jnp.concatenate([jnp.where(first, gram, beside), jnp.where(first, beside, gram)], axis=0)
    rows = [pair] + [shift_along(pair, "y", step) for step in range(1, 4)]

    pieces = [shard] + [shift_along(shard, "z", 2 * step) for step in range(1, 4)]
    near, far = call(quad_kernel, [(144, RANK)] * 2, (place, *pieces), "quads", [(288, RANK)])
    (joined,) = call(
        join_kernel, [(576, RANK)], (place, near, far, *neighbours(near, far)), "joins"
    )
    joined, rows = lax.optimization_barrier((joined, rows))
    before = shift_along(joined, "y", -1)
    after = shift_along(joined, "y", 1)
    lower, upper = call(forward_kernel, [(288, RANK)] * 2, (place, before, after), "forwards")

    packed, mine = call(
        inverse_kernel,
        [(192, RANK), (96, RANK)],
        (place, *rows),
        "inverse",
        [(RANK, RANK), (RANK, RANK), (RANK, 2 * RANK)],
        11,
    )
    mine, lower, upper = lax.optimization_barrier((mine, lower, upper))
    lower = shift_along(lower, "y", -1)
    upper = shift_along(upper, "y", 1)
    same = [shift_along(mine, "x", step) for step in range(1, 4)]
    other = [shift_along(piece, "core", 1) for piece in same]
    orthos, inverses = call(
        ortho_kernel,
        [(4, RANK, RANK)] * 2,
        (place, packed, *same, *other, products),
        "orthos",
        [(4, 192, RANK)],
        2,
    )

    tall = [(momentum.shape[1], RANK) for momentum in momenta]
    flat = [momentum.shape for momentum in momenta]
    *columns, squares = call(
        column_kernel,
        tall + [(4, RANK)],
        (place, inverses, joined, after, lower, upper, before),
        "columns",
        [(2, 1024, RANK), (2, 128, RANK)],
        3,
    )
    squares = squares + shift_along(squares, "core", 1)
    squares = squares + sum(shift_along(squares, "x", step) for step in range(1, 4))
    new_momenta = call(
        momentum_kernel, flat, (place, *momenta, *gradients, *columns, orthos), "momenta", (), 3
    )
    scales = [math.sqrt(height * 32 * shape[1] * 8 / RANK) for shape in flat]
    outs = call(
        functools.partial(update_kernel, scales),
        flat + tall,
        (place, squares, *columns, orthos),
        "updates",
        (),
        3,
    )
    results = []
    for number in range(4):
        results = results + [outs[number], new_momenta[number], outs[4 + number]]
    return tuple(results)


def solution(mesh):
    devices = mesh.devices.reshape(tuple(SIZES.values()))
    finer = Mesh(devices, tuple(SIZES))
    wide = P(("z", "y"), ("x", "core"))
    tall = P(("x", "core"), None)
    return jax.shard_map(
        local,
        mesh=finer,
        in_specs=(wide, wide, tall) * 4,
        out_specs=(wide, wide, tall) * 4,
        check_vma=False,
    )
```

```python
import functools
import math

import jax
import jax.numpy as jnp
from jax import lax
from jax.experimental import pallas as pl
from jax.experimental.pallas import tpu as pltpu
from jax.sharding import Mesh
from jax.sharding import PartitionSpec as P

PRECISE = lax.Precision.HIGHEST
MOMENTUM_DECAY = 0.95
SHIFT_RATIO = 0.0001
EPSILON = 1e-06
RANK = 256
PANEL = 16
FOUR = (0, 2, 1, 3)
SIZES = {"z": 8, "y": 4, "x": 4, "core": 2}


def dot(left, right, dims):
    return lax.dot_general(
        left, right, (dims, ((), ())), precision=PRECISE, preferred_element_type=jnp.float32
    )


def dot_three(left, right):
    dims = (((1,), (1,)), ((), ()))
    parts = []
    for values in (left, right):
        high = values.astype(jnp.bfloat16)
        parts.append((high, (values - high.astype(jnp.float32)).astype(jnp.bfloat16)))
    (left_high, left_low), (right_high, right_low) = parts
    total = lax.dot_general(left_low, right_high, dims, preferred_element_type=jnp.float32)
    total = total + lax.dot_general(left_high, right_low, dims, preferred_element_type=jnp.float32)
    return total + lax.dot_general(left_high, right_high, dims, preferred_element_type=jnp.float32)


def split3(values):
    high = values.astype(jnp.bfloat16)
    rest = values - high.astype(jnp.float32)
    mid = rest.astype(jnp.bfloat16)
    low = (rest - mid.astype(jnp.float32)).astype(jnp.bfloat16)
    return high, mid, low


def inverse_kernel(place, *refs):
    pieces, (packed, mine, gram_ref, out_ref, work) = refs[:4], refs[4:]
    for step, piece in zip(FOUR, pieces):
        rows = 32 * lax.rem(place[1] + step, 4)
        gram_ref[pl.ds(pl.multiple_of(rows, 32), 32), :] = piece[:32, :]
        gram_ref[pl.ds(pl.multiple_of(rows + 128, 32), 32), :] = piece[32:, :]
    gram = gram_ref[...]
    rows = lax.broadcasted_iota(jnp.int32, (RANK, RANK), 0)
    cols = lax.broadcasted_iota(jnp.int32, (RANK, RANK), 1)
    unit = jnp.where(rows == cols, 1.0, 0.0).astype(jnp.float32)
    shift = SHIFT_RATIO * jnp.sum(gram * unit) / RANK
    work[:, :RANK] = gram + shift * unit
    work[:, RANK:] = unit
    sub = lax.broadcasted_iota(jnp.int32, (PANEL, 128), 0)
    lane = lax.broadcasted_iota(jnp.int32, (PANEL, RANK), 1)

    def step(number, carry):
        start = pl.multiple_of(number * PANEL, PANEL)
        panel = work[pl.ds(start, PANEL), :]
        block = pltpu.roll(panel[:, :RANK], RANK - start, axis=1)[:, :128]
        columns = [jnp.broadcast_to(block[:, j : j + 1], (PANEL, 128)) for j in range(PANEL)]
        parts = [panel[:, 128 * i : 128 * (i + 1)] for i in range(4)]
        scale = jnp.zeros((PANEL, 128), jnp.float32)
        for j in range(PANEL):
            pivot = columns[j][j : j + 1, :]
            scale = jnp.where(sub == j, lax.rsqrt(pivot), scale)
            if j == PANEL - 1:
                break
            mult = jnp.where(sub > j, columns[j] * (1.0 / pivot), 0.0)
            for other in range(j + 1, PANEL):
                columns[other] = columns[other] - mult * columns[other][j : j + 1, :]
            parts = [part - mult * part[j : j + 1, :] for part in parts]
        done = jnp.concatenate([part * scale for part in parts], axis=1)
        out_ref[pl.ds(start, PANEL), :] = done[:, RANK:]
        left = jnp.where(lane >= start + PANEL, done[:, :RANK], 0.0)
        left_high, left_mid, left_low = split3(left)
        high, mid, low = split3(done)
        lhs = jnp.concatenate([left_high, left_high, left_mid, left_high, left_low, left_mid], axis=0)
        rhs = jnp.concatenate([high, mid, high, low, high, mid], axis=0)
        work[...] -= lax.dot_general(
            lhs, rhs, (((0,), (0,)), ((), ())), preferred_element_type=jnp.float32
        )
        return carry

    lax.fori_loop(0, RANK // PANEL, step, 0)
    packed[:64, :128] = out_ref[:64, :128]
    packed[:64, 128:] = out_ref[64:128, :128]
    packed[64:, :] = out_ref[128:, :]
    mine[...] = packed[aligned(96 * place[3], 8, 96), :]


def shift_along(values, axis, step):
    size = SIZES[axis]
    return lax.ppermute(values, axis, [((i + step) % size, i) for i in range(size)])


def from_three(values, axis, step):
    return [shift_along(values[index - 1], axis, index * step) for index in FOUR[1:]]


def neighbours(near, far):
    pairs = [(i, i ^ 1) for i in range(8)]
    others = [(i, (i + 1) % 8 if i % 2 else (i + 7) % 8) for i in range(8)]
    return lax.ppermute(near, "z", pairs), lax.ppermute(far, "z", others)


def cost(micros):
    return pl.CostEstimate(flops=int(1.1e9 * micros), bytes_accessed=0, transcendentals=0)


def call(body, outs, operands, name, scratch=(), micros=1):
    memory = pl.BlockSpec(memory_space=pltpu.VMEM)
    return pl.pallas_call(
        body,
        out_shape=[jax.ShapeDtypeStruct(shape, jnp.float32) for shape in outs],
        in_specs=[pl.BlockSpec(memory_space=pltpu.SMEM)] + [memory] * (len(operands) - 1),
        out_specs=[memory] * len(outs),
        scratch_shapes=[pltpu.VMEM(shape, jnp.float32) for shape in scratch],
        cost_estimate=cost(micros),
        compiler_params=pltpu.CompilerParams(vmem_limit_bytes=48 * 1024 * 1024),
        name=name,
    )(*operands)


def aligned(start, multiple, size=None):
    return pl.ds(pl.multiple_of(start, multiple), size or multiple)


def product_kernel(count, place, *refs):
    order = (1, 2, 0, 3)
    send, keep = refs[3 * count : 3 * count + 2]
    held, arrived = refs[3 * count + 2 : -1], refs[-1]
    copies = [
        pltpu.make_async_copy(refs[index], held[index], arrived.at[index])
        for index in range(3 * count)
    ]
    for number in order:
        for index in (2 * count + number, number, count + number):
            copies[index].start()
    first = place[3] == 0
    for number in order:
        for index in (2 * count + number, number, count + number):
            copies[index].wait()
        buffer = held[number][...] + held[count + number][...].astype(jnp.float32)
        product = dot(buffer, held[2 * count + number][...], ((1,), (0,)))
        keep[number] = jnp.where(first, product[:128], product[128:])
        send[number] = jnp.where(first, product[128:], product[:128])


def product_call(place, arguments):
    memory = pl.BlockSpec(memory_space=pltpu.VMEM)
    count = len(arguments) // 3
    return pl.pallas_call(
        functools.partial(product_kernel, count),
        out_shape=[jax.ShapeDtypeStruct((count, 128, RANK), jnp.float32)] * 2,
        in_specs=[pl.BlockSpec(memory_space=pltpu.SMEM)]
        + [pl.BlockSpec(memory_space=pl.ANY)] * (3 * count),
        out_specs=[memory] * 2,
        scratch_shapes=[pltpu.VMEM(value.shape, value.dtype) for value in arguments]
        + [pltpu.SemaphoreType.DMA((3 * count,))],
        cost_estimate=cost(7),
        compiler_params=pltpu.CompilerParams(vmem_limit_bytes=60 * 1024 * 1024),
        name="products",
    )(place, *arguments)


def pair_kernel(place, keep, received, *outs):
    for step in range(4):
        number = lax.rem(place[2] + step, 4)
        outs[step][...] = keep[number] + received[number]


def cross_kernel(query, place, *refs):
    count = 1 if query else 3
    momenta, gradients, refs = refs[:count], refs[count : 2 * count], refs[2 * count :]
    core = place[3]
    if query:
        same, other, products, refs = refs[:4], refs[4:8], refs[13], refs[8:13] + refs[14:]
        for index, step in enumerate(FOUR):
            number = lax.rem(place[2] + step, 4)
            products[number, aligned(128 * core, 128), :] = same[index][...]
            products[number, aligned(128 * (1 - core), 128), :] = other[index][...]
    else:
        products, refs = refs[0], refs[1:]
    (own, plus_first, minus_first, plus_second, minus_second, wide), refs = refs[:6], refs[6:]
    if query:
        buffer = momenta[0][...] + gradients[0][...].astype(jnp.float32)
        wide[...] = dot(buffer, products[0], ((0,), (0,)))
    else:
        narrow, gram = refs
        for number in range(3):
            buffer = momenta[number][...] + gradients[number][...].astype(jnp.float32)
            crossed = dot(buffer, products[1 + number], ((0,), (0,)))
            if number == 2:
                wide[...] = crossed
            else:
                narrow[number] = crossed
        left = products[place[2], :, aligned(128 * core, 128)]
        gram[...] = dot(left, products[place[2]], ((0,), (0,)))

    def put(out, start, step, upper):
        row = lax.rem(place[1] + step, 4)
        for deep in range(4 * upper, 4 * upper + 4):
            out[start : start + 32, :] = wide[aligned(256 * row + 32 * deep, 32), :]
            start = start + 32
            if not query:
                out[start : start + 8, :] = narrow[upper, aligned(32 * row + 8 * (deep % 4), 8), :]
                start = start + 8
        if not query:
            out[start : start + 16, :] = gram[aligned(32 * row + 16 * upper, 16), :]

    half = own.shape[0] // 2
    put(plus_first, 0, 2, 0)
    put(minus_first, 0, 2, 1)
    put(plus_first, half, 1, 1)
    put(minus_first, half, 3, 0)
    put(plus_second, 0, 1, 0)
    put(minus_second, 0, 3, 1)
    put(own, 0, 0, 0)
    put(own, half, 0, 1)


def pass_kernel(place, plus, minus, plus_in, minus_in, plus_out, minus_out):
    half = plus.shape[0]
    plus_out[...] = plus[...] + plus_in[:half, :]
    minus_out[...] = minus[...] + minus_in[:half, :]


def cross_call(query, place, operands):
    half = 128 if query else 176
    outs = [(2 * half, RANK)] * 3 + [(half, RANK)] * 2
    scratch = [(1024, RANK)]
    if query:
        outs = outs + [(4, RANK, RANK)]
    else:
        scratch = scratch + [(2, 128, RANK), (128, RANK)]
    return call(
        functools.partial(cross_kernel, query),
        outs,
        (place, *operands),
        "crosses",
        scratch,
        2 if query else 3,
    )


def pass_call(place, plus, minus, plus_in, minus_in):
    return call(
        pass_kernel, [plus.shape] * 2, (place, plus, minus, plus_in, minus_in), "passes"
    )


def row_kernel(place, *refs):
    (keep, near, far), total = refs[10:13], refs[13]
    for pieces, size, start in ((refs[:5], 32, 0), (refs[5:10], 40, 32)):
        own, plus_in, minus_in, plus, minus = pieces
        half = own.shape[0] // 2
        lower = own[:half, :] + minus_in[half:, :] + plus[...]
        upper = own[half:, :] + plus_in[half:, :] + minus[...]
        for deep in range(8):
            piece = (lower, upper)[deep // 4][size * (deep % 4) : size * (deep % 4) + size, :]
            total[72 * deep + start : 72 * deep + start + size, :] = piece
    total[576:592, :] = lower[160:, :]
    total[592:, :] = upper[160:, :]
    parity = lax.rem(place[0], 2)
    for block in range(4):
        rows = slice(72 * block, 72 * block + 72)
        keep[rows, :] = total[tall_rows(2 * block + parity), :]
        out = (near, far)[block // 2]
        rows = slice(72 * (block % 2), 72 * (block % 2) + 72)
        out[rows, :] = total[tall_rows(2 * block + 1 - parity), :]
    keep[288:, :] = total[576:, :]
    near[144:, :] = total[576:592, :]
    far[144:, :] = total[592:, :]


def tall_rows(block):
    return pl.ds(pl.multiple_of(72 * block, 8), 72)


def neighbour_kernel(place, keep, near, far, *refs):
    outs, total = refs[:4], refs[4]
    total[:144, :] = keep[:144, :] + near[:144, :]
    total[144:288, :] = keep[144:288, :] + far[:144, :]
    total[288:304, :] = keep[288:304, :] + near[144:, :]
    total[304:, :] = keep[304:, :] + far[144:, :]
    for step in range(4):
        block = lax.rem(place[0] // 2 + step, 4)
        outs[step][:72, :] = total[tall_rows(block), :]
        outs[step][72:, :] = total[288:, :]


def deep_kernel(place, *refs):
    pieces, shard, gram, terms = refs[:4], refs[4], refs[5], refs[6]
    shard[...] = (
        pieces[0][:72, :] + pieces[1][:72, :] + pieces[2][:72, :] + pieces[3][:72, :]
    )
    for index, step in enumerate(FOUR):
        source = lax.rem(place[0] + 8 - 2 * step, 8)
        terms[source // 2, :16, :] = pieces[index][72:88, :]
        terms[lax.rem((source + 1) // 2, 4), 16:, :] = pieces[index][88:, :]
    gram[...] = terms[0] + terms[1] + terms[2] + terms[3]


def quad_kernel(place, *refs):
    pieces, near, far, total = refs[:4], refs[4], refs[5], refs[6]
    for index, step in enumerate(FOUR):
        total[tall_rows(lax.rem(place[0] // 2 + step, 4)), :] = pieces[index][...]
    near[...] = total[:144, :]
    far[...] = total[144:, :]


def join_kernel(place, *refs):
    same, other, total = refs[:2], refs[2:4], refs[4]
    parity = lax.rem(place[0], 2)
    for block in range(4):
        rows = slice(72 * (block % 2), 72 * (block % 2) + 72)
        total[tall_rows(2 * block + parity), :] = same[block // 2][rows, :]
        total[tall_rows(2 * block + 1 - parity), :] = other[block // 2][rows, :]


def forward_kernel(place, before, after, lower, upper):
    lower[...] = before[:288, :]
    upper[...] = after[288:, :]


def ortho_kernel(place, *refs):
    packed, same, other = refs[0], refs[1:4], refs[4:7]
    products, orthos, inverses, joined = refs[7:]
    core = place[3]
    joined[0] = packed[...]
    for index, step in enumerate(FOUR[1:]):
        joined[step, aligned(96 * core, 8, 96), :] = same[index][...]
        joined[step, aligned(96 * (1 - core), 8, 96), :] = other[index][...]
    zero = jnp.zeros((128, 128), jnp.float32)
    for step in range(4):
        number = lax.rem(place[2] + step, 4)
        inverses[number, :64, :128] = joined[step, :64, :128]
        inverses[number, 64:128, :128] = joined[step, :64, 128:]
        inverses[number, :128, 128:] = zero
        inverses[number, 128:, :] = joined[step, 64:, :]
    for number in range(4):
        orthos[number] = dot(products[number], inverses[number], ((1,), (1,)))


def column_kernel(place, *refs):
    inverses, pieces = refs[0], refs[1:6]
    columns, squares, wide, narrow = refs[6:10], refs[10], refs[11], refs[12]
    for step in range(4):
        row = lax.rem(place[1] + step, 4)
        for deep in range(8):
            piece = pieces[(0, 1, 2 + deep // 4, 4)[step]]
            start = 72 * (deep % 4 if step == 2 else deep)
            rows = aligned(256 * row + 32 * deep, 32)
            wide[0, rows, :] = piece[start : start + 32, :]
            wide[1, rows, :] = piece[start + 32 : start + 64, :]
            rows = aligned(32 * row + 8 * (deep % 4), 8)
            narrow[deep // 4, rows, :] = piece[start + 64 : start + 72, :]
    for number in range(4):
        crossed = wide[number // 3] if number in (0, 3) else narrow[number - 1]
        column = dot(crossed, inverses[number], ((1,), (1,)))
        columns[number][...] = column
        squares[number : number + 1, :] = jnp.sum(column * column, axis=0, keepdims=True)


def momentum_kernel(place, *refs):
    momenta, gradients, columns, orthos, outs = refs[:4], refs[4:8], refs[8:12], refs[12], refs[13:17]
    held, sent = refs[17:21], refs[21]
    copies = [pltpu.make_async_copy(held[i], outs[i], sent.at[i]) for i in range(4)]
    for number in (0, 3, 1, 2):
        buffer = momenta[number][...] + gradients[number][...].astype(jnp.float32)
        change = dot_three(orthos[number], columns[number][...])
        held[number][...] = buffer - (1.0 - MOMENTUM_DECAY) * change
        copies[number].start()
    for copy in copies:
        copy.wait()


def update_kernel(scales, place, *refs):
    squares, columns, orthos, outs = refs[0], refs[1:5], refs[5], refs[6:14]
    held, sent = refs[14:22], refs[22]
    copies = [pltpu.make_async_copy(held[i], outs[i], sent.at[i]) for i in range(8)]
    inverse = 1.0 / jnp.sqrt(squares[...] + EPSILON)
    for number in (0, 3, 1, 2):
        basis = columns[number][...] * inverse[number : number + 1, :]
        held[4 + number][...] = basis
        copies[4 + number].start()
        held[number][...] = scales[number] * dot_three(orthos[number], basis)
        copies[number].start()
    for copy in copies:
        copy.wait()


def result_call(body, shapes, operands, name):
    return pl.pallas_call(
        body,
        out_shape=[jax.ShapeDtypeStruct(shape, jnp.float32) for shape in shapes],
        in_specs=[pl.BlockSpec(memory_space=pltpu.SMEM)]
        + [pl.BlockSpec(memory_space=pltpu.VMEM)] * (len(operands) - 1),
        out_specs=[pl.BlockSpec(memory_space=pl.ANY)] * len(shapes),
        scratch_shapes=[pltpu.VMEM(shape, jnp.float32) for shape in shapes]
        + [pltpu.SemaphoreType.DMA((len(shapes),))],
        cost_estimate=cost(3),
        compiler_params=pltpu.CompilerParams(vmem_limit_bytes=48 * 1024 * 1024),
        name=name,
    )(*operands)


def local(*arguments):
    momenta = arguments[0::3]
    gradients = arguments[1::3]
    factors = arguments[2::3]
    height = momenta[0].shape[0]
    place = jnp.stack([lax.axis_index(axis) for axis in SIZES]).astype(jnp.int32)

    half = (128, RANK)
    send, keep = product_call(place, (*momenta, *gradients, *factors))
    received = shift_along(send, "core", 1)
    pieces = call(pair_kernel, [half] * 4, (place, keep, received), "pairs")
    shard = sum(reversed(from_three(pieces[1:], "x", -1)), pieces[0])
    same = [shard] + from_three([shard] * 3, "x", 1)
    other = [shift_along(piece, "core", 1) for piece in same]

    *query, products = cross_call(True, place, (momenta[0], gradients[0], *same, *other))
    others = cross_call(False, place, (*momenta[1:], *gradients[1:], products))
    query_in = shift_along(query[1], "y", -1), shift_along(query[2], "y", 1)
    others_in = shift_along(others[1], "y", -1), shift_along(others[2], "y", 1)
    plus, minus = pass_call(place, query[3], query[4], *query_in)
    others_in, plus, minus = lax.optimization_barrier((others_in, plus, minus))
    query_pieces = (query[0], *query_in, shift_along(plus, "y", -1), shift_along(minus, "y", 1))
    plus, minus = pass_call(place, others[3], others[4], *others_in)
    other_pieces = (others[0], *others_in, shift_along(plus, "y", -1), shift_along(minus, "y", 1))

    keep, near, far = call(
        row_kernel,
        [(320, RANK), (160, RANK), (160, RANK)],
        (place, *query_pieces, *other_pieces),
        "rows",
        [(608, RANK)],
    )
    near, far = neighbours(near, far)
    pieces = call(
        neighbour_kernel, [(104, RANK)] * 4, (place, keep, near, far), "neighbours", [(320, RANK)]
    )
    pieces = [pieces[0]] + from_three(pieces[1:], "z", -2)
    shard, gram = call(
        deep_kernel, [(72, RANK), (32, RANK)], (place, *pieces), "deeps", [(4, 32, RANK)]
    )

    beside = shift_along(gram, "core", 1)
    first = place[3] == 0
    pair = jnp.concatenate([jnp.where(first, gram, beside), jnp.where(first, beside, gram)], axis=0)
    rows = [pair] + from_three([pair] * 3, "y", 1)

    pieces = [shard] + from_three([shard] * 3, "z", 2)
    near, far = call(quad_kernel, [(144, RANK)] * 2, (place, *pieces), "quads", [(288, RANK)])
    (joined,) = call(
        join_kernel, [(576, RANK)], (place, near, far, *neighbours(near, far)), "joins"
    )
    before = shift_along(joined, "y", -1)
    after = shift_along(joined, "y", 1)
    lower, upper = call(forward_kernel, [(288, RANK)] * 2, (place, before, after), "forwards")

    packed, mine = call(
        inverse_kernel,
        [(192, RANK), (96, RANK)],
        (place, *rows),
        "inverse",
        [(RANK, RANK), (RANK, RANK), (RANK, 2 * RANK)],
        11,
    )
    mine, lower, upper = lax.optimization_barrier((mine, lower, upper))
    lower = shift_along(lower, "y", -1)
    upper = shift_along(upper, "y", 1)
    same = from_three([mine] * 3, "x", 1)
    same, lower, upper = lax.optimization_barrier((same, lower, upper))
    other = [shift_along(piece, "core", 1) for piece in same]
    orthos, inverses = call(
        ortho_kernel,
        [(4, RANK, RANK)] * 2,
        (place, packed, *same, *other, products),
        "orthos",
        [(4, 192, RANK)],
        2,
    )

    tall = [(momentum.shape[1], RANK) for momentum in momenta]
    flat = [momentum.shape for momentum in momenta]
    *columns, squares = call(
        column_kernel,
        tall + [(4, RANK)],
        (place, inverses, joined, after, lower, upper, before),
        "columns",
        [(2, 1024, RANK), (2, 128, RANK)],
        3,
    )
    squares = squares + shift_along(squares, "core", 1)
    squares = squares + sum(reversed(from_three([squares] * 3, "x", 1)))
    new_momenta = result_call(
        momentum_kernel, flat, (place, *momenta, *gradients, *columns, orthos), "momenta"
    )
    scales = [math.sqrt(height * 32 * shape[1] * 8 / RANK) for shape in flat]
    outs = result_call(
        functools.partial(update_kernel, scales),
        flat + tall,
        (place, squares, *columns, orthos),
        "updates",
    )
    results = []
    for number in range(4):
        results = results + [outs[number], new_momenta[number], outs[4 + number]]
    return tuple(results)


def solution(mesh):
    devices = mesh.devices.reshape(tuple(SIZES.values()))
    finer = Mesh(devices, tuple(SIZES))
    wide = P(("z", "y"), ("x", "core"))
    tall = P(("x", "core"), None)
    return jax.shard_map(
        local,
        mesh=finer,
        in_specs=(wide, wide, tall) * 4,
        out_specs=(wide, wide, tall) * 4,
        check_vma=False,
    )
```

```python
import functools
import math

import jax
import jax.numpy as jnp
from jax import lax
from jax.experimental import pallas as pl
from jax.experimental.pallas import tpu as pltpu
from jax.sharding import Mesh
from jax.sharding import PartitionSpec as P

PRECISE = lax.Precision.HIGHEST
MOMENTUM_DECAY = 0.95
SHIFT_RATIO = 0.0001
EPSILON = 1e-06
RANK = 256
PANEL = 16
FOUR = (0, 2, 1, 3)
SIZES = {"z": 8, "y": 4, "x": 4, "core": 2}


def dot(left, right, dims):
    return lax.dot_general(
        left, right, (dims, ((), ())), precision=PRECISE, preferred_element_type=jnp.float32
    )


def dot_three(left, right, dims=((1,), (1,))):
    parts = []
    for values in (left, right):
        high = values.astype(jnp.bfloat16)
        parts.append((high, (values - high.astype(jnp.float32)).astype(jnp.bfloat16)))
    (left_high, left_low), (right_high, right_low) = parts

    def one(first, second):
        return lax.dot_general(
            first, second, (dims, ((), ())), preferred_element_type=jnp.float32
        )

    return one(left_low, right_high) + one(left_high, right_low) + one(left_high, right_high)


def split3(values):
    high = values.astype(jnp.bfloat16)
    rest = values - high.astype(jnp.float32)
    mid = rest.astype(jnp.bfloat16)
    low = (rest - mid.astype(jnp.float32)).astype(jnp.bfloat16)
    return high, mid, low


def inverse_kernel(place, *refs):
    pieces, (packed, mine, gram_ref, out_ref, work) = refs[:4], refs[4:]
    for step, piece in zip(FOUR, pieces):
        rows = 32 * lax.rem(place[1] + step, 4)
        gram_ref[pl.ds(pl.multiple_of(rows, 32), 32), :] = piece[:32, :]
        gram_ref[pl.ds(pl.multiple_of(rows + 128, 32), 32), :] = piece[32:, :]
    gram = gram_ref[...]
    rows = lax.broadcasted_iota(jnp.int32, (RANK, RANK), 0)
    cols = lax.broadcasted_iota(jnp.int32, (RANK, RANK), 1)
    unit = jnp.where(rows == cols, 1.0, 0.0).astype(jnp.float32)
    shift = SHIFT_RATIO * jnp.sum(gram * unit) / RANK
    work[:, :RANK] = gram + shift * unit
    work[:, RANK:] = unit
    sub = lax.broadcasted_iota(jnp.int32, (PANEL, 128), 0)
    for start in range(0, RANK, PANEL):
        here, end = start // 128, start + PANEL
        blocks = list(range(here, 3 + here))
        panel = {i: work[start:end, 128 * i : 128 * (i + 1)] for i in blocks}
        columns = [
            jnp.broadcast_to(panel[here][:, j : j + 1], (PANEL, 128))
            for j in range(start % 128, start % 128 + PANEL)
        ]
        scale = jnp.zeros((PANEL, 128), jnp.float32)
        for j in range(PANEL):
            root = lax.rsqrt(columns[j][j : j + 1, :])
            scale = jnp.where(sub == j, root, scale)
            mult = jnp.where(sub > j, columns[j] * (root * root), 0.0)
            for other in range(j + 1, PANEL):
                columns[other] = columns[other] - mult * columns[other][j : j + 1, :]
            if j < PANEL - 1:
                panel = {i: panel[i] - mult * panel[i][j : j + 1, :] for i in blocks}
        panel = {i: panel[i] * scale for i in blocks}
        for i in range(2, 4):
            out_ref[start:end, 128 * (i - 2) : 128 * (i - 1)] = panel.get(i, jnp.zeros_like(scale))
        first = end // 128
        if first == 2:
            break
        changed = [i for i in blocks if i >= first]
        left = jnp.concatenate([panel[i] for i in changed if i < 2], axis=1)
        lane = lax.broadcasted_iota(jnp.int32, left.shape, 1) + 128 * first
        left_high, left_mid, left_low = split3(jnp.where(lane >= end, left, 0.0))
        high, mid, low = split3(jnp.concatenate([panel[i] for i in changed], axis=1))
        lhs = jnp.concatenate([left_high, left_high, left_mid, left_high, left_low, left_mid], axis=0)
        rhs = jnp.concatenate([high, mid, high, low, high, mid], axis=0)
        change = lax.dot_general(
            lhs, rhs, (((0,), (0,)), ((), ())), preferred_element_type=jnp.float32
        )
        for place_in, i in enumerate(changed):
            work[end:, 128 * i : 128 * (i + 1)] -= change[
                end - 128 * first :, 128 * place_in : 128 * (place_in + 1)
            ]

    packed[:64, :128] = out_ref[:64, :128]
    packed[:64, 128:] = out_ref[64:128, :128]
    packed[64:, :] = out_ref[128:, :]
    mine[...] = packed[aligned(96 * place[3], 8, 96), :]


def shift_along(values, axis, step):
    size = SIZES[axis]
    return lax.ppermute(values, axis, [((i + step) % size, i) for i in range(size)])


def from_three(values, axis, step):
    return [shift_along(values[index - 1], axis, index * step) for index in FOUR[1:]]


def neighbours(near, far):
    pairs = [(i, i ^ 1) for i in range(8)]
    others = [(i, (i + 1) % 8 if i % 2 else (i + 7) % 8) for i in range(8)]
    return lax.ppermute(near, "z", pairs), lax.ppermute(far, "z", others)


def cost(micros):
    return pl.CostEstimate(flops=int(1.1e9 * micros), bytes_accessed=0, transcendentals=0)


def call(body, outs, operands, name, scratch=(), micros=1):
    memory = pl.BlockSpec(memory_space=pltpu.VMEM)
    return pl.pallas_call(
        body,
        out_shape=[jax.ShapeDtypeStruct(shape, jnp.float32) for shape in outs],
        in_specs=[pl.BlockSpec(memory_space=pltpu.SMEM)] + [memory] * (len(operands) - 1),
        out_specs=[memory] * len(outs),
        scratch_shapes=[pltpu.VMEM(shape, jnp.float32) for shape in scratch],
        cost_estimate=cost(micros),
        compiler_params=pltpu.CompilerParams(vmem_limit_bytes=48 * 1024 * 1024),
        name=name,
    )(*operands)


def aligned(start, multiple, size=None):
    return pl.ds(pl.multiple_of(start, multiple), size or multiple)


def product_kernel(count, place, *refs):
    order = (1, 2, 0, 3)
    send, keep = refs[3 * count : 3 * count + 2]
    held, arrived = refs[3 * count + 2 : -1], refs[-1]
    copies = [
        pltpu.make_async_copy(refs[index], held[index], arrived.at[index])
        for index in range(3 * count)
    ]
    for number in order:
        for index in (2 * count + number, number, count + number):
            copies[index].start()
    first = place[3] == 0
    for number in order:
        for index in (2 * count + number, number, count + number):
            copies[index].wait()
        buffer = held[number][...] + held[count + number][...].astype(jnp.float32)
        product = dot(buffer, held[2 * count + number][...], ((1,), (0,)))
        keep[number] = jnp.where(first, product[:128], product[128:])
        send[number] = jnp.where(first, product[128:], product[:128])


def product_call(place, arguments):
    memory = pl.BlockSpec(memory_space=pltpu.VMEM)
    count = len(arguments) // 3
    return pl.pallas_call(
        functools.partial(product_kernel, count),
        out_shape=[jax.ShapeDtypeStruct((count, 128, RANK), jnp.float32)] * 2,
        in_specs=[pl.BlockSpec(memory_space=pltpu.SMEM)]
        + [pl.BlockSpec(memory_space=pl.ANY)] * (3 * count),
        out_specs=[memory] * 2,
        scratch_shapes=[pltpu.VMEM(value.shape, value.dtype) for value in arguments]
        + [pltpu.SemaphoreType.DMA((3 * count,))],
        cost_estimate=cost(7),
        compiler_params=pltpu.CompilerParams(vmem_limit_bytes=60 * 1024 * 1024),
        name="products",
    )(place, *arguments)


def pair_kernel(place, keep, received, *outs):
    for step in range(4):
        number = lax.rem(place[2] + step, 4)
        outs[step][...] = keep[number] + received[number]


def cross_kernel(query, place, *refs):
    count = 1 if query else 3
    momenta, gradients, refs = refs[:count], refs[count : 2 * count], refs[2 * count :]
    core = place[3]
    if query:
        same, other, products, refs = refs[:4], refs[4:8], refs[13], refs[8:13] + refs[14:]
        for index, step in enumerate(FOUR):
            number = lax.rem(place[2] + step, 4)
            products[number, aligned(128 * core, 128), :] = same[index][...]
            products[number, aligned(128 * (1 - core), 128), :] = other[index][...]
    else:
        products, refs = refs[0], refs[1:]
    (own, plus_first, minus_first, plus_second, minus_second, wide), refs = refs[:6], refs[6:]
    if query:
        buffer = momenta[0][...] + gradients[0][...].astype(jnp.float32)
        wide[...] = dot_three(buffer, products[0], ((0,), (0,)))
    else:
        narrow, gram = refs
        for number in range(3):
            buffer = momenta[number][...] + gradients[number][...].astype(jnp.float32)
            crossed = dot_three(buffer, products[1 + number], ((0,), (0,)))
            if number == 2:
                wide[...] = crossed
            else:
                narrow[number] = crossed
        left = products[place[2], :, aligned(128 * core, 128)]
        gram[...] = dot(left, products[place[2]], ((0,), (0,)))

    def put(out, start, step, upper):
        row = lax.rem(place[1] + step, 4)
        for deep in range(4 * upper, 4 * upper + 4):
            out[start : start + 32, :] = wide[aligned(256 * row + 32 * deep, 32), :]
            start = start + 32
            if not query:
                out[start : start + 8, :] = narrow[upper, aligned(32 * row + 8 * (deep % 4), 8), :]
                start = start + 8
        if not query:
            out[start : start + 16, :] = gram[aligned(32 * row + 16 * upper, 16), :]

    half = own.shape[0] // 2
    put(plus_first, 0, 2, 0)
    put(minus_first, 0, 2, 1)
    put(plus_first, half, 1, 1)
    put(minus_first, half, 3, 0)
    put(plus_second, 0, 1, 0)
    put(minus_second, 0, 3, 1)
    put(own, 0, 0, 0)
    put(own, half, 0, 1)


def pass_kernel(place, plus, minus, plus_in, minus_in, plus_out, minus_out):
    half = plus.shape[0]
    plus_out[...] = plus[...] + plus_in[:half, :]
    minus_out[...] = minus[...] + minus_in[:half, :]


def cross_call(query, place, operands):
    half = 128 if query else 176
    outs = [(2 * half, RANK)] * 3 + [(half, RANK)] * 2
    scratch = [(1024, RANK)]
    if query:
        outs = outs + [(4, RANK, RANK)]
    else:
        scratch = scratch + [(2, 128, RANK), (128, RANK)]
    return call(
        functools.partial(cross_kernel, query),
        outs,
        (place, *operands),
        "crosses",
        scratch,
        2 if query else 3,
    )


def pass_call(place, plus, minus, plus_in, minus_in):
    return call(
        pass_kernel, [plus.shape] * 2, (place, plus, minus, plus_in, minus_in), "passes"
    )


def row_kernel(place, *refs):
    (keep, near, far), total = refs[10:13], refs[13]
    for pieces, size, start in ((refs[:5], 32, 0), (refs[5:10], 40, 32)):
        own, plus_in, minus_in, plus, minus = pieces
        half = own.shape[0] // 2
        lower = own[:half, :] + minus_in[half:, :] + plus[...]
        upper = own[half:, :] + plus_in[half:, :] + minus[...]
        for deep in range(8):
            piece = (lower, upper)[deep // 4][size * (deep % 4) : size * (deep % 4) + size, :]
            total[72 * deep + start : 72 * deep + start + size, :] = piece
    total[576:592, :] = lower[160:, :]
    total[592:, :] = upper[160:, :]
    parity = lax.rem(place[0], 2)
    for block in range(4):
        rows = slice(72 * block, 72 * block + 72)
        keep[rows, :] = total[tall_rows(2 * block + parity), :]
        out = (near, far)[block // 2]
        rows = slice(72 * (block % 2), 72 * (block % 2) + 72)
        out[rows, :] = total[tall_rows(2 * block + 1 - parity), :]
    keep[288:, :] = total[576:, :]
    near[144:, :] = total[576:592, :]
    far[144:, :] = total[592:, :]


def tall_rows(block):
    return pl.ds(pl.multiple_of(72 * block, 8), 72)


def neighbour_kernel(place, keep, near, far, *refs):
    outs, total = refs[:4], refs[4]
    total[:144, :] = keep[:144, :] + near[:144, :]
    total[144:288, :] = keep[144:288, :] + far[:144, :]
    total[288:304, :] = keep[288:304, :] + near[144:, :]
    total[304:, :] = keep[304:, :] + far[144:, :]
    for step in range(4):
        block = lax.rem(place[0] // 2 + step, 4)
        outs[step][:72, :] = total[tall_rows(block), :]
        outs[step][72:, :] = total[288:, :]


def deep_kernel(place, *refs):
    pieces, shard, gram, terms = refs[:4], refs[4], refs[5], refs[6]
    shard[...] = (
        pieces[0][:72, :] + pieces[1][:72, :] + pieces[2][:72, :] + pieces[3][:72, :]
    )
    for index, step in enumerate(FOUR):
        source = lax.rem(place[0] + 8 - 2 * step, 8)
        terms[source // 2, :16, :] = pieces[index][72:88, :]
        terms[lax.rem((source + 1) // 2, 4), 16:, :] = pieces[index][88:, :]
    gram[...] = terms[0] + terms[1] + terms[2] + terms[3]


def quad_kernel(place, *refs):
    pieces, near, far, total = refs[:4], refs[4], refs[5], refs[6]
    for index, step in enumerate(FOUR):
        total[tall_rows(lax.rem(place[0] // 2 + step, 4)), :] = pieces[index][...]
    near[...] = total[:144, :]
    far[...] = total[144:, :]


def join_kernel(place, *refs):
    same, other, total = refs[:2], refs[2:4], refs[4]
    parity = lax.rem(place[0], 2)
    for block in range(4):
        rows = slice(72 * (block % 2), 72 * (block % 2) + 72)
        total[tall_rows(2 * block + parity), :] = same[block // 2][rows, :]
        total[tall_rows(2 * block + 1 - parity), :] = other[block // 2][rows, :]


def forward_kernel(place, before, after, lower, upper):
    lower[...] = before[:288, :]
    upper[...] = after[288:, :]


def ortho_kernel(place, inverses, products, orthos):
    for number in range(4):
        orthos[number] = dot(products[number], inverses[number], ((1,), (1,)))


def column_kernel(place, *refs):
    packed, same, other = refs[0], refs[1:4], refs[4:7]
    pieces, columns, squares, inverses = refs[7:12], refs[12:16], refs[16], refs[17]
    wide, narrow, joined = refs[18:]
    core = place[3]
    joined[0] = packed[...]
    for index, step in enumerate(FOUR[1:]):
        joined[step, aligned(96 * core, 8, 96), :] = same[index][...]
        joined[step, aligned(96 * (1 - core), 8, 96), :] = other[index][...]
    zero = jnp.zeros((128, 128), jnp.float32)
    for step in range(4):
        number = lax.rem(place[2] + step, 4)
        inverses[number, :64, :128] = joined[step, :64, :128]
        inverses[number, 64:128, :128] = joined[step, :64, 128:]
        inverses[number, :128, 128:] = zero
        inverses[number, 128:, :] = joined[step, 64:, :]
    for step in range(4):
        row = lax.rem(place[1] + step, 4)
        for deep in range(8):
            piece = pieces[(0, 1, 2 + deep // 4, 4)[step]]
            start = 72 * (deep % 4 if step == 2 else deep)
            rows = aligned(256 * row + 32 * deep, 32)
            wide[0, rows, :] = piece[start : start + 32, :]
            wide[1, rows, :] = piece[start + 32 : start + 64, :]
            rows = aligned(32 * row + 8 * (deep % 4), 8)
            narrow[deep // 4, rows, :] = piece[start + 64 : start + 72, :]
    for number in range(4):
        crossed = wide[number // 3] if number in (0, 3) else narrow[number - 1]
        column = dot_three(crossed, inverses[number])
        columns[number][...] = column
        squares[number : number + 1, :] = jnp.sum(column * column, axis=0, keepdims=True)


def momentum_kernel(place, *refs):
    momenta, gradients, columns, orthos, outs = refs[:4], refs[4:8], refs[8:12], refs[12], refs[13:17]
    held, sent = refs[17:21], refs[21]
    copies = [pltpu.make_async_copy(held[i], outs[i], sent.at[i]) for i in range(4)]
    for number in (0, 3, 1, 2):
        buffer = momenta[number][...] + gradients[number][...].astype(jnp.float32)
        change = dot_three(orthos[number], columns[number][...])
        held[number][...] = buffer - (1.0 - MOMENTUM_DECAY) * change
        copies[number].start()
    for copy in copies:
        copy.wait()


def update_kernel(scales, place, *refs):
    squares, columns, orthos, outs = refs[0], refs[1:5], refs[5], refs[6:14]
    held, sent = refs[14:22], refs[22]
    copies = [pltpu.make_async_copy(held[i], outs[i], sent.at[i]) for i in range(8)]
    inverse = 1.0 / jnp.sqrt(squares[...] + EPSILON)
    for number in (0, 3, 1, 2):
        basis = columns[number][...] * inverse[number : number + 1, :]
        held[4 + number][...] = basis
        copies[4 + number].start()
        held[number][...] = scales[number] * dot_three(orthos[number], basis)
        copies[number].start()
    for copy in copies:
        copy.wait()


def result_call(body, shapes, operands, name):
    return pl.pallas_call(
        body,
        out_shape=[jax.ShapeDtypeStruct(shape, jnp.float32) for shape in shapes],
        in_specs=[pl.BlockSpec(memory_space=pltpu.SMEM)]
        + [pl.BlockSpec(memory_space=pltpu.VMEM)] * (len(operands) - 1),
        out_specs=[pl.BlockSpec(memory_space=pl.ANY)] * len(shapes),
        scratch_shapes=[pltpu.VMEM(shape, jnp.float32) for shape in shapes]
        + [pltpu.SemaphoreType.DMA((len(shapes),))],
        cost_estimate=cost(3),
        compiler_params=pltpu.CompilerParams(vmem_limit_bytes=48 * 1024 * 1024),
        name=name,
    )(*operands)


def local(*arguments):
    momenta = arguments[0::3]
    gradients = arguments[1::3]
    factors = arguments[2::3]
    height = momenta[0].shape[0]
    place = jnp.stack([lax.axis_index(axis) for axis in SIZES]).astype(jnp.int32)

    half = (128, RANK)
    send, keep = product_call(place, (*momenta, *gradients, *factors))
    received = shift_along(send, "core", 1)
    pieces = call(pair_kernel, [half] * 4, (place, keep, received), "pairs")
    shard = sum(reversed(from_three(pieces[1:], "x", -1)), pieces[0])
    same = [shard] + from_three([shard] * 3, "x", 1)
    other = [shift_along(piece, "core", 1) for piece in same]

    *query, products = cross_call(True, place, (momenta[0], gradients[0], *same, *other))
    others = cross_call(False, place, (*momenta[1:], *gradients[1:], products))
    query_in = shift_along(query[1], "y", -1), shift_along(query[2], "y", 1)
    others_in = shift_along(others[1], "y", -1), shift_along(others[2], "y", 1)
    plus, minus = pass_call(place, query[3], query[4], *query_in)
    others_in, plus, minus = lax.optimization_barrier((others_in, plus, minus))
    query_pieces = (query[0], *query_in, shift_along(plus, "y", -1), shift_along(minus, "y", 1))
    plus, minus = pass_call(place, others[3], others[4], *others_in)
    other_pieces = (others[0], *others_in, shift_along(plus, "y", -1), shift_along(minus, "y", 1))

    keep, near, far = call(
        row_kernel,
        [(320, RANK), (160, RANK), (160, RANK)],
        (place, *query_pieces, *other_pieces),
        "rows",
        [(608, RANK)],
    )
    near, far = neighbours(near, far)
    pieces = call(
        neighbour_kernel, [(104, RANK)] * 4, (place, keep, near, far), "neighbours", [(320, RANK)]
    )
    pieces = [pieces[0]] + from_three(pieces[1:], "z", -2)
    shard, gram = call(
        deep_kernel, [(72, RANK), (32, RANK)], (place, *pieces), "deeps", [(4, 32, RANK)]
    )

    beside = shift_along(gram, "core", 1)
    first = place[3] == 0
    pair = jnp.concatenate([jnp.where(first, gram, beside), jnp.where(first, beside, gram)], axis=0)
    rows = [pair] + from_three([pair] * 3, "y", 1)

    pieces = [shard] + from_three([shard] * 3, "z", 2)
    near, far = call(quad_kernel, [(144, RANK)] * 2, (place, *pieces), "quads", [(288, RANK)])
    (joined,) = call(
        join_kernel, [(576, RANK)], (place, near, far, *neighbours(near, far)), "joins"
    )
    before = shift_along(joined, "y", -1)
    after = shift_along(joined, "y", 1)
    lower, upper = call(forward_kernel, [(288, RANK)] * 2, (place, before, after), "forwards")

    packed, mine = call(
        inverse_kernel,
        [(192, RANK), (96, RANK)],
        (place, *rows),
        "inverse",
        [(RANK, RANK), (RANK, RANK), (RANK, 2 * RANK)],
        11,
    )
    mine, lower, upper = lax.optimization_barrier((mine, lower, upper))
    lower = shift_along(lower, "y", -1)
    upper = shift_along(upper, "y", 1)
    same = from_three([mine] * 3, "x", 1)
    same[2], lower, upper = lax.optimization_barrier((same[2], lower, upper))
    other = [shift_along(piece, "core", 1) for piece in same]
    tall = [(momentum.shape[1], RANK) for momentum in momenta]
    flat = [momentum.shape for momentum in momenta]
    *columns, squares, inverses = call(
        column_kernel,
        tall + [(4, RANK), (4, RANK, RANK)],
        (place, packed, *same, *other, joined, after, lower, upper, before),
        "columns",
        [(2, 1024, RANK), (2, 128, RANK), (4, 192, RANK)],
        3,
    )
    (orthos,) = call(ortho_kernel, [(4, RANK, RANK)], (place, inverses, products), "orthos")
    squares = squares + shift_along(squares, "core", 1)
    squares = squares + sum(reversed(from_three([squares] * 3, "x", 1)))
    new_momenta = result_call(
        momentum_kernel, flat, (place, *momenta, *gradients, *columns, orthos), "momenta"
    )
    scales = [math.sqrt(height * 32 * shape[1] * 8 / RANK) for shape in flat]
    outs = result_call(
        functools.partial(update_kernel, scales),
        flat + tall,
        (place, squares, *columns, orthos),
        "updates",
    )
    results = []
    for number in range(4):
        results = results + [outs[number], new_momenta[number], outs[4 + number]]
    return tuple(results)


def solution(mesh):
    devices = mesh.devices.reshape(tuple(SIZES.values()))
    finer = Mesh(devices, tuple(SIZES))
    wide = P(("z", "y"), ("x", "core"))
    tall = P(("x", "core"), None)
    return jax.shard_map(
        local,
        mesh=finer,
        in_specs=(wide, wide, tall) * 4,
        out_specs=(wide, wide, tall) * 4,
        check_vma=False,
    )
```

```python
import functools
import math

import jax
import jax.numpy as jnp
from jax import lax
from jax.experimental import pallas as pl
from jax.experimental.pallas import tpu as pltpu
from jax.sharding import Mesh
from jax.sharding import PartitionSpec as P

PRECISE = lax.Precision.HIGHEST
MOMENTUM_DECAY = 0.95
SHIFT_RATIO = 0.0001
EPSILON = 1e-06
RANK = 256
PANEL = 16
FOUR = (0, 2, 1, 3)
SIZES = {"z": 8, "y": 4, "x": 4, "core": 2}


def dot(left, right, dims):
    return lax.dot_general(
        left, right, (dims, ((), ())), precision=PRECISE, preferred_element_type=jnp.float32
    )


def dot_three(left, right, dims=((1,), (1,))):
    parts = []
    for values in (left, right):
        high = values.astype(jnp.bfloat16)
        parts.append((high, (values - high.astype(jnp.float32)).astype(jnp.bfloat16)))
    (left_high, left_low), (right_high, right_low) = parts

    def one(first, second):
        return lax.dot_general(
            first, second, (dims, ((), ())), preferred_element_type=jnp.float32
        )

    return one(left_low, right_high) + one(left_high, right_low) + one(left_high, right_high)


def split3(values):
    high = values.astype(jnp.bfloat16)
    rest = values - high.astype(jnp.float32)
    mid = rest.astype(jnp.bfloat16)
    low = (rest - mid.astype(jnp.float32)).astype(jnp.bfloat16)
    return high, mid, low


def inverse_kernel(place, *refs):
    pieces, (packed, mine, gram_ref, out_ref, work) = refs[:4], refs[4:]
    for step, piece in zip(FOUR, pieces):
        rows = 32 * lax.rem(place[1] + step, 4)
        gram_ref[pl.ds(pl.multiple_of(rows, 32), 32), :] = piece[:32, :]
        gram_ref[pl.ds(pl.multiple_of(rows + 128, 32), 32), :] = piece[32:, :]
    gram = gram_ref[...]
    rows = lax.broadcasted_iota(jnp.int32, (RANK, RANK), 0)
    cols = lax.broadcasted_iota(jnp.int32, (RANK, RANK), 1)
    unit = jnp.where(rows == cols, 1.0, 0.0).astype(jnp.float32)
    shift = SHIFT_RATIO * jnp.sum(gram * unit) / RANK
    work[:, :RANK] = gram + shift * unit
    work[:, RANK:] = unit
    sub = lax.broadcasted_iota(jnp.int32, (PANEL, 128), 0)
    for start in range(0, RANK, PANEL):
        here, end = start // 128, start + PANEL
        blocks = list(range(here, 3 + here))
        panel = {i: work[start:end, 128 * i : 128 * (i + 1)] for i in blocks}
        columns = [
            jnp.broadcast_to(panel[here][:, j : j + 1], (PANEL, 128))
            for j in range(start % 128, start % 128 + PANEL)
        ]
        scale = jnp.zeros((PANEL, 128), jnp.float32)
        for j in range(PANEL):
            root = lax.rsqrt(columns[j][j : j + 1, :])
            scale = jnp.where(sub == j, root, scale)
            mult = jnp.where(sub > j, columns[j] * (root * root), 0.0)
            for other in range(j + 1, PANEL):
                columns[other] = columns[other] - mult * columns[other][j : j + 1, :]
            if j < PANEL - 1:
                panel = {i: panel[i] - mult * panel[i][j : j + 1, :] for i in blocks}
        panel = {i: panel[i] * scale for i in blocks}
        for i in range(2, 4):
            out_ref[start:end, 128 * (i - 2) : 128 * (i - 1)] = panel.get(i, jnp.zeros_like(scale))
        first = end // 128
        if first == 2:
            break
        changed = [i for i in blocks if i >= first]
        left = jnp.concatenate([panel[i] for i in changed if i < 2], axis=1)
        lane = lax.broadcasted_iota(jnp.int32, left.shape, 1) + 128 * first
        left_high, left_mid, left_low = split3(jnp.where(lane >= end, left, 0.0))
        high, mid, low = split3(jnp.concatenate([panel[i] for i in changed], axis=1))
        lhs = jnp.concatenate([left_high, left_high, left_mid, left_high, left_low, left_mid], axis=0)
        rhs = jnp.concatenate([high, mid, high, low, high, mid], axis=0)
        change = lax.dot_general(
            lhs, rhs, (((0,), (0,)), ((), ())), preferred_element_type=jnp.float32
        )
        for place_in, i in enumerate(changed):
            work[end:, 128 * i : 128 * (i + 1)] -= change[
                end - 128 * first :, 128 * place_in : 128 * (place_in + 1)
            ]

    packed[:64, :128] = out_ref[:64, :128]
    packed[:64, 128:] = out_ref[64:128, :128]
    packed[64:, :] = out_ref[128:, :]
    mine[...] = packed[aligned(96 * place[3], 8, 96), :]


def shift_along(values, axis, step):
    size = SIZES[axis]
    return lax.ppermute(values, axis, [((i + step) % size, i) for i in range(size)])


def from_three(values, axis, step):
    return [shift_along(values[index - 1], axis, index * step) for index in FOUR[1:]]


def neighbours(near, far):
    pairs = [(i, i ^ 1) for i in range(8)]
    others = [(i, (i + 1) % 8 if i % 2 else (i + 7) % 8) for i in range(8)]
    return lax.ppermute(near, "z", pairs), lax.ppermute(far, "z", others)


def cost(micros):
    return pl.CostEstimate(flops=int(1.1e9 * micros), bytes_accessed=0, transcendentals=0)


def call(body, outs, operands, name, scratch=(), micros=1):
    memory = pl.BlockSpec(memory_space=pltpu.VMEM)
    return pl.pallas_call(
        body,
        out_shape=[jax.ShapeDtypeStruct(shape, jnp.float32) for shape in outs],
        in_specs=[pl.BlockSpec(memory_space=pltpu.SMEM)] + [memory] * (len(operands) - 1),
        out_specs=[memory] * len(outs),
        scratch_shapes=[pltpu.VMEM(shape, jnp.float32) for shape in scratch],
        cost_estimate=cost(micros),
        compiler_params=pltpu.CompilerParams(vmem_limit_bytes=24 * 1024 * 1024),
        name=name,
    )(*operands)


def aligned(start, multiple, size=None):
    return pl.ds(pl.multiple_of(start, multiple), size or multiple)


def product_kernel(count, place, *refs):
    order = (1, 2, 0, 3)
    send, keep = refs[3 * count : 3 * count + 2]
    held, arrived = refs[3 * count + 2 : -1], refs[-1]
    copies = [
        pltpu.make_async_copy(refs[index], held[index], arrived.at[index])
        for index in range(3 * count)
    ]
    for number in order:
        for index in (2 * count + number, number, count + number):
            copies[index].start()
    first = place[3] == 0
    for number in order:
        for index in (2 * count + number, number, count + number):
            copies[index].wait()
        buffer = held[number][...] + held[count + number][...].astype(jnp.float32)
        product = dot(buffer, held[2 * count + number][...], ((1,), (0,)))
        keep[number] = jnp.where(first, product[:128], product[128:])
        send[number] = jnp.where(first, product[128:], product[:128])


def product_call(place, arguments):
    memory = pl.BlockSpec(memory_space=pltpu.VMEM)
    count = len(arguments) // 3
    return pl.pallas_call(
        functools.partial(product_kernel, count),
        out_shape=[jax.ShapeDtypeStruct((count, 128, RANK), jnp.float32)] * 2,
        in_specs=[pl.BlockSpec(memory_space=pltpu.SMEM)]
        + [pl.BlockSpec(memory_space=pl.ANY)] * (3 * count),
        out_specs=[memory] * 2,
        scratch_shapes=[pltpu.VMEM(value.shape, value.dtype) for value in arguments]
        + [pltpu.SemaphoreType.DMA((3 * count,))],
        cost_estimate=cost(7),
        compiler_params=pltpu.CompilerParams(vmem_limit_bytes=60 * 1024 * 1024),
        name="products",
    )(place, *arguments)


def pair_kernel(place, keep, received, *outs):
    for step in range(4):
        number = lax.rem(place[2] + step, 4)
        outs[step][...] = keep[number] + received[number]


def cross_kernel(query, place, *refs):
    count = 1 if query else 3
    momenta, gradients, refs = refs[:count], refs[count : 2 * count], refs[2 * count :]
    core = place[3]
    if query:
        products, refs = refs[0], refs[1:]
    else:
        same, other, products, refs = refs[:4], refs[4:8], refs[13], refs[8:13] + refs[14:]
        for index, step in enumerate(FOUR):
            number = lax.rem(place[2] + step, 4)
            products[number, aligned(128 * core, 128), :] = same[index][...]
            products[number, aligned(128 * (1 - core), 128), :] = other[index][...]
    (own, plus_first, minus_first, plus_second, minus_second, wide), refs = refs[:6], refs[6:]
    if query:
        buffer = momenta[0][...] + gradients[0][...].astype(jnp.float32)
        wide[...] = dot_three(buffer, products[0], ((0,), (0,)))
    else:
        narrow, gram = refs
        for number in range(3):
            buffer = momenta[number][...] + gradients[number][...].astype(jnp.float32)
            crossed = dot_three(buffer, products[1 + number], ((0,), (0,)))
            if number == 2:
                wide[...] = crossed
            else:
                narrow[number] = crossed
        left = products[place[2], :, aligned(128 * core, 128)]
        gram[...] = dot(left, products[place[2]], ((0,), (0,)))

    def put(out, start, step, upper):
        row = lax.rem(place[1] + step, 4)
        for deep in range(4 * upper, 4 * upper + 4):
            out[start : start + 32, :] = wide[aligned(256 * row + 32 * deep, 32), :]
            start = start + 32
            if not query:
                out[start : start + 8, :] = narrow[upper, aligned(32 * row + 8 * (deep % 4), 8), :]
                start = start + 8
        if not query:
            out[start : start + 16, :] = gram[aligned(32 * row + 16 * upper, 16), :]

    half = own.shape[0] // 2
    put(plus_first, 0, 2, 0)
    put(minus_first, 0, 2, 1)
    put(plus_first, half, 1, 1)
    put(minus_first, half, 3, 0)
    put(plus_second, 0, 1, 0)
    put(minus_second, 0, 3, 1)
    put(own, 0, 0, 0)
    put(own, half, 0, 1)


def pass_kernel(place, plus, minus, plus_in, minus_in, plus_out, minus_out):
    half = plus.shape[0]
    plus_out[...] = plus[...] + plus_in[:half, :]
    minus_out[...] = minus[...] + minus_in[:half, :]


def cross_call(query, place, operands):
    half = 128 if query else 176
    outs = [(2 * half, RANK)] * 3 + [(half, RANK)] * 2
    scratch = [(1024, RANK)]
    if not query:
        outs = outs + [(4, RANK, RANK)]
        scratch = scratch + [(2, 128, RANK), (128, RANK)]
    return call(
        functools.partial(cross_kernel, query),
        outs,
        (place, *operands),
        "crosses",
        scratch,
        2 if query else 3,
    )


def pass_call(place, plus, minus, plus_in, minus_in, micros=1):
    operands = (place, plus, minus, plus_in, minus_in)
    return call(pass_kernel, [plus.shape] * 2, operands, "passes", (), micros)


def row_kernel(place, *refs):
    (keep, near, far), total = refs[10:13], refs[13]
    for pieces, size, start in ((refs[:5], 32, 0), (refs[5:10], 40, 32)):
        own, plus_in, minus_in, plus, minus = pieces
        half = own.shape[0] // 2
        lower = own[:half, :] + minus_in[half:, :] + plus[...]
        upper = own[half:, :] + plus_in[half:, :] + minus[...]
        for deep in range(8):
            piece = (lower, upper)[deep // 4][size * (deep % 4) : size * (deep % 4) + size, :]
            total[72 * deep + start : 72 * deep + start + size, :] = piece
    total[576:592, :] = lower[160:, :]
    total[592:, :] = upper[160:, :]
    parity = lax.rem(place[0], 2)
    for block in range(4):
        rows = slice(72 * block, 72 * block + 72)
        keep[rows, :] = total[tall_rows(2 * block + parity), :]
        out = (near, far)[block // 2]
        rows = slice(72 * (block % 2), 72 * (block % 2) + 72)
        out[rows, :] = total[tall_rows(2 * block + 1 - parity), :]
    keep[288:, :] = total[576:, :]
    near[144:, :] = total[576:592, :]
    far[144:, :] = total[592:, :]


def tall_rows(block):
    return pl.ds(pl.multiple_of(72 * block, 8), 72)


def neighbour_kernel(place, keep, near, far, *refs):
    outs, total = refs[:4], refs[4]
    total[:144, :] = keep[:144, :] + near[:144, :]
    total[144:288, :] = keep[144:288, :] + far[:144, :]
    total[288:304, :] = keep[288:304, :] + near[144:, :]
    total[304:, :] = keep[304:, :] + far[144:, :]
    for step in range(4):
        block = lax.rem(place[0] // 2 + step, 4)
        outs[step][:72, :] = total[tall_rows(block), :]
        outs[step][72:, :] = total[288:, :]


def deep_kernel(place, *refs):
    pieces, shard, gram, terms = refs[:4], refs[4], refs[5], refs[6]
    shard[...] = (
        pieces[0][:72, :] + pieces[1][:72, :] + pieces[2][:72, :] + pieces[3][:72, :]
    )
    for index, step in enumerate(FOUR):
        source = lax.rem(place[0] + 8 - 2 * step, 8)
        terms[source // 2, :16, :] = pieces[index][72:88, :]
        terms[lax.rem((source + 1) // 2, 4), 16:, :] = pieces[index][88:, :]
    gram[...] = terms[0] + terms[1] + terms[2] + terms[3]


def quad_kernel(place, *refs):
    pieces, near, far, total = refs[:4], refs[4], refs[5], refs[6]
    for index, step in enumerate(FOUR):
        total[tall_rows(lax.rem(place[0] // 2 + step, 4)), :] = pieces[index][...]
    near[...] = total[:144, :]
    far[...] = total[144:, :]


def join_kernel(place, *refs):
    same, other, lower, upper, total = refs[:2], refs[2:4], refs[4], refs[5], refs[6]
    parity = lax.rem(place[0], 2)
    for block in range(4):
        rows = slice(72 * (block % 2), 72 * (block % 2) + 72)
        total[tall_rows(2 * block + parity), :] = same[block // 2][rows, :]
        total[tall_rows(2 * block + 1 - parity), :] = other[block // 2][rows, :]
    lower[...] = total[:288, :]
    upper[...] = total[288:, :]


def column_kernel(place, *refs):
    packed, same, other = refs[0], refs[1:4], refs[4:7]
    pieces, columns, squares, inverses = refs[7:15], refs[15:19], refs[19], refs[20]
    wide, narrow, joined = refs[21:]
    core = place[3]
    joined[0] = packed[...]
    for index, step in enumerate(FOUR[1:]):
        joined[step, aligned(96 * core, 8, 96), :] = same[index][...]
        joined[step, aligned(96 * (1 - core), 8, 96), :] = other[index][...]
    zero = jnp.zeros((128, 128), jnp.float32)
    for step in range(4):
        number = lax.rem(place[2] + step, 4)
        inverses[number, :64, :128] = joined[step, :64, :128]
        inverses[number, 64:128, :128] = joined[step, :64, 128:]
        inverses[number, :128, 128:] = zero
        inverses[number, 128:, :] = joined[step, 64:, :]
    for step in range(4):
        row = lax.rem(place[1] + step, 4)
        for deep in range(8):
            piece = pieces[2 * step + deep // 4]
            start = 72 * (deep % 4)
            rows = aligned(256 * row + 32 * deep, 32)
            wide[0, rows, :] = piece[start : start + 32, :]
            wide[1, rows, :] = piece[start + 32 : start + 64, :]
            rows = aligned(32 * row + 8 * (deep % 4), 8)
            narrow[deep // 4, rows, :] = piece[start + 64 : start + 72, :]
    for number in range(4):
        crossed = wide[number // 3] if number in (0, 3) else narrow[number - 1]
        column = dot_three(crossed, inverses[number])
        columns[number][...] = column
        squares[number : number + 1, :] = jnp.sum(column * column, axis=0, keepdims=True)


def momentum_kernel(place, *refs):
    momenta, gradients, columns, inverses, products = refs[:4], refs[4:8], refs[8:12], refs[12], refs[13]
    outs, orthos, held, sent = refs[14:18], refs[18], refs[19:23], refs[23]
    copies = [pltpu.make_async_copy(held[i], outs[i], sent.at[i]) for i in range(4)]
    for number in (0, 3, 1, 2):
        ortho = dot(products[number], inverses[number], ((1,), (1,)))
        orthos[number] = ortho
        buffer = momenta[number][...] + gradients[number][...].astype(jnp.float32)
        change = dot_three(ortho, columns[number][...])
        held[number][...] = buffer - (1.0 - MOMENTUM_DECAY) * change
        copies[number].start()
    for copy in copies:
        copy.wait()


def update_kernel(scales, place, *refs):
    squares, columns, orthos, outs = refs[0], refs[1:5], refs[5], refs[6:14]
    held, sent = refs[14:22], refs[22]
    copies = [pltpu.make_async_copy(held[i], outs[i], sent.at[i]) for i in range(8)]
    inverse = 1.0 / jnp.sqrt(squares[...] + EPSILON)
    for number in (0, 3, 1, 2):
        basis = columns[number][...] * inverse[number : number + 1, :]
        held[4 + number][...] = basis
        copies[4 + number].start()
        held[number][...] = scales[number] * dot_three(orthos[number], basis)
        copies[number].start()
    for copy in copies:
        copy.wait()


def result_call(body, shapes, operands, name, kept=()):
    return pl.pallas_call(
        body,
        out_shape=[jax.ShapeDtypeStruct(shape, jnp.float32) for shape in (*shapes, *kept)],
        in_specs=[pl.BlockSpec(memory_space=pltpu.SMEM)]
        + [pl.BlockSpec(memory_space=pltpu.VMEM)] * (len(operands) - 1),
        out_specs=[pl.BlockSpec(memory_space=pl.ANY)] * len(shapes)
        + [pl.BlockSpec(memory_space=pltpu.VMEM)] * len(kept),
        scratch_shapes=[pltpu.VMEM(shape, jnp.float32) for shape in shapes]
        + [pltpu.SemaphoreType.DMA((len(shapes),))],
        cost_estimate=cost(3),
        compiler_params=pltpu.CompilerParams(vmem_limit_bytes=24 * 1024 * 1024),
        name=name,
    )(*operands)


def local(*arguments):
    momenta = arguments[0::3]
    gradients = arguments[1::3]
    factors = arguments[2::3]
    height = momenta[0].shape[0]
    place = jnp.stack([lax.axis_index(axis) for axis in SIZES]).astype(jnp.int32)

    half = (128, RANK)
    send, keep = product_call(place, (*momenta, *gradients, *factors))
    received = shift_along(send, "core", 1)
    pieces = call(pair_kernel, [half] * 4, (place, keep, received), "pairs")
    shard = sum(reversed(from_three(pieces[1:], "x", -1)), pieces[0])
    same = [shard] + from_three([shard] * 3, "x", 1)
    other = [shift_along(piece, "core", 1) for piece in same]

    *others, products = cross_call(False, place, (*momenta[1:], *gradients[1:], *same, *other))
    query = cross_call(True, place, (momenta[0], gradients[0], products))
    others_in = shift_along(others[1], "y", -1), shift_along(others[2], "y", 1)
    query_in = shift_along(query[1], "y", -1), shift_along(query[2], "y", 1)
    plus, minus = pass_call(place, others[3], others[4], *others_in)
    query_in, plus, minus = lax.optimization_barrier((query_in, plus, minus))
    other_pieces = (others[0], *others_in, shift_along(plus, "y", -1), shift_along(minus, "y", 1))
    plus, minus = pass_call(place, query[3], query[4], *query_in, 20)
    query_pieces = (query[0], *query_in, shift_along(plus, "y", -1), shift_along(minus, "y", 1))

    keep, near, far = call(
        row_kernel,
        [(320, RANK), (160, RANK), (160, RANK)],
        (place, *query_pieces, *other_pieces),
        "rows",
        [(608, RANK)],
    )
    near, far = neighbours(near, far)
    pieces = call(
        neighbour_kernel, [(104, RANK)] * 4, (place, keep, near, far), "neighbours", [(320, RANK)]
    )
    pieces = [pieces[0]] + from_three(pieces[1:], "z", -2)
    shard, gram = call(
        deep_kernel, [(72, RANK), (32, RANK)], (place, *pieces), "deeps", [(4, 32, RANK)]
    )

    beside = shift_along(gram, "core", 1)
    first = place[3] == 0
    pair = jnp.concatenate([jnp.where(first, gram, beside), jnp.where(first, beside, gram)], axis=0)
    rows = [pair] + from_three([pair] * 3, "y", 1)

    pieces = [shard] + from_three([shard] * 3, "z", 2)
    near, far = call(quad_kernel, [(144, RANK)] * 2, (place, *pieces), "quads", [(288, RANK)])
    lower, upper = call(
        join_kernel,
        [(288, RANK)] * 2,
        (place, near, far, *neighbours(near, far)),
        "joins",
        [(576, RANK)],
    )
    lower, upper, rows = lax.optimization_barrier((lower, upper, rows))
    lower_before = shift_along(lower, "y", -1)
    upper_after = shift_along(upper, "y", 1)
    upper_later, lower_later, rows = lax.optimization_barrier((upper, lower, rows))
    upper_before = shift_along(upper_later, "y", -1)
    lower_after = shift_along(lower_later, "y", 1)

    packed, mine = call(
        inverse_kernel,
        [(192, RANK), (96, RANK)],
        (place, *rows),
        "inverse",
        [(RANK, RANK), (RANK, RANK), (RANK, 2 * RANK)],
        11,
    )
    mine, lower_before, upper_after = lax.optimization_barrier((mine, lower_before, upper_after))
    lower_across = shift_along(lower_before, "y", -1)
    upper_across = shift_along(upper_after, "y", 1)
    mine, upper_before, lower_after = lax.optimization_barrier((mine, upper_before, lower_after))
    same = from_three([mine] * 3, "x", 1)
    same[2], lower_across, upper_across = lax.optimization_barrier(
        (same[2], lower_across, upper_across)
    )
    other = [shift_along(piece, "core", 1) for piece in same]
    tall = [(momentum.shape[1], RANK) for momentum in momenta]
    flat = [momentum.shape for momentum in momenta]
    *columns, squares, inverses = call(
        column_kernel,
        tall + [(4, RANK), (4, RANK, RANK)],
        (place, packed, *same, *other, lower, upper, lower_after, upper_after)
        + (lower_across, upper_across, lower_before, upper_before),
        "columns",
        [(2, 1024, RANK), (2, 128, RANK), (4, 192, RANK)],
        3,
    )
    squares = squares + shift_along(squares, "core", 1)
    squares = squares + sum(reversed(from_three([squares] * 3, "x", 1)))
    *new_momenta, orthos = result_call(
        momentum_kernel,
        flat,
        (place, *momenta, *gradients, *columns, inverses, products),
        "momenta",
        [(4, RANK, RANK)],
    )
    scales = [math.sqrt(height * 32 * shape[1] * 8 / RANK) for shape in flat]
    outs = result_call(
        functools.partial(update_kernel, scales),
        flat + tall,
        (place, squares, *columns, orthos),
        "updates",
    )
    results = []
    for number in range(4):
        results = results + [outs[number], new_momenta[number], outs[4 + number]]
    return tuple(results)


def solution(mesh):
    devices = mesh.devices.reshape(tuple(SIZES.values()))
    finer = Mesh(devices, tuple(SIZES))
    wide = P(("z", "y"), ("x", "core"))
    tall = P(("x", "core"), None)
    return jax.shard_map(
        local,
        mesh=finer,
        in_specs=(wide, wide, tall) * 4,
        out_specs=(wide, wide, tall) * 4,
        check_vma=False,
    )
```

```python
import functools
import math

import jax
import jax.numpy as jnp
from jax import lax
from jax.experimental import pallas as pl
from jax.experimental.pallas import tpu as pltpu
from jax.sharding import Mesh
from jax.sharding import PartitionSpec as P

PRECISE = lax.Precision.HIGHEST
MOMENTUM_DECAY = 0.95
SHIFT_RATIO = 0.0001
EPSILON = 1e-06
RANK = 256
PANEL = 16
FOUR = (0, 2, 1, 3)
TURNED = (0, 3, 1, 2)
SIZES = {"z": 8, "y": 4, "x": 4, "core": 2}


def dot(left, right, dims):
    return lax.dot_general(
        left, right, (dims, ((), ())), precision=PRECISE, preferred_element_type=jnp.float32
    )


def dot_three(left, right, dims=((1,), (1,))):
    parts = []
    for values in (left, right):
        high = values.astype(jnp.bfloat16)
        parts.append((high, (values - high.astype(jnp.float32)).astype(jnp.bfloat16)))
    (left_high, left_low), (right_high, right_low) = parts

    def one(first, second):
        return lax.dot_general(
            first, second, (dims, ((), ())), preferred_element_type=jnp.float32
        )

    return one(left_low, right_high) + one(left_high, right_low) + one(left_high, right_high)


def split3(values):
    high = values.astype(jnp.bfloat16)
    rest = values - high.astype(jnp.float32)
    mid = rest.astype(jnp.bfloat16)
    low = (rest - mid.astype(jnp.float32)).astype(jnp.bfloat16)
    return high, mid, low


def inverse_kernel(place, *refs):
    pieces, (packed, mine, gram_ref, out_ref, work) = refs[:4], refs[4:]
    for step, piece in zip(TURNED, pieces):
        rows = 32 * lax.rem(place[1] + step, 4)
        gram_ref[pl.ds(pl.multiple_of(rows, 32), 32), :] = piece[:32, :]
        gram_ref[pl.ds(pl.multiple_of(rows + 128, 32), 32), :] = piece[32:, :]
    gram = gram_ref[...]
    rows = lax.broadcasted_iota(jnp.int32, (RANK, RANK), 0)
    cols = lax.broadcasted_iota(jnp.int32, (RANK, RANK), 1)
    unit = jnp.where(rows == cols, 1.0, 0.0).astype(jnp.float32)
    shift = SHIFT_RATIO * jnp.sum(gram * unit) / RANK
    work[:, :RANK] = gram + shift * unit
    work[:, RANK:] = unit
    sub = lax.broadcasted_iota(jnp.int32, (PANEL, 128), 0)
    for start in range(0, RANK, PANEL):
        here, end = start // 128, start + PANEL
        blocks = list(range(here, 3 + here))
        panel = {i: work[start:end, 128 * i : 128 * (i + 1)] for i in blocks}
        columns = [
            jnp.broadcast_to(panel[here][:, j : j + 1], (PANEL, 128))
            for j in range(start % 128, start % 128 + PANEL)
        ]
        scale = jnp.zeros((PANEL, 128), jnp.float32)
        for j in range(PANEL):
            root = lax.rsqrt(columns[j][j : j + 1, :])
            scale = jnp.where(sub == j, root, scale)
            mult = jnp.where(sub > j, columns[j] * (root * root), 0.0)
            for other in range(j + 1, PANEL):
                columns[other] = columns[other] - mult * columns[other][j : j + 1, :]
            if j < PANEL - 1:
                panel = {i: panel[i] - mult * panel[i][j : j + 1, :] for i in blocks}
        panel = {i: panel[i] * scale for i in blocks}
        for i in range(2, 4):
            out_ref[start:end, 128 * (i - 2) : 128 * (i - 1)] = panel.get(i, jnp.zeros_like(scale))
        first = end // 128
        if first == 2:
            break
        changed = [i for i in blocks if i >= first]
        left = jnp.concatenate([panel[i] for i in changed if i < 2], axis=1)
        lane = lax.broadcasted_iota(jnp.int32, left.shape, 1) + 128 * first
        left_high, left_mid, left_low = split3(jnp.where(lane >= end, left, 0.0))
        high, mid, low = split3(jnp.concatenate([panel[i] for i in changed], axis=1))
        lhs = jnp.concatenate([left_high, left_high, left_mid, left_high, left_low, left_mid], axis=0)
        rhs = jnp.concatenate([high, mid, high, low, high, mid], axis=0)
        change = lax.dot_general(
            lhs, rhs, (((0,), (0,)), ((), ())), preferred_element_type=jnp.float32
        )
        for place_in, i in enumerate(changed):
            work[end:, 128 * i : 128 * (i + 1)] -= change[
                end - 128 * first :, 128 * place_in : 128 * (place_in + 1)
            ]

    packed[:64, :128] = out_ref[:64, :128]
    packed[:64, 128:] = out_ref[64:128, :128]
    packed[64:, :] = out_ref[128:, :]
    mine[...] = packed[aligned(96 * place[3], 8, 96), :]


def shift_along(values, axis, step):
    size = SIZES[axis]
    return lax.ppermute(values, axis, [((i + step) % size, i) for i in range(size)])


def from_three(values, axis, step):
    return [shift_along(values[index - 1], axis, index * step) for index in FOUR[1:]]


def neighbours(near, far):
    pairs = [(i, i ^ 1) for i in range(8)]
    others = [(i, (i + 1) % 8 if i % 2 else (i + 7) % 8) for i in range(8)]
    return lax.ppermute(near, "z", pairs), lax.ppermute(far, "z", others)


def cost(micros):
    return pl.CostEstimate(flops=int(1.1e9 * micros), bytes_accessed=0, transcendentals=0)


def call(body, outs, operands, name, scratch=(), micros=1):
    memory = pl.BlockSpec(memory_space=pltpu.VMEM)
    return pl.pallas_call(
        body,
        out_shape=[jax.ShapeDtypeStruct(shape, jnp.float32) for shape in outs],
        in_specs=[pl.BlockSpec(memory_space=pltpu.SMEM)] + [memory] * (len(operands) - 1),
        out_specs=[memory] * len(outs),
        scratch_shapes=[pltpu.VMEM(shape, jnp.float32) for shape in scratch],
        cost_estimate=cost(micros),
        compiler_params=pltpu.CompilerParams(vmem_limit_bytes=24 * 1024 * 1024),
        name=name,
    )(*operands)


def aligned(start, multiple, size=None):
    return pl.ds(pl.multiple_of(start, multiple), size or multiple)


def product_kernel(count, place, *refs):
    order = (1, 2, 0, 3)
    send, keep = refs[3 * count : 3 * count + 2]
    held, arrived = refs[3 * count + 2 : -1], refs[-1]
    copies = [
        pltpu.make_async_copy(refs[index], held[index], arrived.at[index])
        for index in range(3 * count)
    ]
    for number in order:
        for index in (2 * count + number, number, count + number):
            copies[index].start()
    first = place[3] == 0
    for number in order:
        for index in (2 * count + number, number, count + number):
            copies[index].wait()
        buffer = held[number][...] + held[count + number][...].astype(jnp.float32)
        product = dot(buffer, held[2 * count + number][...], ((1,), (0,)))
        keep[number] = jnp.where(first, product[:128], product[128:])
        send[number] = jnp.where(first, product[128:], product[:128])


def product_call(place, arguments):
    memory = pl.BlockSpec(memory_space=pltpu.VMEM)
    count = len(arguments) // 3
    return pl.pallas_call(
        functools.partial(product_kernel, count),
        out_shape=[jax.ShapeDtypeStruct((count, 128, RANK), jnp.float32)] * 2,
        in_specs=[pl.BlockSpec(memory_space=pltpu.SMEM)]
        + [pl.BlockSpec(memory_space=pl.ANY)] * (3 * count),
        out_specs=[memory] * 2,
        scratch_shapes=[pltpu.VMEM(value.shape, value.dtype) for value in arguments]
        + [pltpu.SemaphoreType.DMA((3 * count,))],
        cost_estimate=cost(7),
        compiler_params=pltpu.CompilerParams(vmem_limit_bytes=60 * 1024 * 1024),
        name="products",
    )(place, *arguments)


def pair_kernel(place, keep, received, *outs):
    for step in range(4):
        number = lax.rem(place[2] + step, 4)
        outs[step][...] = keep[number] + received[number]


def cross_kernel(query, place, *refs):
    count = 1 if query else 3
    momenta, gradients, refs = refs[:count], refs[count : 2 * count], refs[2 * count :]
    core = place[3]
    if query:
        products, refs = refs[0], refs[1:]
    else:
        same, other, products, refs = refs[:4], refs[4:8], refs[13], refs[8:13] + refs[14:]
        for index, step in enumerate(FOUR):
            number = lax.rem(place[2] + step, 4)
            products[number, aligned(128 * core, 128), :] = same[index][...]
            products[number, aligned(128 * (1 - core), 128), :] = other[index][...]
    (own, plus_first, minus_first, plus_second, minus_second, wide), refs = refs[:6], refs[6:]
    if query:
        buffer = momenta[0][...] + gradients[0][...].astype(jnp.float32)
        wide[...] = dot_three(buffer, products[0], ((0,), (0,)))
    else:
        narrow, gram = refs
        for number in range(3):
            buffer = momenta[number][...] + gradients[number][...].astype(jnp.float32)
            crossed = dot_three(buffer, products[1 + number], ((0,), (0,)))
            if number == 2:
                wide[...] = crossed
            else:
                narrow[number] = crossed
        left = products[place[2], :, aligned(128 * core, 128)]
        gram[...] = dot(left, products[place[2]], ((0,), (0,)))

    def put(out, start, step, upper):
        row = lax.rem(place[1] + step, 4)
        for deep in range(4 * upper, 4 * upper + 4):
            out[start : start + 32, :] = wide[aligned(256 * row + 32 * deep, 32), :]
            start = start + 32
            if not query:
                out[start : start + 8, :] = narrow[upper, aligned(32 * row + 8 * (deep % 4), 8), :]
                start = start + 8
        if not query:
            out[start : start + 16, :] = gram[aligned(32 * row + 16 * upper, 16), :]

    half = own.shape[0] // 2
    put(plus_first, 0, 2, 0)
    put(minus_first, 0, 2, 1)
    put(plus_first, half, 1, 1)
    put(minus_first, half, 3, 0)
    put(plus_second, 0, 1, 0)
    put(minus_second, 0, 3, 1)
    put(own, 0, 0, 0)
    put(own, half, 0, 1)


def pass_kernel(place, plus, minus, plus_in, minus_in, plus_out, minus_out):
    half = plus.shape[0]
    plus_out[...] = plus[...] + plus_in[:half, :]
    minus_out[...] = minus[...] + minus_in[:half, :]


def cross_call(query, place, operands):
    half = 128 if query else 176
    outs = [(2 * half, RANK)] * 3 + [(half, RANK)] * 2
    scratch = [(1024, RANK)]
    if not query:
        outs = outs + [(4, RANK, RANK)]
        scratch = scratch + [(2, 128, RANK), (128, RANK)]
    return call(
        functools.partial(cross_kernel, query),
        outs,
        (place, *operands),
        "crosses",
        scratch,
        2 if query else 3,
    )


def pass_call(place, plus, minus, plus_in, minus_in, micros=1):
    operands = (place, plus, minus, plus_in, minus_in)
    return call(pass_kernel, [plus.shape] * 2, operands, "passes", (), micros)


def row_kernel(place, *refs):
    (keep, near, far), total = refs[10:13], refs[13]
    for pieces, size, start in ((refs[:5], 32, 0), (refs[5:10], 40, 32)):
        own, plus_in, minus_in, plus, minus = pieces
        half = own.shape[0] // 2
        lower = own[:half, :] + minus_in[half:, :] + plus[...]
        upper = own[half:, :] + plus_in[half:, :] + minus[...]
        for deep in range(8):
            piece = (lower, upper)[deep // 4][size * (deep % 4) : size * (deep % 4) + size, :]
            total[72 * deep + start : 72 * deep + start + size, :] = piece
    total[576:592, :] = lower[160:, :]
    total[592:, :] = upper[160:, :]
    parity = lax.rem(place[0], 2)
    for block in range(4):
        rows = slice(72 * block, 72 * block + 72)
        keep[rows, :] = total[tall_rows(2 * block + parity), :]
        out = (near, far)[block // 2]
        rows = slice(72 * (block % 2), 72 * (block % 2) + 72)
        out[rows, :] = total[tall_rows(2 * block + 1 - parity), :]
    keep[288:, :] = total[576:, :]
    near[144:, :] = total[576:592, :]
    far[144:, :] = total[592:, :]


def tall_rows(block):
    return pl.ds(pl.multiple_of(72 * block, 8), 72)


def neighbour_kernel(place, keep, near, far, *refs):
    outs, total = refs[:4], refs[4]
    total[:144, :] = keep[:144, :] + near[:144, :]
    total[144:288, :] = keep[144:288, :] + far[:144, :]
    total[288:304, :] = keep[288:304, :] + near[144:, :]
    total[304:, :] = keep[304:, :] + far[144:, :]
    for step in range(4):
        block = lax.rem(place[0] // 2 + step, 4)
        outs[step][:72, :] = total[tall_rows(block), :]
        outs[step][72:, :] = total[288:, :]


def deep_kernel(place, *refs):
    pieces, shard, gram, terms = refs[:4], refs[4], refs[5], refs[6]
    shard[...] = (
        pieces[0][:72, :] + pieces[1][:72, :] + pieces[2][:72, :] + pieces[3][:72, :]
    )
    for index, step in enumerate(FOUR):
        source = lax.rem(place[0] + 8 - 2 * step, 8)
        terms[source // 2, :16, :] = pieces[index][72:88, :]
        terms[lax.rem((source + 1) // 2, 4), 16:, :] = pieces[index][88:, :]
    gram[...] = terms[0] + terms[1] + terms[2] + terms[3]


def quad_kernel(place, *refs):
    pieces, near, far, total = refs[:4], refs[4], refs[5], refs[6]
    for index, step in enumerate(TURNED):
        total[tall_rows(lax.rem(place[0] // 2 + step, 4)), :] = pieces[index][...]
    near[...] = total[:144, :]
    far[...] = total[144:, :]


def join_kernel(place, *refs):
    same, other, total = refs[:2], refs[2:4], refs[4]
    parity = lax.rem(place[0], 2)
    for block in range(4):
        rows = slice(72 * (block % 2), 72 * (block % 2) + 72)
        total[tall_rows(2 * block + parity), :] = same[block // 2][rows, :]
        total[tall_rows(2 * block + 1 - parity), :] = other[block // 2][rows, :]


def forward_kernel(place, before, after, lower, upper):
    lower[...] = before[:288, :]
    upper[...] = after[288:, :]


def column_kernel(place, *refs):
    packed, same, other = refs[0], refs[1:4], refs[4:7]
    pieces, columns, squares, inverses = refs[7:12], refs[12:16], refs[16], refs[17]
    wide, narrow, joined = refs[18:]
    core = place[3]
    joined[0] = packed[...]
    for index, step in enumerate(TURNED[1:]):
        joined[step, aligned(96 * core, 8, 96), :] = same[index][...]
        joined[step, aligned(96 * (1 - core), 8, 96), :] = other[index][...]
    zero = jnp.zeros((128, 128), jnp.float32)
    for step in range(4):
        number = lax.rem(place[2] + step, 4)
        inverses[number, :64, :128] = joined[step, :64, :128]
        inverses[number, 64:128, :128] = joined[step, :64, 128:]
        inverses[number, :128, 128:] = zero
        inverses[number, 128:, :] = joined[step, 64:, :]
    for step in range(4):
        row = lax.rem(place[1] + step, 4)
        for deep in range(8):
            piece = pieces[(0, 1, 2 + deep // 4, 4)[step]]
            start = 72 * (deep % 4 if step == 2 else deep)
            rows = aligned(256 * row + 32 * deep, 32)
            wide[0, rows, :] = piece[start : start + 32, :]
            wide[1, rows, :] = piece[start + 32 : start + 64, :]
            rows = aligned(32 * row + 8 * (deep % 4), 8)
            narrow[deep // 4, rows, :] = piece[start + 64 : start + 72, :]
    for number in range(4):
        crossed = wide[number // 3] if number in (0, 3) else narrow[number - 1]
        column = dot_three(crossed, inverses[number])
        columns[number][...] = column
        squares[number : number + 1, :] = jnp.sum(column * column, axis=0, keepdims=True)


def momentum_kernel(place, *refs):
    momenta, gradients, columns, inverses, products = refs[:4], refs[4:8], refs[8:12], refs[12], refs[13]
    outs, orthos, held, sent = refs[14:18], refs[18], refs[19:23], refs[23]
    copies = [pltpu.make_async_copy(held[i], outs[i], sent.at[i]) for i in range(4)]
    for number in (0, 3, 1, 2):
        ortho = dot(products[number], inverses[number], ((1,), (1,)))
        orthos[number] = ortho
        buffer = momenta[number][...] + gradients[number][...].astype(jnp.float32)
        change = dot_three(ortho, columns[number][...])
        held[number][...] = buffer - (1.0 - MOMENTUM_DECAY) * change
        copies[number].start()
    for copy in copies:
        copy.wait()


def update_kernel(scales, place, *refs):
    squares, columns, orthos, outs = refs[0], refs[1:5], refs[5], refs[6:14]
    held, sent = refs[14:22], refs[22]
    copies = [pltpu.make_async_copy(held[i], outs[i], sent.at[i]) for i in range(8)]
    inverse = 1.0 / jnp.sqrt(squares[...] + EPSILON)
    for number in (0, 3, 1, 2):
        basis = columns[number][...] * inverse[number : number + 1, :]
        held[4 + number][...] = basis
        copies[4 + number].start()
        held[number][...] = scales[number] * dot_three(orthos[number], basis)
        copies[number].start()
    for copy in copies:
        copy.wait()


def result_call(body, shapes, operands, name, kept=()):
    return pl.pallas_call(
        body,
        out_shape=[jax.ShapeDtypeStruct(shape, jnp.float32) for shape in (*shapes, *kept)],
        in_specs=[pl.BlockSpec(memory_space=pltpu.SMEM)]
        + [pl.BlockSpec(memory_space=pltpu.VMEM)] * (len(operands) - 1),
        out_specs=[pl.BlockSpec(memory_space=pl.ANY)] * len(shapes)
        + [pl.BlockSpec(memory_space=pltpu.VMEM)] * len(kept),
        scratch_shapes=[pltpu.VMEM(shape, jnp.float32) for shape in shapes]
        + [pltpu.SemaphoreType.DMA((len(shapes),))],
        cost_estimate=cost(3),
        compiler_params=pltpu.CompilerParams(vmem_limit_bytes=24 * 1024 * 1024),
        name=name,
    )(*operands)


def local(*arguments):
    momenta = arguments[0::3]
    gradients = arguments[1::3]
    factors = arguments[2::3]
    height = momenta[0].shape[0]
    place = jnp.stack([lax.axis_index(axis) for axis in SIZES]).astype(jnp.int32)

    half = (128, RANK)
    send, keep = product_call(place, (*momenta, *gradients, *factors))
    received = shift_along(send, "core", 1)
    pieces = call(pair_kernel, [half] * 4, (place, keep, received), "pairs")
    shard = sum(reversed(from_three(pieces[1:], "x", -1)), pieces[0])
    same = [shard] + from_three([shard] * 3, "x", 1)
    other = [shift_along(piece, "core", 1) for piece in same]

    *others, products = cross_call(False, place, (*momenta[1:], *gradients[1:], *same, *other))
    query = cross_call(True, place, (momenta[0], gradients[0], products))
    others_in = shift_along(others[1], "y", -1), shift_along(others[2], "y", 1)
    query_in = shift_along(query[1], "y", -1), shift_along(query[2], "y", 1)
    plus, minus = pass_call(place, others[3], others[4], *others_in)
    query_in, plus, minus = lax.optimization_barrier((query_in, plus, minus))
    other_pieces = (others[0], *others_in, shift_along(plus, "y", -1), shift_along(minus, "y", 1))
    plus, minus = pass_call(place, query[3], query[4], *query_in, 20)
    query_pieces = (query[0], *query_in, shift_along(plus, "y", -1), shift_along(minus, "y", 1))

    keep, near, far = call(
        row_kernel,
        [(320, RANK), (160, RANK), (160, RANK)],
        (place, *query_pieces, *other_pieces),
        "rows",
        [(608, RANK)],
    )
    near, far = neighbours(near, far)
    pieces = call(
        neighbour_kernel, [(104, RANK)] * 4, (place, keep, near, far), "neighbours", [(320, RANK)]
    )
    pieces = [pieces[0]] + from_three(pieces[1:], "z", -2)
    shard, gram = call(
        deep_kernel, [(72, RANK), (32, RANK)], (place, *pieces), "deeps", [(4, 32, RANK)]
    )

    beside = shift_along(gram, "core", 1)
    first = place[3] == 0
    pair = jnp.concatenate([jnp.where(first, gram, beside), jnp.where(first, beside, gram)], axis=0)
    rows = [pair] + from_three([pair] * 3, "y", 1)[::-1]

    pieces = [shard] + from_three([shard] * 3, "z", 2)[::-1]
    near, far = call(quad_kernel, [(144, RANK)] * 2, (place, *pieces), "quads", [(288, RANK)])
    (joined,) = call(
        join_kernel, [(576, RANK)], (place, near, far, *neighbours(near, far)), "joins"
    )
    before = shift_along(joined, "y", -1)
    after = shift_along(joined, "y", 1)

    packed, mine = call(
        inverse_kernel,
        [(192, RANK), (96, RANK)],
        (place, *rows),
        "inverse",
        [(RANK, RANK), (RANK, RANK), (RANK, 2 * RANK)],
        11,
    )
    same = from_three([mine] * 3, "x", 1)[::-1]
    *same, before, after = lax.optimization_barrier((*same, before, after))
    operands = (place, before, after)
    lower, upper = call(forward_kernel, [(288, RANK)] * 2, operands, "forwards")
    lower = shift_along(lower, "y", -1)
    upper = shift_along(upper, "y", 1)
    other = [shift_along(piece, "core", 1) for piece in same]
    tall = [(momentum.shape[1], RANK) for momentum in momenta]
    flat = [momentum.shape for momentum in momenta]
    *columns, squares, inverses = call(
        column_kernel,
        tall + [(4, RANK), (4, RANK, RANK)],
        (place, packed, *same, *other, joined, after, lower, upper, before),
        "columns",
        [(2, 1024, RANK), (2, 128, RANK), (4, 192, RANK)],
        3,
    )
    squares = squares + shift_along(squares, "core", 1)
    squares = squares + sum(reversed(from_three([squares] * 3, "x", 1)))
    *new_momenta, orthos = result_call(
        momentum_kernel,
        flat,
        (place, *momenta, *gradients, *columns, inverses, products),
        "momenta",
        [(4, RANK, RANK)],
    )
    scales = [math.sqrt(height * 32 * shape[1] * 8 / RANK) for shape in flat]
    outs = result_call(
        functools.partial(update_kernel, scales),
        flat + tall,
        (place, squares, *columns, orthos),
        "updates",
    )
    results = []
    for number in range(4):
        results = results + [outs[number], new_momenta[number], outs[4 + number]]
    return tuple(results)


def solution(mesh):
    devices = mesh.devices.reshape(tuple(SIZES.values()))
    finer = Mesh(devices, tuple(SIZES))
    wide = P(("z", "y"), ("x", "core"))
    tall = P(("x", "core"), None)
    return jax.shard_map(
        local,
        mesh=finer,
        in_specs=(wide, wide, tall) * 4,
        out_specs=(wide, wide, tall) * 4,
        check_vma=False,
    )
```

```python
import functools
import math

import jax
import jax.numpy as jnp
from jax import lax
from jax.experimental import pallas as pl
from jax.experimental.pallas import tpu as pltpu
from jax.sharding import Mesh
from jax.sharding import PartitionSpec as P

PRECISE = lax.Precision.HIGHEST
MOMENTUM_DECAY = 0.95
SHIFT_RATIO = 0.0001
EPSILON = 1e-06
RANK = 256
PANEL = 16
FOUR = (0, 2, 1, 3)
TURNED = (0, 3, 1, 2)
SIZES = {"z": 8, "y": 4, "x": 4, "core": 2}


def dot(left, right, dims):
    return lax.dot_general(
        left, right, (dims, ((), ())), precision=PRECISE, preferred_element_type=jnp.float32
    )


def dot_three(left, right, dims=((1,), (1,))):
    parts = []
    for values in (left, right):
        high = values.astype(jnp.bfloat16)
        parts.append((high, (values - high.astype(jnp.float32)).astype(jnp.bfloat16)))
    (left_high, left_low), (right_high, right_low) = parts

    def one(first, second):
        return lax.dot_general(
            first, second, (dims, ((), ())), preferred_element_type=jnp.float32
        )

    return one(left_low, right_high) + one(left_high, right_low) + one(left_high, right_high)


def split3(values):
    high = values.astype(jnp.bfloat16)
    rest = values - high.astype(jnp.float32)
    mid = rest.astype(jnp.bfloat16)
    low = (rest - mid.astype(jnp.float32)).astype(jnp.bfloat16)
    return high, mid, low


def inverse_kernel(place, *refs):
    pieces, (packed, mine, gram_ref, out_ref, work) = refs[:4], refs[4:]
    for step, piece in zip(TURNED, pieces):
        rows = 32 * lax.rem(place[1] + step, 4)
        gram_ref[pl.ds(pl.multiple_of(rows, 32), 32), :] = piece[:32, :]
        gram_ref[pl.ds(pl.multiple_of(rows + 128, 32), 32), :] = piece[32:, :]
    gram = gram_ref[...]
    rows = lax.broadcasted_iota(jnp.int32, (RANK, RANK), 0)
    cols = lax.broadcasted_iota(jnp.int32, (RANK, RANK), 1)
    unit = jnp.where(rows == cols, 1.0, 0.0).astype(jnp.float32)
    shift = SHIFT_RATIO * jnp.sum(gram * unit) / RANK
    work[:, :RANK] = gram + shift * unit
    work[:, RANK:] = unit
    sub = lax.broadcasted_iota(jnp.int32, (PANEL, 128), 0)
    for start in range(0, RANK, PANEL):
        here, end = start // 128, start + PANEL
        blocks = list(range(here, 3 + here))
        panel = {i: work[start:end, 128 * i : 128 * (i + 1)] for i in blocks}
        columns = [
            jnp.broadcast_to(panel[here][:, j : j + 1], (PANEL, 128))
            for j in range(start % 128, start % 128 + PANEL)
        ]
        scale = jnp.zeros((PANEL, 128), jnp.float32)
        for j in range(PANEL):
            root = lax.rsqrt(columns[j][j : j + 1, :])
            scale = jnp.where(sub == j, root, scale)
            mult = jnp.where(sub > j, columns[j] * (root * root), 0.0)
            for other in range(j + 1, PANEL):
                columns[other] = columns[other] - mult * columns[other][j : j + 1, :]
            if j < PANEL - 1:
                panel = {i: panel[i] - mult * panel[i][j : j + 1, :] for i in blocks}
        panel = {i: panel[i] * scale for i in blocks}
        for i in range(2, 4):
            out_ref[start:end, 128 * (i - 2) : 128 * (i - 1)] = panel.get(i, jnp.zeros_like(scale))
        first = end // 128
        if first == 2:
            break
        changed = [i for i in blocks if i >= first]
        left = jnp.concatenate([panel[i] for i in changed if i < 2], axis=1)
        lane = lax.broadcasted_iota(jnp.int32, left.shape, 1) + 128 * first
        left_high, left_mid, left_low = split3(jnp.where(lane >= end, left, 0.0))
        high, mid, low = split3(jnp.concatenate([panel[i] for i in changed], axis=1))
        lhs = jnp.concatenate([left_high, left_high, left_mid, left_high, left_low, left_mid], axis=0)
        rhs = jnp.concatenate([high, mid, high, low, high, mid], axis=0)
        change = lax.dot_general(
            lhs, rhs, (((0,), (0,)), ((), ())), preferred_element_type=jnp.float32
        )
        for place_in, i in enumerate(changed):
            work[end:, 128 * i : 128 * (i + 1)] -= change[
                end - 128 * first :, 128 * place_in : 128 * (place_in + 1)
            ]

    packed[:64, :128] = out_ref[:64, :128]
    packed[:64, 128:] = out_ref[64:128, :128]
    packed[64:, :] = out_ref[128:, :]
    mine[...] = packed[aligned(96 * place[3], 8, 96), :]


def shift_along(values, axis, step):
    size = SIZES[axis]
    return lax.ppermute(values, axis, [((i + step) % size, i) for i in range(size)])


def from_three(values, axis, step):
    return [shift_along(values[index - 1], axis, index * step) for index in FOUR[1:]]


def neighbours(near, far):
    pairs = [(i, i ^ 1) for i in range(8)]
    others = [(i, (i + 1) % 8 if i % 2 else (i + 7) % 8) for i in range(8)]
    return lax.ppermute(near, "z", pairs), lax.ppermute(far, "z", others)


def cost(micros):
    return pl.CostEstimate(flops=int(1.1e9 * micros), bytes_accessed=0, transcendentals=0)


def call(body, outs, operands, name, scratch=(), micros=1):
    memory = pl.BlockSpec(memory_space=pltpu.VMEM)
    return pl.pallas_call(
        body,
        out_shape=[jax.ShapeDtypeStruct(shape, jnp.float32) for shape in outs],
        in_specs=[pl.BlockSpec(memory_space=pltpu.SMEM)] + [memory] * (len(operands) - 1),
        out_specs=[memory] * len(outs),
        scratch_shapes=[pltpu.VMEM(shape, jnp.float32) for shape in scratch],
        cost_estimate=cost(micros),
        compiler_params=pltpu.CompilerParams(vmem_limit_bytes=24 * 1024 * 1024),
        name=name,
    )(*operands)


def aligned(start, multiple, size=None):
    return pl.ds(pl.multiple_of(start, multiple), size or multiple)


def product_kernel(count, place, *refs):
    order = (1, 2, 0, 3)
    send, keep = refs[3 * count : 3 * count + 2]
    held, arrived = refs[3 * count + 2 : -1], refs[-1]
    copies = [
        pltpu.make_async_copy(refs[index], held[index], arrived.at[index])
        for index in range(3 * count)
    ]
    for number in order:
        for index in (2 * count + number, number, count + number):
            copies[index].start()
    first = place[3] == 0
    for number in order:
        for index in (2 * count + number, number, count + number):
            copies[index].wait()
        buffer = held[number][...] + held[count + number][...].astype(jnp.float32)
        product = dot(buffer, held[2 * count + number][...], ((1,), (0,)))
        keep[number] = jnp.where(first, product[:128], product[128:])
        send[number] = jnp.where(first, product[128:], product[:128])


def product_call(place, arguments):
    memory = pl.BlockSpec(memory_space=pltpu.VMEM)
    count = len(arguments) // 3
    return pl.pallas_call(
        functools.partial(product_kernel, count),
        out_shape=[jax.ShapeDtypeStruct((count, 128, RANK), jnp.float32)] * 2,
        in_specs=[pl.BlockSpec(memory_space=pltpu.SMEM)]
        + [pl.BlockSpec(memory_space=pl.ANY)] * (3 * count),
        out_specs=[memory] * 2,
        scratch_shapes=[pltpu.VMEM(value.shape, value.dtype) for value in arguments]
        + [pltpu.SemaphoreType.DMA((3 * count,))],
        cost_estimate=cost(7),
        compiler_params=pltpu.CompilerParams(vmem_limit_bytes=60 * 1024 * 1024),
        name="products",
    )(place, *arguments)


def pair_kernel(place, keep, received, *outs):
    for step in range(4):
        number = lax.rem(place[2] + step, 4)
        outs[step][...] = keep[number] + received[number]


def cross_kernel(query, place, *refs):
    count = 1 if query else 3
    momenta, gradients, refs = refs[:count], refs[count : 2 * count], refs[2 * count :]
    core = place[3]
    if query:
        products, refs = refs[0], refs[1:]
    else:
        same, other, products, refs = refs[:4], refs[4:8], refs[13], refs[8:13] + refs[14:]
        for index, step in enumerate(FOUR):
            number = lax.rem(place[2] + step, 4)
            products[number, aligned(128 * core, 128), :] = same[index][...]
            products[number, aligned(128 * (1 - core), 128), :] = other[index][...]
    (own, plus_first, minus_first, plus_second, minus_second, wide), refs = refs[:6], refs[6:]
    if query:
        buffer = momenta[0][...] + gradients[0][...].astype(jnp.float32)
        wide[...] = dot_three(buffer, products[0], ((0,), (0,)))
    else:
        narrow, gram = refs
        for number in range(3):
            buffer = momenta[number][...] + gradients[number][...].astype(jnp.float32)
            crossed = dot_three(buffer, products[1 + number], ((0,), (0,)))
            if number == 2:
                wide[...] = crossed
            else:
                narrow[number] = crossed
        left = products[place[2], :, aligned(128 * core, 128)]
        gram[...] = dot(left, products[place[2]], ((0,), (0,)))

    def put(out, start, step, upper):
        row = lax.rem(place[1] + step, 4)
        for deep in range(4 * upper, 4 * upper + 4):
            out[start : start + 32, :] = wide[aligned(256 * row + 32 * deep, 32), :]
            start = start + 32
            if not query:
                out[start : start + 8, :] = narrow[upper, aligned(32 * row + 8 * (deep % 4), 8), :]
                start = start + 8
        if not query:
            out[start : start + 16, :] = gram[aligned(32 * row + 16 * upper, 16), :]

    half = own.shape[0] // 2
    put(plus_first, 0, 2, 0)
    put(minus_first, 0, 2, 1)
    put(plus_first, half, 1, 1)
    put(minus_first, half, 3, 0)
    put(plus_second, 0, 1, 0)
    put(minus_second, 0, 3, 1)
    put(own, 0, 0, 0)
    put(own, half, 0, 1)


def pass_kernel(place, plus, minus, plus_in, minus_in, plus_out, minus_out):
    half = plus.shape[0]
    plus_out[...] = plus[...] + plus_in[:half, :]
    minus_out[...] = minus[...] + minus_in[:half, :]


def cross_call(query, place, operands):
    half = 128 if query else 176
    outs = [(2 * half, RANK)] * 3 + [(half, RANK)] * 2
    scratch = [(1024, RANK)]
    if not query:
        outs = outs + [(4, RANK, RANK)]
        scratch = scratch + [(2, 128, RANK), (128, RANK)]
    return call(
        functools.partial(cross_kernel, query),
        outs,
        (place, *operands),
        "crosses",
        scratch,
        2 if query else 3,
    )


def pass_call(place, plus, minus, plus_in, minus_in, micros=1):
    operands = (place, plus, minus, plus_in, minus_in)
    return call(pass_kernel, [plus.shape] * 2, operands, "passes", (), micros)


def row_kernel(place, *refs):
    (keep, near, far), total = refs[10:13], refs[13]
    for pieces, size, start in ((refs[:5], 32, 0), (refs[5:10], 40, 32)):
        own, plus_in, minus_in, plus, minus = pieces
        half = own.shape[0] // 2
        lower = own[:half, :] + minus_in[half:, :] + plus[...]
        upper = own[half:, :] + plus_in[half:, :] + minus[...]
        for deep in range(8):
            piece = (lower, upper)[deep // 4][size * (deep % 4) : size * (deep % 4) + size, :]
            total[72 * deep + start : 72 * deep + start + size, :] = piece
    total[576:592, :] = lower[160:, :]
    total[592:, :] = upper[160:, :]
    parity = lax.rem(place[0], 2)
    for block in range(4):
        rows = slice(72 * block, 72 * block + 72)
        keep[rows, :] = total[tall_rows(2 * block + parity), :]
        out = (near, far)[block // 2]
        rows = slice(72 * (block % 2), 72 * (block % 2) + 72)
        out[rows, :] = total[tall_rows(2 * block + 1 - parity), :]
    keep[288:, :] = total[576:, :]
    near[144:, :] = total[576:592, :]
    far[144:, :] = total[592:, :]


def tall_rows(block):
    return pl.ds(pl.multiple_of(72 * block, 8), 72)


def neighbour_kernel(place, keep, near, far, *refs):
    outs, total = refs[:4], refs[4]
    total[:144, :] = keep[:144, :] + near[:144, :]
    total[144:288, :] = keep[144:288, :] + far[:144, :]
    total[288:304, :] = keep[288:304, :] + near[144:, :]
    total[304:, :] = keep[304:, :] + far[144:, :]
    for step in range(4):
        block = lax.rem(place[0] // 2 + step, 4)
        outs[step][:72, :] = total[tall_rows(block), :]
        outs[step][72:, :] = total[aligned(288 + 8 * block, 8), :]


def deep_kernel(place, *refs):
    pieces, shard, terms = refs[:4], refs[4], refs[5]
    shard[:72, :] = pieces[0][:72, :] + pieces[1][:72, :] + pieces[2][:72, :] + pieces[3][:72, :]
    for index, step in enumerate(FOUR):
        source = lax.rem(place[0] + 8 - 2 * step, 8)
        pair = jnp.where(place[0] < 4, source // 2, lax.rem((source + 1) // 2, 4))
        terms[pair] = pieces[index][72:, :]
    shard[72:, :] = terms[0] + terms[1] + terms[2] + terms[3]


def quad_kernel(place, *refs):
    pieces, near, far, gram, total = refs[:4], refs[4], refs[5], refs[6], refs[7]
    for index, step in enumerate(TURNED):
        block = lax.rem(place[0] // 2 + step, 4)
        total[tall_rows(block), :] = pieces[index][:72, :]
        gram[aligned(8 * block, 8), :] = pieces[index][72:, :]
    near[...] = total[:144, :]
    far[...] = total[144:, :]


def join_kernel(place, *refs):
    same, other, total = refs[:2], refs[2:4], refs[4]
    parity = lax.rem(place[0], 2)
    for block in range(4):
        rows = slice(72 * (block % 2), 72 * (block % 2) + 72)
        total[tall_rows(2 * block + parity), :] = same[block // 2][rows, :]
        total[tall_rows(2 * block + 1 - parity), :] = other[block // 2][rows, :]


def forward_kernel(place, before, after, lower, upper):
    lower[...] = before[:288, :]
    upper[...] = after[288:, :]


def column_kernel(place, *refs):
    packed, same, other = refs[0], refs[1:4], refs[4:7]
    pieces, columns, squares, inverses = refs[7:12], refs[12:16], refs[16], refs[17]
    wide, narrow, joined = refs[18:]
    core = place[3]
    joined[0] = packed[...]
    for index, step in enumerate(TURNED[1:]):
        joined[step, aligned(96 * core, 8, 96), :] = same[index][...]
        joined[step, aligned(96 * (1 - core), 8, 96), :] = other[index][...]
    zero = jnp.zeros((128, 128), jnp.float32)
    for step in range(4):
        number = lax.rem(place[2] + step, 4)
        inverses[number, :64, :128] = joined[step, :64, :128]
        inverses[number, 64:128, :128] = joined[step, :64, 128:]
        inverses[number, :128, 128:] = zero
        inverses[number, 128:, :] = joined[step, 64:, :]
    for step in range(4):
        row = lax.rem(place[1] + step, 4)
        for deep in range(8):
            piece = pieces[(0, 1, 2 + deep // 4, 4)[step]]
            start = 72 * (deep % 4 if step == 2 else deep)
            rows = aligned(256 * row + 32 * deep, 32)
            wide[0, rows, :] = piece[start : start + 32, :]
            wide[1, rows, :] = piece[start + 32 : start + 64, :]
            rows = aligned(32 * row + 8 * (deep % 4), 8)
            narrow[deep // 4, rows, :] = piece[start + 64 : start + 72, :]
    for number in range(4):
        crossed = wide[number // 3] if number in (0, 3) else narrow[number - 1]
        column = dot_three(crossed, inverses[number])
        columns[number][...] = column
        squares[number : number + 1, :] = jnp.sum(column * column, axis=0, keepdims=True)


def momentum_kernel(place, *refs):
    momenta, gradients, columns, inverses, products = refs[:4], refs[4:8], refs[8:12], refs[12], refs[13]
    outs, orthos, held, sent = refs[14:18], refs[18], refs[19:23], refs[23]
    copies = [pltpu.make_async_copy(held[i], outs[i], sent.at[i]) for i in range(4)]
    for number in (0, 3, 1, 2):
        ortho = dot(products[number], inverses[number], ((1,), (1,)))
        orthos[number] = ortho
        buffer = momenta[number][...] + gradients[number][...].astype(jnp.float32)
        change = dot_three(ortho, columns[number][...])
        held[number][...] = buffer - (1.0 - MOMENTUM_DECAY) * change
        copies[number].start()
    for copy in copies:
        copy.wait()


def update_kernel(scales, place, *refs):
    squares, columns, orthos, outs = refs[0], refs[1:5], refs[5], refs[6:14]
    held, sent = refs[14:22], refs[22]
    copies = [pltpu.make_async_copy(held[i], outs[i], sent.at[i]) for i in range(8)]
    inverse = 1.0 / jnp.sqrt(squares[...] + EPSILON)
    for number in (0, 3, 1, 2):
        basis = columns[number][...] * inverse[number : number + 1, :]
        held[4 + number][...] = basis
        copies[4 + number].start()
        held[number][...] = scales[number] * dot_three(orthos[number], basis)
        copies[number].start()
    for copy in copies:
        copy.wait()


def result_call(body, shapes, operands, name, kept=()):
    return pl.pallas_call(
        body,
        out_shape=[jax.ShapeDtypeStruct(shape, jnp.float32) for shape in (*shapes, *kept)],
        in_specs=[pl.BlockSpec(memory_space=pltpu.SMEM)]
        + [pl.BlockSpec(memory_space=pltpu.VMEM)] * (len(operands) - 1),
        out_specs=[pl.BlockSpec(memory_space=pl.ANY)] * len(shapes)
        + [pl.BlockSpec(memory_space=pltpu.VMEM)] * len(kept),
        scratch_shapes=[pltpu.VMEM(shape, jnp.float32) for shape in shapes]
        + [pltpu.SemaphoreType.DMA((len(shapes),))],
        cost_estimate=cost(3),
        compiler_params=pltpu.CompilerParams(vmem_limit_bytes=24 * 1024 * 1024),
        name=name,
    )(*operands)


def local(*arguments):
    momenta = arguments[0::3]
    gradients = arguments[1::3]
    factors = arguments[2::3]
    height = momenta[0].shape[0]
    place = jnp.stack([lax.axis_index(axis) for axis in SIZES]).astype(jnp.int32)

    half = (128, RANK)
    send, keep = product_call(place, (*momenta, *gradients, *factors))
    received = shift_along(send, "core", 1)
    pieces = call(pair_kernel, [half] * 4, (place, keep, received), "pairs")
    shard = sum(reversed(from_three(pieces[1:], "x", -1)), pieces[0])
    same = [shard] + from_three([shard] * 3, "x", 1)
    other = [shift_along(piece, "core", 1) for piece in same]

    *others, products = cross_call(False, place, (*momenta[1:], *gradients[1:], *same, *other))
    query = cross_call(True, place, (momenta[0], gradients[0], products))
    others_in = shift_along(others[1], "y", -1), shift_along(others[2], "y", 1)
    query_in = shift_along(query[1], "y", -1), shift_along(query[2], "y", 1)
    plus, minus = pass_call(place, others[3], others[4], *others_in)
    query_in, plus, minus = lax.optimization_barrier((query_in, plus, minus))
    other_pieces = (others[0], *others_in, shift_along(plus, "y", -1), shift_along(minus, "y", 1))
    plus, minus = pass_call(place, query[3], query[4], *query_in, 20)
    query_pieces = (query[0], *query_in, shift_along(plus, "y", -1), shift_along(minus, "y", 1))

    keep, near, far = call(
        row_kernel,
        [(320, RANK), (160, RANK), (160, RANK)],
        (place, *query_pieces, *other_pieces),
        "rows",
        [(608, RANK)],
    )
    near, far = neighbours(near, far)
    pieces = call(
        neighbour_kernel, [(80, RANK)] * 4, (place, keep, near, far), "neighbours", [(320, RANK)]
    )
    pieces = [pieces[0]] + from_three(pieces[1:], "z", -2)
    (shard,) = call(deep_kernel, [(80, RANK)], (place, *pieces), "deeps", [(4, 8, RANK)])

    pieces = [shard] + from_three([shard] * 3, "z", 2)[::-1]
    near, far, gram = call(
        quad_kernel,
        [(144, RANK), (144, RANK), (32, RANK)],
        (place, *pieces),
        "quads",
        [(288, RANK)],
    )

    beside = shift_along(gram, "core", 1)
    first = place[3] == 0
    pair = jnp.concatenate([jnp.where(first, gram, beside), jnp.where(first, beside, gram)], axis=0)
    rows = [pair] + from_three([pair] * 3, "y", 1)[::-1]

    (joined,) = call(
        join_kernel, [(576, RANK)], (place, near, far, *neighbours(near, far)), "joins"
    )
    before = shift_along(joined, "y", -1)
    after = shift_along(joined, "y", 1)

    packed, mine = call(
        inverse_kernel,
        [(192, RANK), (96, RANK)],
        (place, *rows),
        "inverse",
        [(RANK, RANK), (RANK, RANK), (RANK, 2 * RANK)],
        11,
    )
    same = from_three([mine] * 3, "x", 1)[::-1]
    *same, before, after = lax.optimization_barrier((*same, before, after))
    operands = (place, before, after)
    lower, upper = call(forward_kernel, [(288, RANK)] * 2, operands, "forwards")
    lower = shift_along(lower, "y", -1)
    upper = shift_along(upper, "y", 1)
    other = [shift_along(piece, "core", 1) for piece in same]
    tall = [(momentum.shape[1], RANK) for momentum in momenta]
    flat = [momentum.shape for momentum in momenta]
    *columns, squares, inverses = call(
        column_kernel,
        tall + [(4, RANK), (4, RANK, RANK)],
        (place, packed, *same, *other, joined, after, lower, upper, before),
        "columns",
        [(2, 1024, RANK), (2, 128, RANK), (4, 192, RANK)],
        3,
    )
    squares = squares + sum(reversed(from_three([squares] * 3, "x", 1)))
    *new_momenta, orthos = result_call(
        momentum_kernel,
        flat,
        (place, *momenta, *gradients, *columns, inverses, products),
        "momenta",
        [(4, RANK, RANK)],
    )
    squares, orthos = lax.optimization_barrier((squares, orthos))
    squares = squares + shift_along(squares, "core", 1)
    scales = [math.sqrt(height * 32 * shape[1] * 8 / RANK) for shape in flat]
    outs = result_call(
        functools.partial(update_kernel, scales),
        flat + tall,
        (place, squares, *columns, orthos),
        "updates",
    )
    results = []
    for number in range(4):
        results = results + [outs[number], new_momenta[number], outs[4 + number]]
    return tuple(results)


def solution(mesh):
    devices = mesh.devices.reshape(tuple(SIZES.values()))
    finer = Mesh(devices, tuple(SIZES))
    wide = P(("z", "y"), ("x", "core"))
    tall = P(("x", "core"), None)
    return jax.shard_map(
        local,
        mesh=finer,
        in_specs=(wide, wide, tall) * 4,
        out_specs=(wide, wide, tall) * 4,
        check_vma=False,
    )
```

```python
import functools
import math

import jax
import jax.numpy as jnp
from jax import lax
from jax.experimental import pallas as pl
from jax.experimental.pallas import tpu as pltpu
from jax.sharding import Mesh
from jax.sharding import PartitionSpec as P

PRECISE = lax.Precision.HIGHEST
MOMENTUM_DECAY = 0.95
SHIFT_RATIO = 0.0001
EPSILON = 1e-06
RANK = 256
PANEL = 16
FOUR = (0, 2, 1, 3)
TURNED = (0, 3, 1, 2)
SIZES = {"z": 8, "y": 4, "x": 4, "core": 2}


def dot(left, right, dims):
    return lax.dot_general(
        left, right, (dims, ((), ())), precision=PRECISE, preferred_element_type=jnp.float32
    )


def dot_three(left, right, dims=((1,), (1,))):
    parts = []
    for values in (left, right):
        high = values.astype(jnp.bfloat16)
        parts.append((high, (values - high.astype(jnp.float32)).astype(jnp.bfloat16)))
    (left_high, left_low), (right_high, right_low) = parts

    def one(first, second):
        return lax.dot_general(
            first, second, (dims, ((), ())), preferred_element_type=jnp.float32
        )

    return one(left_low, right_high) + one(left_high, right_low) + one(left_high, right_high)


def split3(values):
    high = values.astype(jnp.bfloat16)
    rest = values - high.astype(jnp.float32)
    mid = rest.astype(jnp.bfloat16)
    low = (rest - mid.astype(jnp.float32)).astype(jnp.bfloat16)
    return high, mid, low


def inverse_kernel(place, *refs):
    pieces, (packed, mine, gram_ref, out_ref, work) = refs[:4], refs[4:]
    for step, piece in zip(TURNED, pieces):
        rows = 32 * lax.rem(place[1] + step, 4)
        gram_ref[pl.ds(pl.multiple_of(rows, 32), 32), :] = piece[:32, :]
        gram_ref[pl.ds(pl.multiple_of(rows + 128, 32), 32), :] = piece[32:, :]
    gram = gram_ref[...]
    rows = lax.broadcasted_iota(jnp.int32, (RANK, RANK), 0)
    cols = lax.broadcasted_iota(jnp.int32, (RANK, RANK), 1)
    unit = jnp.where(rows == cols, 1.0, 0.0).astype(jnp.float32)
    shift = SHIFT_RATIO * jnp.sum(gram * unit) / RANK
    work[:, :RANK] = gram + shift * unit
    work[:, RANK:] = unit
    sub = lax.broadcasted_iota(jnp.int32, (PANEL, 128), 0)
    for start in range(0, RANK, PANEL):
        here, end = start // 128, start + PANEL
        blocks = list(range(here, 3 + here))
        panel = {i: work[start:end, 128 * i : 128 * (i + 1)] for i in blocks}
        columns = [
            jnp.broadcast_to(panel[here][:, j : j + 1], (PANEL, 128))
            for j in range(start % 128, start % 128 + PANEL)
        ]
        scale = jnp.zeros((PANEL, 128), jnp.float32)
        for j in range(PANEL):
            root = lax.rsqrt(columns[j][j : j + 1, :])
            scale = jnp.where(sub == j, root, scale)
            mult = jnp.where(sub > j, columns[j] * (root * root), 0.0)
            for other in range(j + 1, PANEL):
                columns[other] = columns[other] - mult * columns[other][j : j + 1, :]
            if j < PANEL - 1:
                panel = {i: panel[i] - mult * panel[i][j : j + 1, :] for i in blocks}
        panel = {i: panel[i] * scale for i in blocks}
        for i in range(2, 4):
            out_ref[start:end, 128 * (i - 2) : 128 * (i - 1)] = panel.get(i, jnp.zeros_like(scale))
        first = end // 128
        if first == 2:
            break
        changed = [i for i in blocks if i >= first]
        left = jnp.concatenate([panel[i] for i in changed if i < 2], axis=1)
        lane = lax.broadcasted_iota(jnp.int32, left.shape, 1) + 128 * first
        left_high, left_mid, left_low = split3(jnp.where(lane >= end, left, 0.0))
        high, mid, low = split3(jnp.concatenate([panel[i] for i in changed], axis=1))
        lhs = jnp.concatenate([left_high, left_high, left_mid, left_high, left_low, left_mid], axis=0)
        rhs = jnp.concatenate([high, mid, high, low, high, mid], axis=0)
        change = lax.dot_general(
            lhs, rhs, (((0,), (0,)), ((), ())), preferred_element_type=jnp.float32
        )
        for place_in, i in enumerate(changed):
            work[end:, 128 * i : 128 * (i + 1)] -= change[
                end - 128 * first :, 128 * place_in : 128 * (place_in + 1)
            ]

    packed[:64, :128] = out_ref[:64, :128]
    packed[:64, 128:] = out_ref[64:128, :128]
    packed[64:, :] = out_ref[128:, :]
    mine[...] = packed[aligned(96 * place[3], 8, 96), :]


def shift_along(values, axis, step):
    size = SIZES[axis]
    return lax.ppermute(values, axis, [((i + step) % size, i) for i in range(size)])


def from_three(values, axis, step):
    return [shift_along(values[index - 1], axis, index * step) for index in FOUR[1:]]


def neighbours(near, far):
    pairs = [(i, i ^ 1) for i in range(8)]
    others = [(i, (i + 1) % 8 if i % 2 else (i + 7) % 8) for i in range(8)]
    return lax.ppermute(near, "z", pairs), lax.ppermute(far, "z", others)


def cost(micros):
    return pl.CostEstimate(flops=int(1.1e9 * micros), bytes_accessed=0, transcendentals=0)


def call(body, outs, operands, name, scratch=(), micros=1):
    memory = pl.BlockSpec(memory_space=pltpu.VMEM)
    return pl.pallas_call(
        body,
        out_shape=[jax.ShapeDtypeStruct(shape, jnp.float32) for shape in outs],
        in_specs=[pl.BlockSpec(memory_space=pltpu.SMEM)] + [memory] * (len(operands) - 1),
        out_specs=[memory] * len(outs),
        scratch_shapes=[pltpu.VMEM(shape, jnp.float32) for shape in scratch],
        cost_estimate=cost(micros),
        compiler_params=pltpu.CompilerParams(vmem_limit_bytes=24 * 1024 * 1024),
        name=name,
    )(*operands)


def aligned(start, multiple, size=None):
    return pl.ds(pl.multiple_of(start, multiple), size or multiple)


def product_kernel(count, place, *refs):
    order = (1, 2, 0, 3)
    send, keep = refs[3 * count : 3 * count + 2]
    held, arrived = refs[3 * count + 2 : -1], refs[-1]
    copies = [
        pltpu.make_async_copy(refs[index], held[index], arrived.at[index])
        for index in range(3 * count)
    ]
    for number in order:
        for index in (2 * count + number, number, count + number):
            copies[index].start()
    first = place[3] == 0
    for number in order:
        for index in (2 * count + number, number, count + number):
            copies[index].wait()
        buffer = held[number][...] + held[count + number][...].astype(jnp.float32)
        product = dot(buffer, held[2 * count + number][...], ((1,), (0,)))
        keep[number] = jnp.where(first, product[:128], product[128:])
        send[number] = jnp.where(first, product[128:], product[:128])


def product_call(place, arguments):
    memory = pl.BlockSpec(memory_space=pltpu.VMEM)
    count = len(arguments) // 3
    return pl.pallas_call(
        functools.partial(product_kernel, count),
        out_shape=[jax.ShapeDtypeStruct((count, 128, RANK), jnp.float32)] * 2,
        in_specs=[pl.BlockSpec(memory_space=pltpu.SMEM)]
        + [pl.BlockSpec(memory_space=pl.ANY)] * (3 * count),
        out_specs=[memory] * 2,
        scratch_shapes=[pltpu.VMEM(value.shape, value.dtype) for value in arguments]
        + [pltpu.SemaphoreType.DMA((3 * count,))],
        cost_estimate=cost(7),
        compiler_params=pltpu.CompilerParams(vmem_limit_bytes=60 * 1024 * 1024),
        name="products",
    )(place, *arguments)


def pair_kernel(place, keep, received, *outs):
    for step in range(4):
        number = lax.rem(place[2] + step, 4)
        outs[step][...] = keep[number] + received[number]


def cross_kernel(query, place, *refs):
    count = 1 if query else 3
    momenta, gradients, refs = refs[:count], refs[count : 2 * count], refs[2 * count :]
    core = place[3]
    if query:
        products, refs = refs[0], refs[1:]
    else:
        same, other, products, refs = refs[:4], refs[4:8], refs[13], refs[8:13] + refs[14:]
        for index, step in enumerate(FOUR):
            number = lax.rem(place[2] + step, 4)
            products[number, aligned(128 * core, 128), :] = same[index][...]
            products[number, aligned(128 * (1 - core), 128), :] = other[index][...]
    (own, plus_first, minus_first, plus_second, minus_second, wide), refs = refs[:6], refs[6:]
    if query:
        buffer = momenta[0][...] + gradients[0][...].astype(jnp.float32)
        wide[...] = dot_three(buffer, products[0], ((0,), (0,)))
    else:
        narrow, gram = refs
        for number in range(3):
            buffer = momenta[number][...] + gradients[number][...].astype(jnp.float32)
            crossed = dot_three(buffer, products[1 + number], ((0,), (0,)))
            if number == 2:
                wide[...] = crossed
            else:
                narrow[number] = crossed
        left = products[place[2], :, aligned(128 * core, 128)]
        gram[...] = dot(left, products[place[2]], ((0,), (0,)))

    def put(out, start, step, upper):
        row = lax.rem(place[1] + step, 4)
        for deep in range(4 * upper, 4 * upper + 4):
            out[start : start + 32, :] = wide[aligned(256 * row + 32 * deep, 32), :]
            start = start + 32
            if not query:
                out[start : start + 8, :] = narrow[upper, aligned(32 * row + 8 * (deep % 4), 8), :]
                start = start + 8
        if not query:
            out[start : start + 16, :] = gram[aligned(32 * row + 16 * upper, 16), :]

    half = own.shape[0] // 2
    put(plus_first, 0, 2, 0)
    put(minus_first, 0, 2, 1)
    put(plus_first, half, 1, 1)
    put(minus_first, half, 3, 0)
    put(plus_second, 0, 1, 0)
    put(minus_second, 0, 3, 1)
    put(own, 0, 0, 0)
    put(own, half, 0, 1)


def pass_kernel(place, plus, minus, plus_in, minus_in, plus_out, minus_out):
    half = plus.shape[0]
    plus_out[...] = plus[...] + plus_in[:half, :]
    minus_out[...] = minus[...] + minus_in[:half, :]


def cross_call(query, place, operands):
    half = 128 if query else 176
    outs = [(2 * half, RANK)] * 3 + [(half, RANK)] * 2
    scratch = [(1024, RANK)]
    if not query:
        outs = outs + [(4, RANK, RANK)]
        scratch = scratch + [(2, 128, RANK), (128, RANK)]
    return call(
        functools.partial(cross_kernel, query),
        outs,
        (place, *operands),
        "crosses",
        scratch,
        2 if query else 3,
    )


def pass_call(place, plus, minus, plus_in, minus_in, micros=1):
    operands = (place, plus, minus, plus_in, minus_in)
    return call(pass_kernel, [plus.shape] * 2, operands, "passes", (), micros)


def row_kernel(place, *refs):
    (keep, near, far), total = refs[10:13], refs[13]
    for pieces, size, start in ((refs[:5], 32, 0), (refs[5:10], 40, 32)):
        own, plus_in, minus_in, plus, minus = pieces
        half = own.shape[0] // 2
        lower = own[:half, :] + minus_in[half:, :] + plus[...]
        upper = own[half:, :] + plus_in[half:, :] + minus[...]
        for deep in range(8):
            piece = (lower, upper)[deep // 4][size * (deep % 4) : size * (deep % 4) + size, :]
            total[72 * deep + start : 72 * deep + start + size, :] = piece
    total[576:592, :] = lower[160:, :]
    total[592:, :] = upper[160:, :]
    parity = lax.rem(place[0], 2)
    for block in range(4):
        rows = slice(72 * block, 72 * block + 72)
        keep[rows, :] = total[tall_rows(2 * block + parity), :]
        out = (near, far)[block // 2]
        rows = slice(72 * (block % 2), 72 * (block % 2) + 72)
        out[rows, :] = total[tall_rows(2 * block + 1 - parity), :]
    keep[288:, :] = total[576:, :]
    near[144:, :] = total[576:592, :]
    far[144:, :] = total[592:, :]


def tall_rows(block):
    return pl.ds(pl.multiple_of(72 * block, 8), 72)


def neighbour_kernel(place, keep, near, far, *refs):
    outs, total = refs[:4], refs[4]
    total[:144, :] = keep[:144, :] + near[:144, :]
    total[144:288, :] = keep[144:288, :] + far[:144, :]
    total[288:304, :] = keep[288:304, :] + near[144:, :]
    total[304:, :] = keep[304:, :] + far[144:, :]
    for step in range(4):
        block = lax.rem(place[0] // 2 + step, 4)
        outs[step][:72, :] = total[tall_rows(block), :]
        outs[step][72:, :] = total[288:, :]


def deep_kernel(place, *refs):
    pieces, shard, gram, terms = refs[:4], refs[4], refs[5], refs[6]
    shard[...] = (
        pieces[0][:72, :] + pieces[1][:72, :] + pieces[2][:72, :] + pieces[3][:72, :]
    )
    for index, step in enumerate(FOUR):
        source = lax.rem(place[0] + 8 - 2 * step, 8)
        terms[source // 2, :16, :] = pieces[index][72:88, :]
        terms[lax.rem((source + 1) // 2, 4), 16:, :] = pieces[index][88:, :]
    gram[...] = terms[0] + terms[1] + terms[2] + terms[3]


def quad_kernel(place, *refs):
    pieces, near, far, total = refs[:4], refs[4], refs[5], refs[6]
    for index, step in enumerate(TURNED):
        total[tall_rows(lax.rem(place[0] // 2 + step, 4)), :] = pieces[index][...]
    near[...] = total[:144, :]
    far[...] = total[144:, :]


def join_kernel(place, *refs):
    same, other, total = refs[:2], refs[2:4], refs[4]
    parity = lax.rem(place[0], 2)
    for block in range(4):
        rows = slice(72 * (block % 2), 72 * (block % 2) + 72)
        total[tall_rows(2 * block + parity), :] = same[block // 2][rows, :]
        total[tall_rows(2 * block + 1 - parity), :] = other[block // 2][rows, :]


def forward_kernel(place, before, after, lower, upper):
    lower[...] = before[:288, :]
    upper[...] = after[288:, :]


def column_kernel(place, *refs):
    packed, same, other = refs[0], refs[1:4], refs[4:7]
    pieces, columns, squares, inverses = refs[7:12], refs[12:16], refs[16], refs[17]
    wide, narrow, joined = refs[18:]
    core = place[3]
    joined[0] = packed[...]
    for index, step in enumerate(TURNED[1:]):
        joined[step, aligned(96 * core, 8, 96), :] = same[index][...]
        joined[step, aligned(96 * (1 - core), 8, 96), :] = other[index][...]
    zero = jnp.zeros((128, 128), jnp.float32)
    for step in range(4):
        number = lax.rem(place[2] + step, 4)
        inverses[number, :64, :128] = joined[step, :64, :128]
        inverses[number, 64:128, :128] = joined[step, :64, 128:]
        inverses[number, :128, 128:] = zero
        inverses[number, 128:, :] = joined[step, 64:, :]
    for step in range(4):
        row = lax.rem(place[1] + step, 4)
        for deep in range(8):
            piece = pieces[(0, 1, 2 + deep // 4, 4)[step]]
            start = 72 * (deep % 4 if step == 2 else deep)
            rows = aligned(256 * row + 32 * deep, 32)
            wide[0, rows, :] = piece[start : start + 32, :]
            wide[1, rows, :] = piece[start + 32 : start + 64, :]
            rows = aligned(32 * row + 8 * (deep % 4), 8)
            narrow[deep // 4, rows, :] = piece[start + 64 : start + 72, :]
    for number in range(4):
        crossed = wide[number // 3] if number in (0, 3) else narrow[number - 1]
        column = dot_three(crossed, inverses[number])
        columns[number][...] = column
        squares[number : number + 1, :] = jnp.sum(column * column, axis=0, keepdims=True)


def momentum_kernel(place, *refs):
    momenta, gradients, columns, inverses, products = refs[:4], refs[4:8], refs[8:12], refs[12], refs[13]
    outs, orthos, held, sent = refs[14:18], refs[18], refs[19:23], refs[23]
    copies = [pltpu.make_async_copy(held[i], outs[i], sent.at[i]) for i in range(4)]
    for number in (0, 3, 1, 2):
        ortho = dot(products[number], inverses[number], ((1,), (1,)))
        orthos[number] = ortho
        buffer = momenta[number][...] + gradients[number][...].astype(jnp.float32)
        change = dot_three(ortho, columns[number][...])
        held[number][...] = buffer - (1.0 - MOMENTUM_DECAY) * change
        copies[number].start()
    for copy in copies:
        copy.wait()


def update_kernel(scales, place, *refs):
    squares, columns, orthos, outs = refs[0], refs[1:5], refs[5], refs[6:14]
    held, sent = refs[14:22], refs[22]
    copies = [pltpu.make_async_copy(held[i], outs[i], sent.at[i]) for i in range(8)]
    inverse = 1.0 / jnp.sqrt(squares[...] + EPSILON)
    for number in (0, 3, 1, 2):
        basis = columns[number][...] * inverse[number : number + 1, :]
        held[4 + number][...] = basis
        copies[4 + number].start()
        held[number][...] = scales[number] * dot_three(orthos[number], basis)
        copies[number].start()
    for copy in copies:
        copy.wait()


def result_call(body, shapes, operands, name, kept=()):
    return pl.pallas_call(
        body,
        out_shape=[jax.ShapeDtypeStruct(shape, jnp.float32) for shape in (*shapes, *kept)],
        in_specs=[pl.BlockSpec(memory_space=pltpu.SMEM)]
        + [pl.BlockSpec(memory_space=pltpu.VMEM)] * (len(operands) - 1),
        out_specs=[pl.BlockSpec(memory_space=pl.ANY)] * len(shapes)
        + [pl.BlockSpec(memory_space=pltpu.VMEM)] * len(kept),
        scratch_shapes=[pltpu.VMEM(shape, jnp.float32) for shape in shapes]
        + [pltpu.SemaphoreType.DMA((len(shapes),))],
        cost_estimate=cost(3),
        compiler_params=pltpu.CompilerParams(vmem_limit_bytes=24 * 1024 * 1024),
        name=name,
    )(*operands)


def local(*arguments):
    momenta = arguments[0::3]
    gradients = arguments[1::3]
    factors = arguments[2::3]
    height = momenta[0].shape[0]
    place = jnp.stack([lax.axis_index(axis) for axis in SIZES]).astype(jnp.int32)

    half = (128, RANK)
    send, keep = product_call(place, (*momenta, *gradients, *factors))
    received = shift_along(send, "core", 1)
    pieces = call(pair_kernel, [half] * 4, (place, keep, received), "pairs")
    shard = sum(reversed(from_three(pieces[1:], "x", -1)), pieces[0])
    same = [shard] + from_three([shard] * 3, "x", 1)
    other = [shift_along(piece, "core", 1) for piece in same]

    *others, products = cross_call(False, place, (*momenta[1:], *gradients[1:], *same, *other))
    query = cross_call(True, place, (momenta[0], gradients[0], products))
    others_in = shift_along(others[1], "y", -1), shift_along(others[2], "y", 1)
    query_in = shift_along(query[1], "y", -1), shift_along(query[2], "y", 1)
    plus, minus = pass_call(place, others[3], others[4], *others_in)
    query_in, plus, minus = lax.optimization_barrier((query_in, plus, minus))
    other_pieces = (others[0], *others_in, shift_along(plus, "y", -1), shift_along(minus, "y", 1))
    plus, minus = pass_call(place, query[3], query[4], *query_in, 20)
    query_pieces = (query[0], *query_in, shift_along(plus, "y", -1), shift_along(minus, "y", 1))

    keep, near, far = call(
        row_kernel,
        [(320, RANK), (160, RANK), (160, RANK)],
        (place, *query_pieces, *other_pieces),
        "rows",
        [(608, RANK)],
    )
    near, far = neighbours(near, far)
    pieces = call(
        neighbour_kernel, [(104, RANK)] * 4, (place, keep, near, far), "neighbours", [(320, RANK)]
    )
    pieces = [pieces[0]] + from_three(pieces[1:], "z", -2)
    shard, gram = call(
        deep_kernel, [(72, RANK), (32, RANK)], (place, *pieces), "deeps", [(4, 32, RANK)]
    )

    beside = shift_along(gram, "core", 1)
    first = place[3] == 0
    pair = jnp.concatenate([jnp.where(first, gram, beside), jnp.where(first, beside, gram)], axis=0)
    rows = [pair] + from_three([pair] * 3, "y", 1)[::-1]

    pieces = [shard] + from_three([shard] * 3, "z", 2)[::-1]
    near, far = call(quad_kernel, [(144, RANK)] * 2, (place, *pieces), "quads", [(288, RANK)])
    (joined,) = call(
        join_kernel, [(576, RANK)], (place, near, far, *neighbours(near, far)), "joins"
    )
    before = shift_along(joined, "y", -1)
    after = shift_along(joined, "y", 1)

    packed, mine = call(
        inverse_kernel,
        [(192, RANK), (96, RANK)],
        (place, *rows),
        "inverse",
        [(RANK, RANK), (RANK, RANK), (RANK, 2 * RANK)],
        11,
    )
    same = from_three([mine] * 3, "x", 1)[::-1]
    same[1], before, after = lax.optimization_barrier((same[1], before, after))
    operands = (place, before, after)
    lower, upper = call(forward_kernel, [(288, RANK)] * 2, operands, "forwards")
    lower = shift_along(lower, "y", -1)
    upper = shift_along(upper, "y", 1)
    other = [shift_along(piece, "core", 1) for piece in same]
    tall = [(momentum.shape[1], RANK) for momentum in momenta]
    flat = [momentum.shape for momentum in momenta]
    *columns, squares, inverses = call(
        column_kernel,
        tall + [(4, RANK), (4, RANK, RANK)],
        (place, packed, *same, *other, joined, after, lower, upper, before),
        "columns",
        [(2, 1024, RANK), (2, 128, RANK), (4, 192, RANK)],
        3,
    )
    squares = squares + shift_along(squares, "core", 1)
    squares = squares + sum(reversed(from_three([squares] * 3, "x", 1)))
    *new_momenta, orthos = result_call(
        momentum_kernel,
        flat,
        (place, *momenta, *gradients, *columns, inverses, products),
        "momenta",
        [(4, RANK, RANK)],
    )
    scales = [math.sqrt(height * 32 * shape[1] * 8 / RANK) for shape in flat]
    outs = result_call(
        functools.partial(update_kernel, scales),
        flat + tall,
        (place, squares, *columns, orthos),
        "updates",
    )
    results = []
    for number in range(4):
        results = results + [outs[number], new_momenta[number], outs[4 + number]]
    return tuple(results)


def solution(mesh):
    devices = mesh.devices.reshape(tuple(SIZES.values()))
    finer = Mesh(devices, tuple(SIZES))
    wide = P(("z", "y"), ("x", "core"))
    tall = P(("x", "core"), None)
    return jax.shard_map(
        local,
        mesh=finer,
        in_specs=(wide, wide, tall) * 4,
        out_specs=(wide, wide, tall) * 4,
        check_vma=False,
    )
```

```python
import functools
import math

import jax
import jax.numpy as jnp
from jax import lax
from jax.experimental import pallas as pl
from jax.experimental.pallas import tpu as pltpu
from jax.sharding import Mesh
from jax.sharding import PartitionSpec as P

PRECISE = lax.Precision.HIGHEST
MOMENTUM_DECAY = 0.95
SHIFT_RATIO = 0.0001
EPSILON = 1e-06
RANK = 256
PANEL = 16
FOUR = (0, 2, 1, 3)
TURNED = (0, 3, 1, 2)
SIZES = {"z": 8, "y": 4, "x": 4, "core": 2}


def dot(left, right, dims):
    return lax.dot_general(
        left, right, (dims, ((), ())), precision=PRECISE, preferred_element_type=jnp.float32
    )


def dot_three(left, right, dims=((1,), (1,))):
    parts = []
    for values in (left, right):
        high = values.astype(jnp.bfloat16)
        parts.append((high, (values - high.astype(jnp.float32)).astype(jnp.bfloat16)))
    (left_high, left_low), (right_high, right_low) = parts

    def one(first, second):
        return lax.dot_general(
            first, second, (dims, ((), ())), preferred_element_type=jnp.float32
        )

    return one(left_low, right_high) + one(left_high, right_low) + one(left_high, right_high)


def split3(values):
    high = values.astype(jnp.bfloat16)
    rest = values - high.astype(jnp.float32)
    mid = rest.astype(jnp.bfloat16)
    low = (rest - mid.astype(jnp.float32)).astype(jnp.bfloat16)
    return high, mid, low


def inverse_kernel(place, *refs):
    pieces, (packed, mine, gram_ref, out_ref, work) = refs[:4], refs[4:]
    for step, piece in zip(TURNED, pieces):
        rows = 32 * lax.rem(place[1] + step, 4)
        gram_ref[pl.ds(pl.multiple_of(rows, 32), 32), :] = piece[:32, :]
        gram_ref[pl.ds(pl.multiple_of(rows + 128, 32), 32), :] = piece[32:, :]
    gram = gram_ref[...]
    rows = lax.broadcasted_iota(jnp.int32, (RANK, RANK), 0)
    cols = lax.broadcasted_iota(jnp.int32, (RANK, RANK), 1)
    unit = jnp.where(rows == cols, 1.0, 0.0).astype(jnp.float32)
    shift = SHIFT_RATIO * jnp.sum(gram * unit) / RANK
    work[:, :RANK] = gram + shift * unit
    work[:, RANK:] = unit
    sub = lax.broadcasted_iota(jnp.int32, (PANEL, 128), 0)
    for start in range(0, RANK, PANEL):
        here, end = start // 128, start + PANEL
        blocks = list(range(here, 3 + here))
        panel = {i: work[start:end, 128 * i : 128 * (i + 1)] for i in blocks}
        columns = [
            jnp.broadcast_to(panel[here][:, j : j + 1], (PANEL, 128))
            for j in range(start % 128, start % 128 + PANEL)
        ]
        scale = jnp.zeros((PANEL, 128), jnp.float32)
        for j in range(PANEL):
            root = lax.rsqrt(columns[j][j : j + 1, :])
            scale = jnp.where(sub == j, root, scale)
            mult = jnp.where(sub > j, columns[j] * (root * root), 0.0)
            for other in range(j + 1, PANEL):
                columns[other] = columns[other] - mult * columns[other][j : j + 1, :]
            if j < PANEL - 1:
                panel = {i: panel[i] - mult * panel[i][j : j + 1, :] for i in blocks}
        panel = {i: panel[i] * scale for i in blocks}
        for i in range(2, 4):
            out_ref[start:end, 128 * (i - 2) : 128 * (i - 1)] = panel.get(i, jnp.zeros_like(scale))
        first = end // 128
        if first == 2:
            break
        changed = [i for i in blocks if i >= first]
        left = jnp.concatenate([panel[i] for i in changed if i < 2], axis=1)
        lane = lax.broadcasted_iota(jnp.int32, left.shape, 1) + 128 * first
        left_high, left_mid, left_low = split3(jnp.where(lane >= end, left, 0.0))
        high, mid, low = split3(jnp.concatenate([panel[i] for i in changed], axis=1))
        lhs = jnp.concatenate([left_high, left_high, left_mid, left_high, left_low, left_mid], axis=0)
        rhs = jnp.concatenate([high, mid, high, low, high, mid], axis=0)
        change = lax.dot_general(
            lhs, rhs, (((0,), (0,)), ((), ())), preferred_element_type=jnp.float32
        )
        for place_in, i in enumerate(changed):
            work[end:, 128 * i : 128 * (i + 1)] -= change[
                end - 128 * first :, 128 * place_in : 128 * (place_in + 1)
            ]

    packed[:64, :128] = out_ref[:64, :128]
    packed[:64, 128:] = out_ref[64:128, :128]
    packed[64:, :] = out_ref[128:, :]
    mine[...] = packed[aligned(96 * place[3], 8, 96), :]


def shift_along(values, axis, step):
    size = SIZES[axis]
    return lax.ppermute(values, axis, [((i + step) % size, i) for i in range(size)])


def from_three(values, axis, step):
    return [shift_along(values[index - 1], axis, index * step) for index in FOUR[1:]]


def neighbours(near, far):
    pairs = [(i, i ^ 1) for i in range(8)]
    others = [(i, (i + 1) % 8 if i % 2 else (i + 7) % 8) for i in range(8)]
    return lax.ppermute(near, "z", pairs), lax.ppermute(far, "z", others)


def cost(micros):
    return pl.CostEstimate(flops=int(1.1e9 * micros), bytes_accessed=0, transcendentals=0)


def call(body, outs, operands, name, scratch=(), micros=1):
    memory = pl.BlockSpec(memory_space=pltpu.VMEM)
    return pl.pallas_call(
        body,
        out_shape=[jax.ShapeDtypeStruct(shape, jnp.float32) for shape in outs],
        in_specs=[pl.BlockSpec(memory_space=pltpu.SMEM)] + [memory] * (len(operands) - 1),
        out_specs=[memory] * len(outs),
        scratch_shapes=[pltpu.VMEM(shape, jnp.float32) for shape in scratch],
        cost_estimate=cost(micros),
        compiler_params=pltpu.CompilerParams(vmem_limit_bytes=24 * 1024 * 1024),
        name=name,
    )(*operands)


def aligned(start, multiple, size=None):
    return pl.ds(pl.multiple_of(start, multiple), size or multiple)


def product_kernel(count, place, *refs):
    order = (1, 2, 0, 3)
    send, keep = refs[3 * count : 3 * count + 2]
    held, arrived = refs[3 * count + 2 : -1], refs[-1]
    copies = [
        pltpu.make_async_copy(refs[index], held[index], arrived.at[index])
        for index in range(3 * count)
    ]
    for number in order:
        for index in (2 * count + number, number, count + number):
            copies[index].start()
    first = place[3] == 0
    for number in order:
        for index in (2 * count + number, number, count + number):
            copies[index].wait()
        buffer = held[number][...] + held[count + number][...].astype(jnp.float32)
        product = dot_three(buffer, held[2 * count + number][...], ((1,), (0,)))
        keep[number] = jnp.where(first, product[:128], product[128:])
        send[number] = jnp.where(first, product[128:], product[:128])


def product_call(place, arguments):
    memory = pl.BlockSpec(memory_space=pltpu.VMEM)
    count = len(arguments) // 3
    return pl.pallas_call(
        functools.partial(product_kernel, count),
        out_shape=[jax.ShapeDtypeStruct((count, 128, RANK), jnp.float32)] * 2,
        in_specs=[pl.BlockSpec(memory_space=pltpu.SMEM)]
        + [pl.BlockSpec(memory_space=pl.ANY)] * (3 * count),
        out_specs=[memory] * 2,
        scratch_shapes=[pltpu.VMEM(value.shape, value.dtype) for value in arguments]
        + [pltpu.SemaphoreType.DMA((3 * count,))],
        cost_estimate=cost(7),
        compiler_params=pltpu.CompilerParams(vmem_limit_bytes=60 * 1024 * 1024),
        name="products",
    )(place, *arguments)


def pair_kernel(place, keep, received, *outs):
    for step in range(4):
        number = lax.rem(place[2] + step, 4)
        outs[step][...] = keep[number] + received[number]


def cross_kernel(query, place, *refs):
    count = 1 if query else 3
    momenta, gradients, refs = refs[:count], refs[count : 2 * count], refs[2 * count :]
    core = place[3]
    if query:
        products, refs = refs[0], refs[1:]
    else:
        same, other, products, refs = refs[:4], refs[4:8], refs[13], refs[8:13] + refs[14:]
        for index, step in enumerate(FOUR):
            number = lax.rem(place[2] + step, 4)
            products[number, aligned(128 * core, 128), :] = same[index][...]
            products[number, aligned(128 * (1 - core), 128), :] = other[index][...]
    (own, plus_first, minus_first, plus_second, minus_second, wide), refs = refs[:6], refs[6:]
    if query:
        buffer = momenta[0][...] + gradients[0][...].astype(jnp.float32)
        wide[...] = dot_three(buffer, products[0], ((0,), (0,)))
    else:
        narrow, gram = refs
        for number in range(3):
            buffer = momenta[number][...] + gradients[number][...].astype(jnp.float32)
            crossed = dot_three(buffer, products[1 + number], ((0,), (0,)))
            if number == 2:
                wide[...] = crossed
            else:
                narrow[number] = crossed
        left = products[place[2], :, aligned(128 * core, 128)]
        gram[...] = dot(left, products[place[2]], ((0,), (0,)))

    def put(out, start, step, upper):
        row = lax.rem(place[1] + step, 4)
        for deep in range(4 * upper, 4 * upper + 4):
            out[start : start + 32, :] = wide[aligned(256 * row + 32 * deep, 32), :]
            start = start + 32
            if not query:
                out[start : start + 8, :] = narrow[upper, aligned(32 * row + 8 * (deep % 4), 8), :]
                start = start + 8
        if not query:
            out[start : start + 16, :] = gram[aligned(32 * row + 16 * upper, 16), :]

    half = own.shape[0] // 2
    put(plus_first, 0, 2, 0)
    put(minus_first, 0, 2, 1)
    put(plus_first, half, 1, 1)
    put(minus_first, half, 3, 0)
    put(plus_second, 0, 1, 0)
    put(minus_second, 0, 3, 1)
    put(own, 0, 0, 0)
    put(own, half, 0, 1)


def pass_kernel(place, plus, minus, plus_in, minus_in, plus_out, minus_out):
    half = plus.shape[0]
    plus_out[...] = plus[...] + plus_in[:half, :]
    minus_out[...] = minus[...] + minus_in[:half, :]


def cross_call(query, place, operands):
    half = 128 if query else 176
    outs = [(2 * half, RANK)] * 3 + [(half, RANK)] * 2
    scratch = [(1024, RANK)]
    if not query:
        outs = outs + [(4, RANK, RANK)]
        scratch = scratch + [(2, 128, RANK), (128, RANK)]
    return call(
        functools.partial(cross_kernel, query),
        outs,
        (place, *operands),
        "crosses",
        scratch,
        2 if query else 3,
    )


def pass_call(place, plus, minus, plus_in, minus_in, micros=1):
    operands = (place, plus, minus, plus_in, minus_in)
    return call(pass_kernel, [plus.shape] * 2, operands, "passes", (), micros)


def row_kernel(place, *refs):
    (keep, near, far), total = refs[10:13], refs[13]
    for pieces, size, start in ((refs[:5], 32, 0), (refs[5:10], 40, 32)):
        own, plus_in, minus_in, plus, minus = pieces
        half = own.shape[0] // 2
        lower = own[:half, :] + minus_in[half:, :] + plus[...]
        upper = own[half:, :] + plus_in[half:, :] + minus[...]
        for deep in range(8):
            piece = (lower, upper)[deep // 4][size * (deep % 4) : size * (deep % 4) + size, :]
            total[72 * deep + start : 72 * deep + start + size, :] = piece
    total[576:592, :] = lower[160:, :]
    total[592:, :] = upper[160:, :]
    parity = lax.rem(place[0], 2)
    for block in range(4):
        rows = slice(72 * block, 72 * block + 72)
        keep[rows, :] = total[tall_rows(2 * block + parity), :]
        out = (near, far)[block // 2]
        rows = slice(72 * (block % 2), 72 * (block % 2) + 72)
        out[rows, :] = total[tall_rows(2 * block + 1 - parity), :]
    keep[288:, :] = total[576:, :]
    near[144:, :] = total[576:592, :]
    far[144:, :] = total[592:, :]


def tall_rows(block):
    return pl.ds(pl.multiple_of(72 * block, 8), 72)


def neighbour_kernel(place, keep, near, far, *refs):
    outs, total = refs[:4], refs[4]
    total[:144, :] = keep[:144, :] + near[:144, :]
    total[144:288, :] = keep[144:288, :] + far[:144, :]
    total[288:304, :] = keep[288:304, :] + near[144:, :]
    total[304:, :] = keep[304:, :] + far[144:, :]
    for step in range(4):
        block = lax.rem(place[0] // 2 + step, 4)
        outs[step][:72, :] = total[tall_rows(block), :]
        outs[step][72:, :] = total[288:, :]


def deep_kernel(place, *refs):
    pieces, shard, gram, terms = refs[:4], refs[4], refs[5], refs[6]
    shard[...] = (
        pieces[0][:72, :] + pieces[1][:72, :] + pieces[2][:72, :] + pieces[3][:72, :]
    )
    for index, step in enumerate(FOUR):
        source = lax.rem(place[0] + 8 - 2 * step, 8)
        terms[source // 2, :16, :] = pieces[index][72:88, :]
        terms[lax.rem((source + 1) // 2, 4), 16:, :] = pieces[index][88:, :]
    gram[...] = terms[0] + terms[1] + terms[2] + terms[3]


def quad_kernel(place, *refs):
    pieces, near, far, total = refs[:4], refs[4], refs[5], refs[6]
    for index, step in enumerate(TURNED):
        total[tall_rows(lax.rem(place[0] // 2 + step, 4)), :] = pieces[index][...]
    near[...] = total[:144, :]
    far[...] = total[144:, :]


def join_kernel(place, *refs):
    same, other, total = refs[:2], refs[2:4], refs[4]
    parity = lax.rem(place[0], 2)
    for block in range(4):
        rows = slice(72 * (block % 2), 72 * (block % 2) + 72)
        total[tall_rows(2 * block + parity), :] = same[block // 2][rows, :]
        total[tall_rows(2 * block + 1 - parity), :] = other[block // 2][rows, :]


def forward_kernel(place, before, after, lower, upper):
    lower[...] = before[:288, :]
    upper[...] = after[288:, :]


def column_kernel(place, *refs):
    packed, same, other = refs[0], refs[1:4], refs[4:7]
    pieces, columns, squares, inverses = refs[7:12], refs[12:16], refs[16], refs[17]
    wide, narrow, joined = refs[18:]
    core = place[3]
    joined[0] = packed[...]
    for index, step in enumerate(TURNED[1:]):
        joined[step, aligned(96 * core, 8, 96), :] = same[index][...]
        joined[step, aligned(96 * (1 - core), 8, 96), :] = other[index][...]
    zero = jnp.zeros((128, 128), jnp.float32)
    for step in range(4):
        number = lax.rem(place[2] + step, 4)
        inverses[number, :64, :128] = joined[step, :64, :128]
        inverses[number, 64:128, :128] = joined[step, :64, 128:]
        inverses[number, :128, 128:] = zero
        inverses[number, 128:, :] = joined[step, 64:, :]
    for step in range(4):
        row = lax.rem(place[1] + step, 4)
        for deep in range(8):
            piece = pieces[(0, 1, 2 + deep // 4, 4)[step]]
            start = 72 * (deep % 4 if step == 2 else deep)
            rows = aligned(256 * row + 32 * deep, 32)
            wide[0, rows, :] = piece[start : start + 32, :]
            wide[1, rows, :] = piece[start + 32 : start + 64, :]
            rows = aligned(32 * row + 8 * (deep % 4), 8)
            narrow[deep // 4, rows, :] = piece[start + 64 : start + 72, :]
    for number in range(4):
        crossed = wide[number // 3] if number in (0, 3) else narrow[number - 1]
        column = dot_three(crossed, inverses[number])
        columns[number][...] = column
        squares[number : number + 1, :] = jnp.sum(column * column, axis=0, keepdims=True)


def momentum_kernel(place, *refs):
    momenta, gradients, columns, inverses, products = refs[:4], refs[4:8], refs[8:12], refs[12], refs[13]
    outs, orthos, held, sent = refs[14:18], refs[18], refs[19:23], refs[23]
    copies = [pltpu.make_async_copy(held[i], outs[i], sent.at[i]) for i in range(4)]
    for number in (0, 3, 1, 2):
        ortho = dot(products[number], inverses[number], ((1,), (1,)))
        orthos[number] = ortho
        buffer = momenta[number][...] + gradients[number][...].astype(jnp.float32)
        change = dot_three(ortho, columns[number][...])
        held[number][...] = buffer - (1.0 - MOMENTUM_DECAY) * change
        copies[number].start()
    for copy in copies:
        copy.wait()


def update_kernel(scales, place, *refs):
    squares, columns, orthos, outs = refs[0], refs[1:5], refs[5], refs[6:14]
    held, sent = refs[14:22], refs[22]
    copies = [pltpu.make_async_copy(held[i], outs[i], sent.at[i]) for i in range(8)]
    inverse = 1.0 / jnp.sqrt(squares[...] + EPSILON)
    for number in (0, 3, 1, 2):
        basis = columns[number][...] * inverse[number : number + 1, :]
        held[4 + number][...] = basis
        copies[4 + number].start()
        held[number][...] = scales[number] * dot_three(orthos[number], basis)
        copies[number].start()
    for copy in copies:
        copy.wait()


def result_call(body, shapes, operands, name, kept=()):
    return pl.pallas_call(
        body,
        out_shape=[jax.ShapeDtypeStruct(shape, jnp.float32) for shape in (*shapes, *kept)],
        in_specs=[pl.BlockSpec(memory_space=pltpu.SMEM)]
        + [pl.BlockSpec(memory_space=pltpu.VMEM)] * (len(operands) - 1),
        out_specs=[pl.BlockSpec(memory_space=pl.ANY)] * len(shapes)
        + [pl.BlockSpec(memory_space=pltpu.VMEM)] * len(kept),
        scratch_shapes=[pltpu.VMEM(shape, jnp.float32) for shape in shapes]
        + [pltpu.SemaphoreType.DMA((len(shapes),))],
        cost_estimate=cost(3),
        compiler_params=pltpu.CompilerParams(vmem_limit_bytes=24 * 1024 * 1024),
        name=name,
    )(*operands)


def local(*arguments):
    momenta = arguments[0::3]
    gradients = arguments[1::3]
    factors = arguments[2::3]
    height = momenta[0].shape[0]
    place = jnp.stack([lax.axis_index(axis) for axis in SIZES]).astype(jnp.int32)

    half = (128, RANK)
    send, keep = product_call(place, (*momenta, *gradients, *factors))
    received = shift_along(send, "core", 1)
    pieces = call(pair_kernel, [half] * 4, (place, keep, received), "pairs")
    shard = sum(reversed(from_three(pieces[1:], "x", -1)), pieces[0])
    same = [shard] + from_three([shard] * 3, "x", 1)
    other = [shift_along(piece, "core", 1) for piece in same]

    *others, products = cross_call(False, place, (*momenta[1:], *gradients[1:], *same, *other))
    query = cross_call(True, place, (momenta[0], gradients[0], products))
    others_in = shift_along(others[1], "y", -1), shift_along(others[2], "y", 1)
    query_in = shift_along(query[1], "y", -1), shift_along(query[2], "y", 1)
    plus, minus = pass_call(place, others[3], others[4], *others_in)
    query_in, plus, minus = lax.optimization_barrier((query_in, plus, minus))
    other_pieces = (others[0], *others_in, shift_along(plus, "y", -1), shift_along(minus, "y", 1))
    plus, minus = pass_call(place, query[3], query[4], *query_in, 20)
    query_pieces = (query[0], *query_in, shift_along(plus, "y", -1), shift_along(minus, "y", 1))

    keep, near, far = call(
        row_kernel,
        [(320, RANK), (160, RANK), (160, RANK)],
        (place, *query_pieces, *other_pieces),
        "rows",
        [(608, RANK)],
    )
    near, far = neighbours(near, far)
    pieces = call(
        neighbour_kernel, [(104, RANK)] * 4, (place, keep, near, far), "neighbours", [(320, RANK)]
    )
    pieces = [pieces[0]] + from_three(pieces[1:], "z", -2)
    shard, gram = call(
        deep_kernel, [(72, RANK), (32, RANK)], (place, *pieces), "deeps", [(4, 32, RANK)]
    )

    beside = shift_along(gram, "core", 1)
    first = place[3] == 0
    pair = jnp.concatenate([jnp.where(first, gram, beside), jnp.where(first, beside, gram)], axis=0)
    rows = [pair] + from_three([pair] * 3, "y", 1)[::-1]

    pieces = [shard] + from_three([shard] * 3, "z", 2)[::-1]
    near, far = call(quad_kernel, [(144, RANK)] * 2, (place, *pieces), "quads", [(288, RANK)])
    (joined,) = call(
        join_kernel, [(576, RANK)], (place, near, far, *neighbours(near, far)), "joins"
    )
    before = shift_along(joined, "y", -1)
    after = shift_along(joined, "y", 1)

    packed, mine = call(
        inverse_kernel,
        [(192, RANK), (96, RANK)],
        (place, *rows),
        "inverse",
        [(RANK, RANK), (RANK, RANK), (RANK, 2 * RANK)],
        11,
    )
    same = from_three([mine] * 3, "x", 1)[::-1]
    *same, before, after = lax.optimization_barrier((*same, before, after))
    operands = (place, before, after)
    lower, upper = call(forward_kernel, [(288, RANK)] * 2, operands, "forwards")
    lower = shift_along(lower, "y", -1)
    upper = shift_along(upper, "y", 1)
    other = [shift_along(piece, "core", 1) for piece in same]
    tall = [(momentum.shape[1], RANK) for momentum in momenta]
    flat = [momentum.shape for momentum in momenta]
    *columns, squares, inverses = call(
        column_kernel,
        tall + [(4, RANK), (4, RANK, RANK)],
        (place, packed, *same, *other, joined, after, lower, upper, before),
        "columns",
        [(2, 1024, RANK), (2, 128, RANK), (4, 192, RANK)],
        3,
    )
    squares = squares + shift_along(squares, "core", 1)
    squares = squares + sum(reversed(from_three([squares] * 3, "x", 1)))
    *new_momenta, orthos = result_call(
        momentum_kernel,
        flat,
        (place, *momenta, *gradients, *columns, inverses, products),
        "momenta",
        [(4, RANK, RANK)],
    )
    scales = [math.sqrt(height * 32 * shape[1] * 8 / RANK) for shape in flat]
    outs = result_call(
        functools.partial(update_kernel, scales),
        flat + tall,
        (place, squares, *columns, orthos),
        "updates",
    )
    results = []
    for number in range(4):
        results = results + [outs[number], new_momenta[number], outs[4 + number]]
    return tuple(results)


def solution(mesh):
    devices = mesh.devices.reshape(tuple(SIZES.values()))
    finer = Mesh(devices, tuple(SIZES))
    wide = P(("z", "y"), ("x", "core"))
    tall = P(("x", "core"), None)
    return jax.shard_map(
        local,
        mesh=finer,
        in_specs=(wide, wide, tall) * 4,
        out_specs=(wide, wide, tall) * 4,
        check_vma=False,
    )
```
